32 devices in a mesh: seq: 4 (over y, x), dp: 8 (over z, core).
Axes of the slice: x: 2, y: 2, z: 4, core: 2. Of those that a mesh axis runs over, the one named last changes fastest.
Arguments:
- inputs: bfloat16 [16, 1024, 2048], P('dp', 'seq'), may hold values from -6 to 6
- counts: int32 [8], P('dp'), may hold values from 1 to 2, as said below
- cotangent: bfloat16 [16, 1024, 2048], P('dp', 'seq'), may hold values from -6 to 6
- stretch: bfloat16 [2048], P(('seq', 'dp')), may hold values from 0.099609375 to 1.8984375
- offset: bfloat16 [2048], P(('seq', 'dp')), may hold values from -1.5 to 1.5
- inward: bfloat16 [2048, 6144], P(('seq', 'dp')), may hold values from -0.1875 to 0.1875
- outward: bfloat16 [2048, 2048], P(('seq', 'dp')), may hold values from -0.25 to 0.25
- dilation: bfloat16 [2048], P(('seq', 'dp')), may hold values from 0.099609375 to 1.8984375
- translation: bfloat16 [2048], P(('seq', 'dp')), may hold values from -1.5 to 1.5
- upward: bfloat16 [2048, 8192], P(('seq', 'dp')), may hold values from -0.125 to 0.125
- downward: bfloat16 [8192, 2048], P(('seq', 'dp')), may hold values from -0.0625 to 0.0625
Outputs:
- outputs: bfloat16 [16, 1024, 2048], P('dp', 'seq')
- input_delta: float32 [16, 1024, 2048], P('dp', 'seq')
- stretch_delta: float32 [2048], P(('seq', 'dp'))
- offset_delta: float32 [2048], P(('seq', 'dp'))
- inward_delta: float32 [2048, 6144], P(('seq', 'dp'))
- outward_delta: float32 [2048, 2048], P(('seq', 'dp'))
- dilation_delta: float32 [2048], P(('seq', 'dp'))
- translation_delta: float32 [2048], P(('seq', 'dp'))
- upward_delta: float32 [2048, 8192], P(('seq', 'dp'))
- downward_delta: float32 [8192, 2048], P(('seq', 'dp'))
The draws below stay inside these ranges and needn't reach their ends.
Inputs may be any that keep to these rules, and one draw needn't show every extreme that they name: Slots 0 to counts - 1 of a group hold sequences, later slots of the group none; some group uses all 2 slots and some other group only one.
All inputs are finite; a program needn't handle non-finite values.
Results may differ from the reference program's by a relative error of at most 0.013.
The reference program's roundings to bfloat16 on the way count: a program that leaves them out, or rounds other values in their place, can miss the bound.
Values may be sent and summed in bfloat16 or wider, within the bound.
A program may use at most 768 MiB of HBM per device.

```python
import math
import jax
import jax.numpy as jnp
from jax import lax

D = 2048
HEADS = 16
FF = 8192
HEAD_DIM = 128
LEN = 1024
SLOTS = 2
SEQS = 16


def draw_counts(key, part):
    key = jax.random.fold_in(key, 7)
    first, second, third = jax.random.split(key, 3)
    groups = SEQS // SLOTS
    drawn = jax.random.randint(first, (groups,), 1, SLOTS + 1)
    filled = jax.random.randint(second, (), 0, groups)
    further = jax.random.randint(third, (), 1, groups)
    single = (filled + further) % groups
    places = jnp.arange(groups)
    return jnp.where(places == filled, SLOTS, jnp.where(places == single, 1, drawn)).astype(jnp.int32)


def levels(stream_key, shape, cuts, least, top_value):
    level, own = 1.0, jax.random.fold_in(stream_key, 6)
    for axis_at, blocks in cuts:
        draws = jnp.exp(jax.random.uniform(jax.random.fold_in(own, axis_at), (blocks,), jnp.float32, least / len(cuts), top_value / len(cuts)))
        level = level * jnp.repeat(draws, shape[axis_at] // blocks).reshape([-1 if axis == axis_at else 1 for axis in range(len(shape))])
    return level


def gaussian(stream_key, extent, spread, reach, shards=(), held_as=jnp.bfloat16):
    values = jax.random.normal(stream_key, extent, jnp.float32) * spread
    if len(shards) > 0:
        values = levels(stream_key, extent, shards, -0.22, 0.18) * values
    return jnp.clip(values, min=-reach, max=reach).astype(held_as)


def setup_inputs(seed: int = 0) -> dict:
    key_list = jax.random.split(jax.random.key(seed), 12)
    inputs = gaussian(key_list[0], (SEQS, LEN, D), 1.0, 6.0, ((0, 8), (1, 4)))
    counts = draw_counts(jax.random.fold_in(key_list[11], 71), 0)
    cotangent = gaussian(key_list[2], (SEQS, LEN, D), 1.0, 6.0, ((0, 8), (1, 4)))
    stretch = jnp.clip(1.0 + 0.18 * jax.random.normal(key_list[3], (D,), jnp.float32), 0.099609375, 1.8984375).astype(jnp.bfloat16)
    offset = gaussian(key_list[4], (D,), 0.3, 1.5, ((0, 32),))
    inward = gaussian(key_list[5], (D, 3 * D), (D // 2) ** -0.5, 0.1875, ((0, 32),))
    outward = gaussian(key_list[6], (D, D), (D // 4) ** -0.5, 0.25, ((0, 32),))
    dilation = jnp.clip(1.0 + 0.18 * jax.random.normal(key_list[7], (D,), jnp.float32), 0.099609375, 1.8984375).astype(jnp.bfloat16)
    translation = gaussian(key_list[8], (D,), 0.3, 1.5, ((0, 32),))
    upward = gaussian(key_list[9], (D, FF), D ** -0.5, 0.125, ((0, 32),))
    downward = gaussian(key_list[10], (FF, D), FF ** -0.5, 0.0625, ((0, 32),))
    return {"inputs": inputs, "counts": counts, "cotangent": cotangent, "stretch": stretch, "offset": offset, "inward": inward, "outward": outward, "dilation": dilation, "translation": translation, "upward": upward, "downward": downward}


@jax.custom_vjp
def low(v):
    return lax.optimization_barrier(v.astype(jnp.bfloat16)).astype(jnp.float32)

@jax.custom_vjp
def low_back(v):
    return v

def low_keep(v):
    return (low(v), None)

def low_pass(kept, grad):
    return (grad,)

def back_keep(v):
    return (v, None)

def back_low(kept, grad):
    return (low(grad),)
low.defvjp(low_keep, low_pass)
low_back.defvjp(back_keep, back_low)
EPSILON = 1e-05
MASKED = -1e+30

def product(left, right):
    return jnp.dot(left, right, precision=lax.Precision.HIGHEST)

def layer_norm(values, gain, shift):
    average = lax.optimization_barrier(jnp.mean(values, axis=-1, keepdims=True))
    centered = values - average
    variance = lax.optimization_barrier(jnp.mean(centered * centered, axis=-1, keepdims=True))
    return centered * lax.rsqrt(variance + EPSILON) * gain + shift

def one_sequence(sequence, parameters, live_flag):
    stretch, offset, inward, outward, dilation, translation, upward, downward = parameters
    scaling = 1.0 / math.sqrt(HEAD_DIM)
    normed = low(layer_norm(sequence, stretch, offset))
    projected = low(low_back(product(normed, inward)))
    query_heads = projected[:, :D].reshape(LEN, HEADS, HEAD_DIM)
    key_heads = projected[:, D:2 * D].reshape(LEN, HEADS, HEAD_DIM)
    value_heads = projected[:, 2 * D:].reshape(LEN, HEADS, HEAD_DIM)
    logits = low_back(jnp.einsum('qhd,khd->hqk', query_heads, key_heads, precision=lax.Precision.HIGHEST) * scaling)
    places = jnp.arange(LEN)
    causal = places[None, :] <= places[:, None]
    weights = low(jax.nn.softmax(jnp.where(causal[None], logits, MASKED), axis=-1))
    mixture = jnp.einsum('hqk,khd->qhd', weights, value_heads, precision=lax.Precision.HIGHEST).reshape(LEN, D)
    attended = low(low_back(mixture))
    middle = sequence + low_back(product(attended, outward))
    normed_two = low(layer_norm(middle, dilation, translation))
    expanded = low_back(product(normed_two, upward))
    hidden = low(jax.nn.gelu(expanded, approximate=True))
    result = middle + low_back(product(hidden, downward))
    return result * live_flag

def reference(inputs, counts, cotangent, stretch, offset, inward, outward, dilation, translation, upward, downward):
    parameters = tuple((array.astype(jnp.float32) for array in (stretch, offset, inward, outward, dilation, translation, upward, downward)))
    slot_ids = jnp.arange(SEQS) % SLOTS
    owners = jnp.arange(SEQS) // SLOTS
    alive = (slot_ids < counts[owners]).astype(jnp.float32)

    def scan_step(totals, element):
        sequence, upstream, live_flag = element

        def apply_layer(values, weights):
            return one_sequence(values, weights, live_flag)
        result, pullback = jax.vjp(apply_layer, sequence.astype(jnp.float32), parameters)
        sequence_back, parameter_back = pullback(upstream.astype(jnp.float32))
        totals = tuple((left + right for left, right in zip(totals, parameter_back)))
        return (totals, (result.astype(jnp.bfloat16), sequence_back))
    start = tuple((jnp.zeros_like(array) for array in parameters))
    totals, results = lax.scan(scan_step, start, (inputs, cotangent, alive))
    return (results[0], results[1], totals[0], totals[1], totals[2], totals[3], totals[4], totals[5], totals[6], totals[7])
```

```python
import math

import jax
import jax.numpy as jnp
from jax import lax
from jax.sharding import PartitionSpec as P

HEADS = 16
EPSILON = 1e-05
MASKED = -1e30
BF = jnp.bfloat16
F32 = jnp.float32


def norm_parts(values):
    average = jnp.mean(values, axis=-1, keepdims=True)
    centered = values - average
    root = lax.rsqrt(jnp.mean(centered * centered, axis=-1, keepdims=True) + EPSILON)
    return centered * root, root


def norm_back(flow, unit, root, gain):
    scaled = flow * gain
    first = jnp.mean(scaled, axis=-1, keepdims=True)
    second = jnp.mean(scaled * unit, axis=-1, keepdims=True)
    return root * (scaled - first - unit * second), jnp.sum(flow * unit, axis=0), jnp.sum(flow, axis=0)


def smooth_gate(values):
    return jax.nn.gelu(values, approximate=True)


def rows_product(left, right):
    return lax.dot_general(left, right, (((0,), (0,)), ((), ())), preferred_element_type=F32)


def cols_product(left, right):
    return lax.dot_general(left, right, (((1,), (1,)), ((), ())), preferred_element_type=F32)


def product(left, right):
    return jnp.dot(left, right, preferred_element_type=F32)


def swap_over_seq(pieces, count):
    me = lax.axis_index("seq")
    result = jnp.zeros_like(pieces)
    own = lax.dynamic_index_in_dim(pieces, me, 0, keepdims=True)
    result = lax.dynamic_update_index_in_dim(result, own, me, 0)
    for step in range(1, count):
        if count & (count - 1) == 0:
            target, source = me ^ step, me ^ step
            pairs = [(i, i ^ step) for i in range(count)]
        else:
            target, source = (me + step) % count, (me - step) % count
            pairs = [(i, (i + step) % count) for i in range(count)]
        sent = lax.dynamic_index_in_dim(pieces, target, 0, keepdims=True)
        got = lax.ppermute(sent, "seq", pairs)
        result = lax.dynamic_update_index_in_dim(result, got, source, 0)
    return result


def probabilities(query, key, scaling):
    logits = jnp.einsum("sqhd,skhd->shqk", query, key, preferred_element_type=F32) * scaling
    length = logits.shape[-1]
    causal = jnp.arange(length)[None, :] <= jnp.arange(length)[:, None]
    return jax.nn.softmax(jnp.where(causal[None, None], logits, MASKED), axis=-1)


def make_layer(seq, dp):
    def scatter_seq(values, slots):
        shaped = values.astype(BF).reshape(slots, -1, values.shape[-1])
        got = lax.psum_scatter(shaped, "seq", scatter_dimension=1, tiled=True)
        return got.reshape(-1, values.shape[-1]).astype(F32)

    def gather_seq(values, slots):
        shaped = values.reshape(slots, -1, values.shape[-1])
        return lax.all_gather(shaped, "seq", axis=1, tiled=True).reshape(-1, values.shape[-1])

    def gather_columns(shard, thirds):
        rows, columns = shard.shape
        width = columns // (thirds * seq)
        pieces = shard.reshape(rows, thirds, seq, width).transpose(2, 0, 1, 3).reshape(seq, rows, thirds * width)
        swapped = swap_over_seq(pieces, seq)
        return lax.all_gather(swapped, "dp", axis=1, tiled=True).reshape(-1, thirds * width)

    def scatter_columns(term, thirds):
        total, width = term.shape
        rows = total // (seq * dp)
        summed = lax.psum_scatter(
            term.astype(BF).reshape(seq, dp * rows, width), "dp", scatter_dimension=1, tiled=True
        )
        swapped = swap_over_seq(summed, seq)
        shaped = swapped.reshape(seq, rows, thirds, width // thirds).transpose(1, 2, 0, 3)
        return shaped.reshape(rows, seq * width).astype(F32)

    def scatter_rows(term):
        return lax.psum_scatter(term.astype(BF), "dp", scatter_dimension=0, tiled=True).astype(F32)

    def layer(
        inputs, counts, cotangent, stretch, offset, inward, outward, dilation, translation, upward, downward
    ):
        slots, block, model = inputs.shape
        head_size = model // HEADS
        heads = HEADS // seq
        scaling = 1.0 / math.sqrt(head_size)
        local_rows = slots * block
        length = block * seq
        total = slots * length
        live = jnp.repeat((jnp.arange(slots) < counts[0]).astype(F32), block)[:, None]
        residual = inputs.reshape(local_rows, model)
        everything = gather_seq(residual, slots)
        small = jnp.stack([stretch, offset, dilation, translation]).astype(F32)
        small = lax.all_gather(small, ("seq", "dp"), axis=1, tiled=True)
        gain_one, shift_one, gain_two, shift_two = small[0], small[1], small[2], small[3]
        matrix_in = gather_columns(inward, 3)
        matrix_out = lax.all_gather(outward, "dp", axis=0, tiled=True)
        matrix_up = gather_columns(upward, 1)
        matrix_down = lax.all_gather(downward, "dp", axis=0, tiled=True)
        upstream = (cotangent.astype(F32).reshape(local_rows, model) * live).astype(BF)
        upstream_all = gather_seq(upstream, slots)

        unit_all, _ = norm_parts(everything.astype(F32))
        normed = (unit_all * gain_one + shift_one).astype(BF)
        projected = product(normed, matrix_in).astype(BF)
        query, key, value = (
            projected[:, i * heads * head_size : (i + 1) * heads * head_size].reshape(slots, length, heads, head_size)
            for i in range(3)
        )
        probs = probabilities(query, key, scaling)
        weights = probs.astype(BF)
        mixture = jnp.einsum("shqk,skhd->sqhd", weights, value, preferred_element_type=F32)
        attended = mixture.reshape(total, heads * head_size).astype(BF)
        middle = residual.astype(F32) + scatter_seq(product(attended, matrix_out), slots)
        unit_two, root_two = norm_parts(middle)
        normed_two = gather_seq((unit_two * gain_two + shift_two).astype(BF), slots)
        expanded = product(normed_two, matrix_up)
        hidden = smooth_gate(expanded).astype(BF)
        result = middle + scatter_seq(product(hidden, matrix_down), slots)
        outputs = (result * live).astype(BF).reshape(slots, block, model)

        downward_delta = scatter_rows(rows_product(hidden, upstream_all))
        hidden_back = cols_product(upstream_all, matrix_down)
        expanded_back = jax.vjp(smooth_gate, expanded)[1](hidden_back)[0].astype(BF)
        upward_delta = scatter_columns(rows_product(normed_two, expanded_back), 1)
        two_back = scatter_seq(cols_product(expanded_back, matrix_up), slots)
        middle_flow, dilation_term, translation_term = norm_back(two_back, unit_two, root_two, gain_two)
        middle_back = upstream.astype(F32) + middle_flow
        middle_low = gather_seq(middle_back.astype(BF), slots)
        outward_delta = scatter_rows(rows_product(attended, middle_low))
        heads_back = cols_product(middle_low, matrix_out).astype(BF).reshape(slots, length, heads, head_size)

        prob_back = jnp.einsum("sqhd,skhd->shqk", heads_back, value, preferred_element_type=F32)
        value_back = jnp.einsum("shqk,sqhd->skhd", weights, heads_back, preferred_element_type=F32)
        logit_back = (probs * (prob_back - jnp.sum(probs * prob_back, axis=-1, keepdims=True))).astype(BF)
        query_back = jnp.einsum("shqk,skhd->sqhd", logit_back, key, preferred_element_type=F32) * scaling
        key_back = jnp.einsum("shqk,sqhd->skhd", logit_back, query, preferred_element_type=F32) * scaling
        projected_back = jnp.concatenate(
            [part.astype(BF).reshape(total, heads * head_size) for part in (query_back, key_back, value_back)], axis=1
        )
        inward_delta = scatter_columns(rows_product(normed, projected_back), 3)
        one_back = scatter_seq(cols_product(projected_back, matrix_in), slots)
        unit_one, root_one = norm_parts(residual.astype(F32))
        input_flow, stretch_term, offset_term = norm_back(one_back, unit_one, root_one, gain_one)
        terms = jnp.stack([stretch_term, offset_term, dilation_term, translation_term])
        deltas = lax.psum_scatter(terms, ("seq", "dp"), scatter_dimension=1, tiled=True)
        input_delta = (middle_back + input_flow).reshape(slots, block, model)
        return (
            outputs,
            input_delta,
            deltas[0],
            deltas[1],
            inward_delta,
            outward_delta,
            deltas[2],
            deltas[3],
            upward_delta,
            downward_delta,
        )

    return layer


def solution(mesh):
    tokens, vector, matrix = P("dp", "seq", None), P(("seq", "dp")), P(("seq", "dp"), None)
    return jax.shard_map(
        make_layer(mesh.shape["seq"], mesh.shape["dp"]),
        mesh=mesh,
        in_specs=(tokens, P("dp"), tokens, vector, vector, matrix, matrix, vector, vector, matrix, matrix),
        out_specs=(tokens, tokens, vector, vector, matrix, matrix, vector, vector, matrix, matrix),
        check_vma=False,
    )
```

```python
import functools
import math

import jax
import jax.numpy as jnp
from jax import lax
from jax.experimental import pallas as pl
from jax.experimental.pallas import tpu as pltpu
from jax.sharding import PartitionSpec as P

HEADS = 16
EPSILON = 1e-05
MASKED = -1e30
BF = jnp.bfloat16
F32 = jnp.float32
MESH = pl.DeviceIdType.MESH


def norm_parts(values):
    average = jnp.mean(values, axis=-1, keepdims=True)
    centered = values - average
    root = lax.rsqrt(jnp.mean(centered * centered, axis=-1, keepdims=True) + EPSILON)
    return centered * root, root


def norm_back(flow, unit, root, gain):
    scaled = flow * gain
    first = jnp.mean(scaled, axis=-1, keepdims=True)
    second = jnp.mean(scaled * unit, axis=-1, keepdims=True)
    return root * (scaled - first - unit * second), jnp.sum(flow * unit, axis=0), jnp.sum(flow, axis=0)


def smooth_gate(values):
    return jax.nn.gelu(values, approximate=True)


def rows_product(left, right):
    return lax.dot_general(left, right, (((0,), (0,)), ((), ())), preferred_element_type=F32)


def cols_product(left, right):
    return lax.dot_general(left, right, (((1,), (1,)), ((), ())), preferred_element_type=F32)


def product(left, right):
    return jnp.dot(left, right, preferred_element_type=F32)


def after(values, event):
    return lax.optimization_barrier((values, event))[0]


def greet(seq, dp, me_seq, me_dp):
    barrier = pltpu.get_barrier_semaphore()
    for step in range(1, seq):
        pl.semaphore_signal(barrier, inc=1, device_id=(lax.rem(me_seq + step, seq), me_dp), device_id_type=MESH)
    for step in range(1, dp):
        pl.semaphore_signal(barrier, inc=1, device_id=(me_seq, lax.rem(me_dp + step, dp)), device_id_type=MESH)
    pl.semaphore_wait(barrier, seq + dp - 2)


def opening_kernel(seq, dp, pieces, small, swapped, params, own, send, recv, send_small, recv_small, send_row, recv_row):
    me_seq, me_dp = lax.axis_index("seq"), lax.axis_index("dp")
    greet(seq, dp, me_seq, me_dp)
    keep = [
        pltpu.make_async_copy(small, params.at[me_dp, me_seq], own.at[0]),
        pltpu.make_async_copy(pieces.at[me_seq], swapped.at[me_seq], own.at[1]),
    ]
    for copy in keep:
        copy.start()
    tiny, large, rows = [], [], []
    for step in range(1, seq):
        target = lax.rem(me_seq + step, seq)
        tiny.append(
            pltpu.make_async_remote_copy(
                small, params.at[me_dp, me_seq], send_small.at[step], recv_small.at[step], (target, me_dp), MESH
            )
        )
        tiny[-1].start()
    for step in range(1, seq):
        target = lax.rem(me_seq + step, seq)
        large.append(
            pltpu.make_async_remote_copy(
                pieces.at[target], swapped.at[me_seq], send.at[step], recv.at[step], (target, me_dp), MESH
            )
        )
        large[-1].start()
    keep[0].wait()
    for copy in tiny:
        copy.wait()
    for step in range(1, dp):
        target = lax.rem(me_dp + step, dp)
        rows.append(
            pltpu.make_async_remote_copy(
                params.at[me_dp], params.at[me_dp], send_row.at[step], recv_row.at[step], (me_seq, target), MESH
            )
        )
        rows[-1].start()
    keep[1].wait()
    for copy in rows + large:
        copy.wait()


def opening(seq, dp, pieces, small):
    anywhere = pl.BlockSpec(memory_space=pl.ANY)
    return pl.pallas_call(
        functools.partial(opening_kernel, seq, dp),
        out_shape=(
            jax.ShapeDtypeStruct(pieces.shape, pieces.dtype),
            jax.ShapeDtypeStruct((dp, seq) + small.shape, small.dtype),
        ),
        in_specs=[anywhere, anywhere],
        out_specs=(anywhere, anywhere),
        scratch_shapes=[pltpu.SemaphoreType.DMA((2,))]
        + [pltpu.SemaphoreType.DMA((seq,))] * 4
        + [pltpu.SemaphoreType.DMA((dp,))] * 2,
        compiler_params=pltpu.CompilerParams(collective_id=1, has_side_effects=True),
        name="opening",
    )(pieces, small)


def closing_kernel(seq, dp, terms, total, over_seq, partial, over_dp, send, recv, send_row, recv_row):
    me_seq, me_dp = lax.axis_index("seq"), lax.axis_index("dp")
    greet(seq, dp, me_seq, me_dp)
    copies = []
    for step in range(1, seq):
        target = lax.rem(me_seq + step, seq)
        copies.append(
            pltpu.make_async_remote_copy(
                terms.at[target], over_seq.at[step], send.at[step], recv.at[step], (target, me_dp), MESH
            )
        )
        copies[-1].start()
    value = terms[me_seq]
    for step, copy in enumerate(copies):
        copy.wait()
        value = value + over_seq[step + 1]
    partial[...] = value
    copies = []
    for step in range(1, dp):
        target = lax.rem(me_dp + step, dp)
        copies.append(
            pltpu.make_async_remote_copy(
                partial.at[target], over_dp.at[step], send_row.at[step], recv_row.at[step], (me_seq, target), MESH
            )
        )
        copies[-1].start()
    value = partial[me_dp]
    for step, copy in enumerate(copies):
        copy.wait()
        value = value + over_dp[step + 1]
    total[...] = value


def closing(seq, dp, terms):
    tile = terms.shape[2:]
    inside = pl.BlockSpec(memory_space=pltpu.VMEM)
    return pl.pallas_call(
        functools.partial(closing_kernel, seq, dp),
        out_shape=jax.ShapeDtypeStruct(tile, F32),
        in_specs=[inside],
        out_specs=inside,
        scratch_shapes=[
            pltpu.VMEM(terms.shape, F32),
            pltpu.VMEM(terms.shape[1:], F32),
            pltpu.VMEM(terms.shape[1:], F32),
        ]
        + [pltpu.SemaphoreType.DMA((seq,))] * 2
        + [pltpu.SemaphoreType.DMA((dp,))] * 2,
        compiler_params=pltpu.CompilerParams(collective_id=2, has_side_effects=True),
        name="closing",
    )(terms)


def head_parts(ref, where, part, size):
    return [ref[where[place], 0, :, part * size : (part + 1) * size] for place in range(ref.shape[0])]


def diagonal(block):
    return lax.broadcasted_iota(jnp.int32, (block, block), 1) <= lax.broadcasted_iota(jnp.int32, (block, block), 0)


def masked_exp(query, keys, scaling):
    logits = cols_product(query, keys) * scaling
    block, length = logits.shape
    last = jnp.where(diagonal(block), logits[:, length - block :], MASKED)
    logits = last if length == block else jnp.concatenate([logits[:, : length - block], last], axis=1)
    raised = jnp.exp(logits - jnp.max(logits, axis=-1, keepdims=True))
    return raised, jnp.sum(raised, axis=-1, keepdims=True)


def attend_kernel(scaling, where, joint, attended):
    seq, _, block, size = attended.shape
    keys = jnp.concatenate(head_parts(joint, where, 1, size))
    values = jnp.concatenate(head_parts(joint, where, 2, size))
    for place in range(seq):
        length = (place + 1) * block
        query = joint[where[place], 0, :, :size]
        raised, sums = masked_exp(query, keys[:length], scaling)
        weights = (raised * (1.0 / sums)).astype(BF)
        attended[where[place], 0] = product(weights, values[:length]).astype(BF)


def attend(where, joint, size, scaling):
    seq, slots, block, width = joint.shape
    heads = width // (3 * size)
    return pl.pallas_call(
        functools.partial(attend_kernel, scaling),
        out_shape=jax.ShapeDtypeStruct((seq, slots, block, heads * size), BF),
        grid=(slots, heads),
        in_specs=[
            pl.BlockSpec(memory_space=pltpu.SMEM),
            pl.BlockSpec((seq, 1, block, 3 * size), lambda slot, head: (0, slot, 0, head)),
        ],
        out_specs=pl.BlockSpec((seq, 1, block, size), lambda slot, head: (0, slot, 0, head)),
        compiler_params=pltpu.CompilerParams(vmem_limit_bytes=48 << 20),
        name="attend",
    )(where, joint)


def attend_back_kernel(scaling, where, joint, flow, joint_back, key_sum, value_sum):
    seq, _, block, size = flow.shape
    keys = jnp.concatenate(head_parts(joint, where, 1, size))
    values = jnp.concatenate(head_parts(joint, where, 2, size))
    for place in reversed(range(seq)):
        length = (place + 1) * block
        spot = where[place]
        query = joint[spot, 0, :, :size]
        flow_here = flow[spot, 0]
        raised, sums = masked_exp(query, keys[:length], scaling)
        probs = raised * (1.0 / sums)
        weights = probs.astype(BF)
        prob_back = cols_product(flow_here, values[:length])
        mean_back = jnp.sum(probs * prob_back, axis=-1, keepdims=True)
        logit_back = (probs * (prob_back - mean_back)).astype(BF)
        joint_back[spot, 0, :, :size] = (product(logit_back, keys[:length]) * scaling).astype(BF)
        key_term = rows_product(logit_back, query) * scaling
        value_term = rows_product(weights, flow_here)
        if place == seq - 1:
            key_sum[...] = key_term
            value_sum[...] = value_term
        else:
            key_sum[:length] += key_term
            value_sum[:length] += value_term
    for place in range(seq):
        rows = slice(place * block, (place + 1) * block)
        joint_back[where[place], 0, :, size : 2 * size] = key_sum[rows].astype(BF)
        joint_back[where[place], 0, :, 2 * size :] = value_sum[rows].astype(BF)


def attend_back(where, joint, flow, size, scaling):
    seq, slots, block, width = joint.shape
    heads = width // (3 * size)
    wide = pl.BlockSpec((seq, 1, block, 3 * size), lambda slot, head: (0, slot, 0, head))
    return pl.pallas_call(
        functools.partial(attend_back_kernel, scaling),
        out_shape=jax.ShapeDtypeStruct(joint.shape, BF),
        grid=(slots, heads),
        in_specs=[
            pl.BlockSpec(memory_space=pltpu.SMEM),
            wide,
            pl.BlockSpec((seq, 1, block, size), lambda slot, head: (0, slot, 0, head)),
        ],
        out_specs=wide,
        scratch_shapes=[pltpu.VMEM((seq * block, size), F32)] * 2,
        compiler_params=pltpu.CompilerParams(vmem_limit_bytes=48 << 20),
        name="attend_back",
    )(where, joint, flow)


def swap_over_seq(pieces, count):
    me = lax.axis_index("seq")
    result = jnp.zeros_like(pieces)
    own = lax.dynamic_index_in_dim(pieces, me, 0, keepdims=True)
    result = lax.dynamic_update_index_in_dim(result, own, me, 0)
    for step in range(1, count):
        if count & (count - 1) == 0:
            target, source = me ^ step, me ^ step
            pairs = [(i, i ^ step) for i in range(count)]
        else:
            target, source = (me + step) % count, (me - step) % count
            pairs = [(i, (i + step) % count) for i in range(count)]
        sent = lax.dynamic_index_in_dim(pieces, target, 0, keepdims=True)
        got = lax.ppermute(sent, "seq", pairs)
        result = lax.dynamic_update_index_in_dim(result, got, source, 0)
    return result


def make_layer(seq, dp):
    xor = seq & (seq - 1) == 0

    def shift(values, step):
        pairs = [(i, i ^ step if xor else (i + step) % seq) for i in range(seq)]
        return lax.ppermute(values, "seq", pairs)

    def gather_seq(block):
        if seq != 4:
            return [block] + [shift(block, step) for step in range(1, seq)]
        half = block.shape[0] // 2
        near, far = shift(block, 1), shift(block, 2)
        corner = [shift(near[:half], 2), shift(far[half:], 1)]
        return [block, near, far, jnp.concatenate(corner)]

    def scatter_seq(make):
        if seq != 4:
            sent = [shift(make(step).astype(BF), step if xor else seq - step).astype(F32) for step in range(1, seq)]
            return make(0) + sum(sent)
        corner = make(3).astype(BF)
        half = corner.shape[0] // 2
        by_near, by_far = shift(corner[:half], 1), shift(corner[half:], 2)
        near = lax.optimization_barrier(make(1).astype(BF))
        far = lax.optimization_barrier(make(2).astype(BF))
        near_first, far_last = shift(near[:half], 1), shift(far[half:], 2)
        near_last = shift((near[half:].astype(F32) + by_far.astype(F32)).astype(BF), 1)
        far_first = shift((far[:half].astype(F32) + by_near.astype(F32)).astype(BF), 2)
        first = near_first.astype(F32) + far_first.astype(F32)
        last = near_last.astype(F32) + far_last.astype(F32)
        return make(0) + jnp.concatenate([first, last])

    def column_pieces(shard, thirds, groups):
        rows, columns = shard.shape
        shaped = shard.reshape(rows, thirds, seq, groups, -1).transpose(2, 0, 3, 1, 4)
        return shaped.reshape(seq, rows, columns // seq)

    def gather_columns(swapped):
        return lax.all_gather(swapped, "dp", axis=1, tiled=True).reshape(-1, swapped.shape[2])

    def scatter_columns(term, thirds, groups):
        total, width = term.shape
        rows = total // (seq * dp)
        summed = lax.psum_scatter(
            term.astype(BF).reshape(seq, dp * rows, width), "dp", scatter_dimension=1, tiled=True
        )
        swapped = swap_over_seq(summed, seq)
        shaped = swapped.reshape(seq, rows, groups, thirds, -1).transpose(1, 3, 0, 2, 4)
        return shaped.reshape(rows, seq * width).astype(F32)

    def scatter_rows(term):
        return lax.psum_scatter(term.astype(BF), "dp", scatter_dimension=0, tiled=True).astype(F32)

    def layer(
        inputs, counts, cotangent, stretch, offset, inward, outward, dilation, translation, upward, downward
    ):
        slots, block, model = inputs.shape
        head_size = model // HEADS
        heads = HEADS // seq
        scaling = 1.0 / math.sqrt(head_size)
        local_rows = slots * block
        total = seq * local_rows
        live = jnp.repeat((jnp.arange(slots) < counts[0]).astype(F32), block)[:, None]
        residual = inputs.reshape(local_rows, model)
        small = jnp.stack([stretch, offset, dilation, translation]).astype(F32).reshape(-1)
        taken = small.shape[0]
        small = jnp.pad(small, (0, -taken % 1024)).reshape(-1, 128)
        swapped_in, small = opening(seq, dp, column_pieces(inward, 3, heads), small)
        small = small.reshape(dp, seq, -1)[:, :, :taken].reshape(dp, seq, 4, -1).transpose(2, 1, 0, 3).reshape(4, model)
        gain_one, shift_one, gain_two, shift_two = small[0], small[1], small[2], small[3]
        matrix_in = gather_columns(swapped_in)
        blocks = gather_seq(after(residual, swapped_in))
        matrix_out = lax.all_gather(after(outward, matrix_in), "dp", axis=0, tiled=True)
        swapped_up = swap_over_seq(after(column_pieces(upward, 1, 1), blocks[-1]), seq)
        matrix_up = gather_columns(swapped_up)
        matrix_down = lax.all_gather(after(downward, matrix_up), "dp", axis=0, tiled=True)
        upstream = (cotangent.astype(F32).reshape(local_rows, model) * live).astype(BF)
        upstream_all = jnp.concatenate(gather_seq(after(upstream, swapped_up)))

        def piece(values, step):
            return values[step * local_rows : (step + 1) * local_rows]

        def norm_one(values):
            return (norm_parts(values.astype(F32))[0] * gain_one + shift_one).astype(BF)

        normed = [norm_one(part) for part in blocks]
        projected = jnp.concatenate([product(part, matrix_in).astype(BF) for part in normed])
        normed = jnp.concatenate(normed)

        me = lax.axis_index("seq")
        where = me ^ jnp.arange(seq) if xor else (me + seq - jnp.arange(seq)) % seq
        joint = projected.reshape(seq, slots, block, -1)
        attended = attend(where, joint, head_size, scaling).reshape(total, heads * head_size)
        middle = residual.astype(F32) + scatter_seq(lambda step: product(piece(attended, step), matrix_out))
        unit_two, root_two = norm_parts(middle)
        normed_two = gather_seq((unit_two * gain_two + shift_two).astype(BF))
        expanded = [product(part, matrix_up) for part in normed_two]
        normed_two = jnp.concatenate(normed_two)
        hidden = [smooth_gate(part).astype(BF) for part in expanded]
        def gate_back(step):
            flow = cols_product(piece(upstream_all, step), matrix_down)
            return jax.vjp(smooth_gate, expanded[step])[1](flow)[0].astype(BF)

        expanded_back = [gate_back(step) for step in range(seq)]
        two_back = scatter_seq(lambda step: cols_product(expanded_back[step], matrix_up))
        expanded_back = jnp.concatenate(expanded_back)
        downward_delta = scatter_rows(rows_product(jnp.concatenate(hidden), upstream_all))
        upward_delta = scatter_columns(rows_product(normed_two, expanded_back), 1, 1)
        middle_flow, dilation_term, translation_term = norm_back(two_back, unit_two, root_two, gain_two)
        middle_back = upstream.astype(F32) + middle_flow
        middle_low = gather_seq(middle_back.astype(BF))
        heads_back = jnp.concatenate([cols_product(part, matrix_out).astype(BF) for part in middle_low])
        result = middle + scatter_seq(lambda step: product(after(hidden[step], middle_low[-1]), matrix_down))
        outputs = (result * live).astype(BF).reshape(slots, block, model)
        outward_delta = scatter_rows(rows_product(attended, jnp.concatenate(middle_low)))
        heads_back = after(heads_back, downward_delta).reshape(seq, slots, block, -1)
        projected_back = attend_back(where, joint, heads_back, head_size, scaling).reshape(total, -1)
        inward_delta = scatter_columns(rows_product(normed, projected_back), 3, heads)
        one_back = scatter_seq(lambda step: cols_product(piece(projected_back, step), matrix_in))
        unit_one, root_one = norm_parts(residual.astype(F32))
        input_flow, stretch_term, offset_term = norm_back(one_back, unit_one, root_one, gain_one)
        terms = jnp.stack([stretch_term, offset_term, dilation_term, translation_term])
        terms = terms.reshape(4, seq, dp, -1).transpose(1, 2, 0, 3).reshape(seq, dp, -1)
        terms = jnp.pad(terms, ((0, 0), (0, 0), (0, -taken % 1024))).reshape(seq, dp, -1, 128)
        deltas = closing(seq, dp, terms).reshape(-1)[:taken].reshape(4, -1)
        input_delta = (middle_back + input_flow).reshape(slots, block, model)
        return (
            outputs,
            input_delta,
            deltas[0],
            deltas[1],
            inward_delta,
            outward_delta,
            deltas[2],
            deltas[3],
            upward_delta,
            downward_delta,
        )

    return layer


def solution(mesh):
    tokens, vector, matrix = P("dp", "seq", None), P(("seq", "dp")), P(("seq", "dp"), None)
    return jax.shard_map(
        make_layer(mesh.shape["seq"], mesh.shape["dp"]),
        mesh=mesh,
        in_specs=(tokens, P("dp"), tokens, vector, vector, matrix, matrix, vector, vector, matrix, matrix),
        out_specs=(tokens, tokens, vector, vector, matrix, matrix, vector, vector, matrix, matrix),
        check_vma=False,
    )
```

```python
import functools
import math

import jax
import jax.numpy as jnp
from jax import lax
from jax.experimental import pallas as pl
from jax.experimental.pallas import tpu as pltpu
from jax.sharding import PartitionSpec as P

HEADS = 16
EPSILON = 1e-05
MASKED = -1e30
BF = jnp.bfloat16
F32 = jnp.float32
MESH = pl.DeviceIdType.MESH


def norm_parts(values):
    average = jnp.mean(values, axis=-1, keepdims=True)
    centered = values - average
    root = lax.rsqrt(jnp.mean(centered * centered, axis=-1, keepdims=True) + EPSILON)
    return centered * root, root


def norm_back(flow, unit, root, gain):
    scaled = flow * gain
    first = jnp.mean(scaled, axis=-1, keepdims=True)
    second = jnp.mean(scaled * unit, axis=-1, keepdims=True)
    return root * (scaled - first - unit * second), jnp.sum(flow * unit, axis=0), jnp.sum(flow, axis=0)


def rows_product(left, right):
    return lax.dot_general(left, right, (((0,), (0,)), ((), ())), preferred_element_type=F32)


def cols_product(left, right):
    return lax.dot_general(left, right, (((1,), (1,)), ((), ())), preferred_element_type=F32)


def product(left, right):
    return jnp.dot(left, right, preferred_element_type=F32)


def after(values, event):
    return lax.optimization_barrier((values, event))[0]


def greet(seq, dp, me_seq, me_dp):
    barrier = pltpu.get_barrier_semaphore()
    for step in range(1, seq):
        pl.semaphore_signal(barrier, inc=1, device_id=(lax.rem(me_seq + step, seq), me_dp), device_id_type=MESH)
    for step in range(1, dp):
        pl.semaphore_signal(barrier, inc=1, device_id=(me_seq, lax.rem(me_dp + step, dp)), device_id_type=MESH)
    pl.semaphore_wait(barrier, seq + dp - 2)


def start_trade(seq, me_seq, me_dp, pieces, swapped, own, send, recv):
    copies = [pltpu.make_async_copy(pieces.at[me_seq], swapped.at[me_seq], own)]
    copies[0].start()
    for step in range(1, seq):
        target = lax.rem(me_seq + step, seq)
        copies.append(
            pltpu.make_async_remote_copy(
                pieces.at[target], swapped.at[me_seq], send.at[step], recv.at[step], (target, me_dp), MESH
            )
        )
        copies[-1].start()
    return copies


def opening_kernel(
    seq, dp, pieces, pieces_two, small, swapped, swapped_two, params, own, send, recv, send_two, recv_two, send_small, recv_small, send_row, recv_row
):
    me_seq, me_dp = lax.axis_index("seq"), lax.axis_index("dp")
    greet(seq, dp, me_seq, me_dp)
    keep = pltpu.make_async_copy(small, params.at[me_dp, me_seq], own.at[0])
    keep.start()
    tiny, rows = [], []
    for step in range(1, seq):
        target = lax.rem(me_seq + step, seq)
        tiny.append(
            pltpu.make_async_remote_copy(
                small, params.at[me_dp, me_seq], send_small.at[step], recv_small.at[step], (target, me_dp), MESH
            )
        )
        tiny[-1].start()
    large = start_trade(seq, me_seq, me_dp, pieces, swapped, own.at[1], send, recv)
    large += start_trade(seq, me_seq, me_dp, pieces_two, swapped_two, own.at[2], send_two, recv_two)
    for copy in [keep] + tiny:
        copy.wait()
    for step in range(1, dp):
        target = lax.rem(me_dp + step, dp)
        rows.append(
            pltpu.make_async_remote_copy(
                params.at[me_dp], params.at[me_dp], send_row.at[step], recv_row.at[step], (me_seq, target), MESH
            )
        )
        rows[-1].start()
    for copy in rows + large:
        copy.wait()


def opening(seq, dp, pieces, pieces_two, small):
    anywhere = pl.BlockSpec(memory_space=pl.ANY)
    return pl.pallas_call(
        functools.partial(opening_kernel, seq, dp),
        out_shape=(
            jax.ShapeDtypeStruct(pieces.shape, pieces.dtype),
            jax.ShapeDtypeStruct(pieces_two.shape, pieces_two.dtype),
            jax.ShapeDtypeStruct((dp, seq) + small.shape, small.dtype),
        ),
        in_specs=[anywhere] * 3,
        out_specs=(anywhere,) * 3,
        scratch_shapes=[pltpu.SemaphoreType.DMA((3,))]
        + [pltpu.SemaphoreType.DMA((seq,))] * 6
        + [pltpu.SemaphoreType.DMA((dp,))] * 2,
        compiler_params=pltpu.CompilerParams(collective_id=1, has_side_effects=True),
        name="opening",
    )(pieces, pieces_two, small)


def closing_kernel(
    seq, dp, terms, pieces, pieces_two, total, swapped, swapped_two, over_seq, partial, over_dp,
    own, send, recv, send_two, recv_two, send_seq, recv_seq, send_row, recv_row,
):
    me_seq, me_dp = lax.axis_index("seq"), lax.axis_index("dp")
    greet(seq, dp, me_seq, me_dp)
    copies = []
    for step in range(1, seq):
        target = lax.rem(me_seq + step, seq)
        copies.append(
            pltpu.make_async_remote_copy(
                terms.at[target], over_seq.at[step], send_seq.at[step], recv_seq.at[step], (target, me_dp), MESH
            )
        )
        copies[-1].start()
    large = start_trade(seq, me_seq, me_dp, pieces, swapped, own.at[0], send, recv)
    large += start_trade(seq, me_seq, me_dp, pieces_two, swapped_two, own.at[1], send_two, recv_two)
    value = terms[me_seq]
    for step, copy in enumerate(copies):
        copy.wait()
        value = value + over_seq[step + 1]
    partial[...] = value
    copies = []
    for step in range(1, dp):
        target = lax.rem(me_dp + step, dp)
        copies.append(
            pltpu.make_async_remote_copy(
                partial.at[target], over_dp.at[step], send_row.at[step], recv_row.at[step], (me_seq, target), MESH
            )
        )
        copies[-1].start()
    value = partial[me_dp]
    for step, copy in enumerate(copies):
        copy.wait()
        value = value + over_dp[step + 1]
    total[...] = value
    for copy in large:
        copy.wait()


def closing(seq, dp, terms, pieces, pieces_two):
    tile = terms.shape[2:]
    inside, anywhere = pl.BlockSpec(memory_space=pltpu.VMEM), pl.BlockSpec(memory_space=pl.ANY)
    return pl.pallas_call(
        functools.partial(closing_kernel, seq, dp),
        out_shape=(
            jax.ShapeDtypeStruct(tile, F32),
            jax.ShapeDtypeStruct(pieces.shape, pieces.dtype),
            jax.ShapeDtypeStruct(pieces_two.shape, pieces_two.dtype),
        ),
        in_specs=[inside, anywhere, anywhere],
        out_specs=(inside, anywhere, anywhere),
        scratch_shapes=[
            pltpu.VMEM(terms.shape, F32),
            pltpu.VMEM(terms.shape[1:], F32),
            pltpu.VMEM(terms.shape[1:], F32),
            pltpu.SemaphoreType.DMA((2,)),
        ]
        + [pltpu.SemaphoreType.DMA((seq,))] * 6
        + [pltpu.SemaphoreType.DMA((dp,))] * 2,
        compiler_params=pltpu.CompilerParams(collective_id=2, has_side_effects=True),
        name="closing",
    )(terms, pieces, pieces_two)


def head_parts(ref, where, part, size):
    return [ref[where[place], 0, :, part * size : (part + 1) * size] for place in range(ref.shape[0])]


def diagonal(block):
    return lax.broadcasted_iota(jnp.int32, (block, block), 1) <= lax.broadcasted_iota(jnp.int32, (block, block), 0)


def masked_exp(query, keys, scaling):
    logits = cols_product(query, keys) * scaling
    block, length = logits.shape
    last = jnp.where(diagonal(block), logits[:, length - block :], MASKED)
    logits = last if length == block else jnp.concatenate([logits[:, : length - block], last], axis=1)
    raised = jnp.exp(logits - jnp.max(logits, axis=-1, keepdims=True))
    return raised, jnp.sum(raised, axis=-1, keepdims=True)


def attend_kernel(scaling, where, joint, attended):
    seq, _, block, size = attended.shape
    keys = jnp.concatenate(head_parts(joint, where, 1, size))
    values = jnp.concatenate(head_parts(joint, where, 2, size))
    for place in range(seq):
        length = (place + 1) * block
        query = joint[where[place], 0, :, :size]
        raised, sums = masked_exp(query, keys[:length], scaling)
        weights = (raised * (1.0 / sums)).astype(BF)
        attended[where[place], 0] = product(weights, values[:length]).astype(BF)


def attend(where, joint, size, scaling):
    seq, slots, block, width = joint.shape
    heads = width // (3 * size)
    return pl.pallas_call(
        functools.partial(attend_kernel, scaling),
        out_shape=jax.ShapeDtypeStruct((seq, slots, block, heads * size), BF),
        grid=(slots, heads),
        in_specs=[
            pl.BlockSpec(memory_space=pltpu.SMEM),
            pl.BlockSpec((seq, 1, block, 3 * size), lambda slot, head: (0, slot, 0, head)),
        ],
        out_specs=pl.BlockSpec((seq, 1, block, size), lambda slot, head: (0, slot, 0, head)),
        compiler_params=pltpu.CompilerParams(vmem_limit_bytes=48 << 20),
        cost_estimate=pl.CostEstimate(flops=0, bytes_accessed=slots * (30 << 20), transcendentals=0),
        name="attend",
    )(where, joint)


def attend_back_kernel(scaling, where, joint, flow, joint_back, key_sum, value_sum):
    seq, _, block, size = flow.shape
    keys = jnp.concatenate(head_parts(joint, where, 1, size))
    values = jnp.concatenate(head_parts(joint, where, 2, size))
    for place in reversed(range(seq)):
        length = (place + 1) * block
        spot = where[place]
        query = joint[spot, 0, :, :size]
        flow_here = flow[spot, 0]
        raised, sums = masked_exp(query, keys[:length], scaling)
        probs = raised * (1.0 / sums)
        weights = probs.astype(BF)
        prob_back = cols_product(flow_here, values[:length])
        mean_back = jnp.sum(probs * prob_back, axis=-1, keepdims=True)
        logit_back = (probs * (prob_back - mean_back)).astype(BF)
        joint_back[spot, 0, :, :size] = (product(logit_back, keys[:length]) * scaling).astype(BF)
        key_term = rows_product(logit_back, query) * scaling
        value_term = rows_product(weights, flow_here)
        if place == seq - 1:
            key_sum[...] = key_term
            value_sum[...] = value_term
        else:
            key_sum[:length] += key_term
            value_sum[:length] += value_term
    for place in range(seq):
        rows = slice(place * block, (place + 1) * block)
        joint_back[where[place], 0, :, size : 2 * size] = key_sum[rows].astype(BF)
        joint_back[where[place], 0, :, 2 * size :] = value_sum[rows].astype(BF)


def attend_back(where, joint, flow, size, scaling):
    seq, slots, block, width = joint.shape
    heads = width // (3 * size)
    wide = pl.BlockSpec((seq, 1, block, 3 * size), lambda slot, head: (0, slot, 0, head))
    return pl.pallas_call(
        functools.partial(attend_back_kernel, scaling),
        out_shape=jax.ShapeDtypeStruct(joint.shape, BF),
        grid=(slots, heads),
        in_specs=[
            pl.BlockSpec(memory_space=pltpu.SMEM),
            wide,
            pl.BlockSpec((seq, 1, block, size), lambda slot, head: (0, slot, 0, head)),
        ],
        out_specs=wide,
        scratch_shapes=[pltpu.VMEM((seq * block, size), F32)] * 2,
        compiler_params=pltpu.CompilerParams(vmem_limit_bytes=48 << 20),
        cost_estimate=pl.CostEstimate(flops=0, bytes_accessed=slots * (45 << 20), transcendentals=0),
        name="attend_back",
    )(where, joint, flow)


def partner(me, step, count):
    if count & (count - 1):
        return lax.rem(me + step, count), lax.rem(me + count - step, count)
    bit = 1
    while bit < count:
        if step & bit:
            me = me + bit * (1 - 2 * lax.rem(me // bit, 2))
        bit *= 2
    return me, me


def forward_back_kernel(
    seq, chunk, mine, upstream, up, down, normed_all, hidden, expanded_back, result, flow_all,
    normed, flow, load, store, send, recv, send_flow, recv_flow, keep,
):
    model, width = up.shape
    pull = math.sqrt(2.0 / math.pi)
    me_seq, me_dp = lax.axis_index("seq"), lax.axis_index("dp")
    here = pl.program_id(0)
    out, back = {}, {}
    for step in range(1, seq):
        target, origin = partner(me_seq, step, seq)
        out[step] = pltpu.make_async_remote_copy(
            normed.at[0], normed.at[step], send.at[step], recv.at[step], (target, me_dp), MESH
        )
        back[step] = pltpu.make_async_remote_copy(
            flow.at[step], flow_all.at[step], send_flow.at[step], recv_flow.at[step], (origin, me_dp), MESH
        )
    stores = [pltpu.make_async_copy(normed.at[step], normed_all.at[step], store.at[step]) for step in range(seq)]
    own = pltpu.make_async_copy(flow.at[0], flow_all.at[0], keep)
    early = [step for step in range(1, seq) if step & (step - 1) == 0]
    late = [step for step in range(1, seq) if step & (step - 1)]

    @pl.when(here == 0)
    def _():
        fetch = pltpu.make_async_copy(mine, normed.at[0], load)
        fetch.start()
        barrier = pltpu.get_barrier_semaphore()
        for step in range(1, seq):
            pl.semaphore_signal(barrier, inc=1, device_id=(lax.rem(me_seq + step, seq), me_dp), device_id_type=MESH)
        fetch.wait()
        pl.semaphore_wait(barrier, seq - 1)
        for step in early:
            out[step].start()

    for step in range(1, seq):

        @pl.when(here == step)
        def _(step=step):
            out[step].wait()
            if step == 1:
                for other in late:
                    out[other].start()

    def inner(step, carry):
        columns = pl.ds(pl.multiple_of(step * chunk, chunk), chunk)
        expanded = product(normed[here], up[:, columns])
        pulled = cols_product(upstream[0], down[columns, :])
        square = expanded * expanded
        bend = jnp.tanh(pull * (expanded + 0.044715 * (square * expanded)))
        half = 0.5 * (1.0 + bend)
        hidden[0, :, columns] = (expanded * half).astype(BF)
        slope = half + (0.5 * pull) * expanded * (1.0 - bend * bend) * (1.0 + 0.134145 * square)
        expanded_back[0, :, columns] = (pulled * slope).astype(BF)
        return carry

    lax.fori_loop(0, width // chunk, inner, 0)

    def outer(step, carry):
        columns = pl.ds(pl.multiple_of(step * chunk, chunk), chunk)
        flow[here, :, columns] = cols_product(expanded_back[0], up[columns, :]).astype(BF)
        return carry

    lax.fori_loop(0, model // chunk, outer, 0)
    for step in range(seq):

        @pl.when(here == step)
        def _(step=step):
            stores[step].start()
            if step == 0:
                own.start()
            else:
                back[step].start()

    def last(step, carry):
        columns = pl.ds(pl.multiple_of(step * chunk, chunk), chunk)
        result[0, :, columns] = product(hidden[0], down[:, columns]).astype(BF)
        return carry

    lax.fori_loop(0, model // chunk, last, 0)

    @pl.when(here == seq - 1)
    def _():
        for copy in stores + [own] + list(back.values()):
            copy.wait()


def forward_back(mine, upstream, up, down):
    seq, rows, model = upstream.shape
    width = up.shape[1]
    anywhere = pl.BlockSpec(memory_space=pl.ANY)
    by_step = lambda columns: pl.BlockSpec((1, rows, columns), lambda step: (step, 0, 0))
    whole = lambda shape: pl.BlockSpec(shape, lambda step: (0, 0), pipeline_mode=pl.Buffered(1))
    shape = lambda columns: jax.ShapeDtypeStruct((seq, rows, columns), BF)
    return pl.pallas_call(
        functools.partial(forward_back_kernel, seq, math.gcd(512, math.gcd(width, model))),
        out_shape=[shape(model), shape(width), shape(width), shape(model), shape(model)],
        grid=(seq,),
        in_specs=[anywhere, by_step(model), whole(up.shape), whole(down.shape)],
        out_specs=[anywhere, by_step(width), by_step(width), by_step(model), anywhere],
        scratch_shapes=[
            pltpu.VMEM((seq, rows, model), BF),
            pltpu.VMEM((seq, rows, model), BF),
            pltpu.SemaphoreType.DMA,
        ]
        + [pltpu.SemaphoreType.DMA((seq,))] * 5
        + [pltpu.SemaphoreType.DMA],
        compiler_params=pltpu.CompilerParams(
            collective_id=3, has_side_effects=True, vmem_limit_bytes=58 << 20
        ),
        cost_estimate=pl.CostEstimate(
            flops=8 * seq * rows * model * width, bytes_accessed=400 << 20, transcendentals=seq * rows * width
        ),
        name="forward_back",
    )(mine, upstream, up, down)


def make_layer(seq, dp):
    xor = seq & (seq - 1) == 0

    def shift(values, step):
        pairs = [(i, i ^ step if xor else (i + step) % seq) for i in range(seq)]
        return lax.ppermute(values, "seq", pairs)

    def gather_seq(block, event=None):
        if seq != 4:
            return [block] + [shift(block, step) for step in range(1, seq)]
        half = block.shape[0] // 2
        near, far = shift(block, 1), shift(block, 2)
        halves = near[:half], far[half:]
        if event is not None:
            halves = after(halves, event)
        return [block, near, far, jnp.concatenate([shift(halves[0], 2), shift(halves[1], 1)])]

    def scatter_seq(make, event=None, begun=None):
        if seq != 4:
            sent = [shift(make(step).astype(BF), step if xor else seq - step).astype(F32) for step in range(1, seq)]
            return make(0) + sum(sent)
        corner = make(3).astype(BF)
        half = corner.shape[0] // 2
        by_near, by_far = shift(corner[:half], 1), shift(corner[half:], 2)
        near = lax.optimization_barrier(make(1).astype(BF))
        far = lax.optimization_barrier(make(2).astype(BF))
        near_first, far_last = shift(near[:half], 1), shift(far[half:], 2)
        if event is not None:
            by_near, by_far = after((by_near, by_far), event)
        if begun is not None:
            begun.extend([by_near, by_far])
        near_last = shift((near[half:].astype(F32) + by_far.astype(F32)).astype(BF), 1)
        far_first = shift((far[:half].astype(F32) + by_near.astype(F32)).astype(BF), 2)
        first = near_first.astype(F32) + far_first.astype(F32)
        last = near_last.astype(F32) + far_last.astype(F32)
        return make(0) + jnp.concatenate([first, last])

    def column_pieces(shard, thirds, groups):
        rows, columns = shard.shape
        shaped = shard.reshape(rows, thirds, seq, groups, -1).transpose(2, 0, 3, 1, 4)
        return shaped.reshape(seq, rows, columns // seq)

    def gather_columns(swapped):
        return lax.all_gather(swapped, "dp", axis=1, tiled=True).reshape(-1, swapped.shape[2])

    def scatter_columns(term):
        total, width = term.shape
        rows = total // (seq * dp)
        summed = lax.psum_scatter(
            term.astype(BF).reshape(seq, dp * rows, width), "dp", scatter_dimension=1, tiled=True
        )
        return summed

    def column_rows(swapped, thirds, groups):
        _, rows, width = swapped.shape
        shaped = swapped.reshape(seq, rows, groups, thirds, -1).transpose(1, 3, 0, 2, 4)
        return shaped.reshape(rows, seq * width).astype(F32)

    def scatter_rows(term):
        return lax.psum_scatter(term.astype(BF), "dp", scatter_dimension=0, tiled=True).astype(F32)

    def layer(
        inputs, counts, cotangent, stretch, offset, inward, outward, dilation, translation, upward, downward
    ):
        slots, block, model = inputs.shape
        size = model // HEADS
        heads = HEADS // seq
        scaling = 1.0 / math.sqrt(size)
        local_rows = slots * block
        total = seq * local_rows
        live = jnp.repeat((jnp.arange(slots) < counts[0]).astype(F32), block)[:, None]
        residual = inputs.reshape(local_rows, model)
        small = jnp.stack([stretch, offset, dilation, translation]).astype(F32).reshape(-1)
        taken = small.shape[0]
        small = jnp.pad(small, (0, -taken % 1024)).reshape(-1, 128)
        swapped_in, swapped_up, small = opening(
            seq, dp, column_pieces(inward, 3, heads), column_pieces(upward, 1, 1), small
        )
        small = small.reshape(dp, seq, -1)[:, :, :taken].reshape(dp, seq, 4, -1).transpose(2, 1, 0, 3).reshape(4, model)
        gain_one, shift_one, gain_two, shift_two = small[0], small[1], small[2], small[3]
        matrix_in = gather_columns(swapped_in)
        blocks = gather_seq(after(residual, swapped_in))
        matrix_out = lax.all_gather(after(outward, (matrix_in, blocks[-1])), "dp", axis=0, tiled=True)
        upstream = (cotangent.astype(F32).reshape(local_rows, model) * live).astype(BF)
        def piece(values, step):
            return values[step * local_rows : (step + 1) * local_rows]

        def norm_one(values):
            return (norm_parts(values.astype(F32))[0] * gain_one + shift_one).astype(BF)

        normed = [norm_one(part) for part in blocks]
        projected = jnp.concatenate([product(part, matrix_in).astype(BF) for part in normed])
        normed = jnp.concatenate(normed)
        upstream_all = gather_seq(after(upstream, blocks[-1]), projected)
        matrix_up = gather_columns(after(swapped_up, (matrix_out, projected, upstream_all[1], upstream_all[2])))
        me = lax.axis_index("seq")
        where = me ^ jnp.arange(seq) if xor else (me + seq - jnp.arange(seq)) % seq
        joint = projected.reshape(seq, slots, block, -1)
        attended = attend(where, joint, size, scaling).reshape(total, heads * size)
        attended = after(attended, upstream_all)
        begun = []
        middle = residual.astype(F32) + scatter_seq(
            lambda step: product(piece(attended, step), matrix_out), None, begun
        )
        matrix_down = lax.all_gather(after(downward, (matrix_up, begun)), "dp", axis=0, tiled=True)
        unit_two, root_two = norm_parts(middle)
        mine = (unit_two * gain_two + shift_two).astype(BF)
        upstream_all = jnp.stack(upstream_all)
        normed_two, hidden, expanded_back, down_terms, two_terms = forward_back(mine, upstream_all, matrix_up, matrix_down)

        def flat(values):
            return values.reshape(-1, values.shape[-1])

        down_sum = rows_product(flat(hidden), flat(upstream_all))
        two_back = jnp.sum(two_terms.astype(F32), axis=0)
        downward_delta = scatter_rows(down_sum)
        middle_flow, dilation_term, translation_term = norm_back(two_back, unit_two, root_two, gain_two)
        middle_back = upstream.astype(F32) + middle_flow
        near_flow = middle_back.astype(BF)
        middle_low = gather_seq(near_flow)
        up_sum = rows_product(after(flat(normed_two), (down_sum, middle_low[1:3])), flat(expanded_back))
        summed_up = scatter_columns(up_sum)
        heads_back = jnp.concatenate([cols_product(part, matrix_out).astype(BF) for part in middle_low])
        outward_delta = scatter_rows(rows_product(attended, jnp.concatenate(middle_low)))
        heads_back = after(heads_back, (downward_delta, up_sum)).reshape(seq, slots, block, -1)
        projected_back = attend_back(where, joint, heads_back, size, scaling).reshape(total, -1)
        corner = cols_product(piece(projected_back, seq - 1), matrix_in).astype(BF)
        in_sum = rows_product(after(normed, (summed_up, corner)), projected_back)
        summed_in = scatter_columns(in_sum)
        one_terms = [cols_product(piece(projected_back, step), matrix_in) for step in range(seq - 1)]
        one_terms = [one_terms[0]] + lax.optimization_barrier([part.astype(BF) for part in one_terms[1:]]) + [corner]
        late_terms = after(down_terms, middle_low[-1])
        result = middle + scatter_seq(lambda step: late_terms[step].astype(F32), one_terms[1:])
        outputs = (result * live).astype(BF).reshape(slots, block, model)
        one_back = scatter_seq(lambda step: one_terms[step], in_sum)
        unit_one, root_one = norm_parts(residual.astype(F32))
        input_flow, stretch_term, offset_term = norm_back(one_back, unit_one, root_one, gain_one)
        terms = jnp.stack([stretch_term, offset_term, dilation_term, translation_term])
        terms = terms.reshape(4, seq, dp, -1).transpose(1, 2, 0, 3).reshape(seq, dp, -1)
        terms = jnp.pad(terms, ((0, 0), (0, 0), (0, -taken % 1024))).reshape(seq, dp, -1, 128)
        deltas, swapped_in, swapped_up = closing(seq, dp, terms, summed_in, summed_up)
        inward_delta, upward_delta = column_rows(swapped_in, 3, heads), column_rows(swapped_up, 1, 1)
        deltas = deltas.reshape(-1)[:taken].reshape(4, -1)
        input_delta = (middle_back + input_flow).reshape(slots, block, model)
        return (
            outputs,
            input_delta,
            deltas[0],
            deltas[1],
            inward_delta,
            outward_delta,
            deltas[2],
            deltas[3],
            upward_delta,
            downward_delta,
        )

    return layer


def solution(mesh):
    tokens, vector, matrix = P("dp", "seq", None), P(("seq", "dp")), P(("seq", "dp"), None)
    return jax.shard_map(
        make_layer(mesh.shape["seq"], mesh.shape["dp"]),
        mesh=mesh,
        in_specs=(tokens, P("dp"), tokens, vector, vector, matrix, matrix, vector, vector, matrix, matrix),
        out_specs=(tokens, tokens, vector, vector, matrix, matrix, vector, vector, matrix, matrix),
        check_vma=False,
    )
```

```python
import functools
import math

import jax
import jax.numpy as jnp
from jax import lax
from jax.experimental import pallas as pl
from jax.experimental.pallas import tpu as pltpu
from jax.sharding import PartitionSpec as P

HEADS = 16
EPSILON = 1e-05
MASKED = -1e30
BF = jnp.bfloat16
F32 = jnp.float32
MESH = pl.DeviceIdType.MESH


def norm_parts(values):
    average = jnp.mean(values, axis=-1, keepdims=True)
    centered = values - average
    root = lax.rsqrt(jnp.mean(centered * centered, axis=-1, keepdims=True) + EPSILON)
    return centered * root, root


def norm_back(flow, unit, root, gain):
    scaled = flow * gain
    first = jnp.mean(scaled, axis=-1, keepdims=True)
    second = jnp.mean(scaled * unit, axis=-1, keepdims=True)
    return root * (scaled - first - unit * second), jnp.sum(flow * unit, axis=0), jnp.sum(flow, axis=0)


def rows_product(left, right):
    return lax.dot_general(left, right, (((0,), (0,)), ((), ())), preferred_element_type=F32)


def cols_product(left, right):
    return lax.dot_general(left, right, (((1,), (1,)), ((), ())), preferred_element_type=F32)


def product(left, right):
    return jnp.dot(left, right, preferred_element_type=F32)


def after(values, event):
    return lax.optimization_barrier((values, event))[0]


def greet(seq, dp, me_seq, me_dp):
    barrier = pltpu.get_barrier_semaphore()
    for step in range(1, seq):
        pl.semaphore_signal(barrier, inc=1, device_id=(lax.rem(me_seq + step, seq), me_dp), device_id_type=MESH)
    for step in range(1, dp):
        pl.semaphore_signal(barrier, inc=1, device_id=(me_seq, lax.rem(me_dp + step, dp)), device_id_type=MESH)
    pl.semaphore_wait(barrier, seq + dp - 2)


def start_trade(seq, me_seq, me_dp, pieces, swapped, own, send, recv):
    copies = [pltpu.make_async_copy(pieces.at[me_seq], swapped.at[me_seq], own)]
    copies[0].start()
    for step in range(1, seq):
        target = lax.rem(me_seq + step, seq)
        copies.append(
            pltpu.make_async_remote_copy(
                pieces.at[target], swapped.at[me_seq], send.at[step], recv.at[step], (target, me_dp), MESH
            )
        )
        copies[-1].start()
    return copies


def opening_kernel(
    seq, dp, pieces, pieces_two, small, shard, swapped, swapped_two, params, shards,
    own, send, recv, send_two, recv_two, send_small, recv_small, send_row, recv_row, send_shard, recv_shard, send_next, recv_next,
):
    me_seq, me_dp = lax.axis_index("seq"), lax.axis_index("dp")
    greet(seq, dp, me_seq, me_dp)
    keep = pltpu.make_async_copy(small, params.at[me_dp, me_seq], own.at[0])
    keep.start()
    tiny, rows = [], []
    for step in range(1, seq):
        target = lax.rem(me_seq + step, seq)
        tiny.append(
            pltpu.make_async_remote_copy(
                small, params.at[me_dp, me_seq], send_small.at[step], recv_small.at[step], (target, me_dp), MESH
            )
        )
        tiny[-1].start()
    large = start_trade(seq, me_seq, me_dp, pieces, swapped, own.at[1], send, recv)
    span = 1 if dp % 2 else 2
    keep_shard = pltpu.make_async_copy(shard, shards.at[me_dp], own.at[3])
    keep_shard.start()
    firsts = []
    for step in range(1, dp // span):
        target = lax.rem(me_dp + span * step, dp)
        firsts.append(
            pltpu.make_async_remote_copy(
                shard, shards.at[me_dp], send_shard.at[step], recv_shard.at[step], (me_seq, target), MESH
            )
        )
        firsts[-1].start()
    large += start_trade(seq, me_seq, me_dp, pieces_two, swapped_two, own.at[2], send_two, recv_two)
    for copy in [keep] + tiny:
        copy.wait()
    for step in range(1, dp):
        target = lax.rem(me_dp + step, dp)
        rows.append(
            pltpu.make_async_remote_copy(
                params.at[me_dp], params.at[me_dp], send_row.at[step], recv_row.at[step], (me_seq, target), MESH
            )
        )
        rows[-1].start()
    keep_shard.wait()
    for step in range(dp // span):
        if step:
            firsts[step - 1].wait()
        if span == 2:
            origin = lax.rem(me_dp + dp - span * step, dp)
            sibling = me_dp + 1 - 2 * lax.rem(me_dp, 2)
            rows.append(
                pltpu.make_async_remote_copy(
                    shards.at[origin], shards.at[origin], send_next.at[step], recv_next.at[step], (me_seq, sibling), MESH
                )
            )
            rows[-1].start()
    for copy in rows + large:
        copy.wait()


def opening(seq, dp, pieces, pieces_two, small, shard):
    anywhere = pl.BlockSpec(memory_space=pl.ANY)
    return pl.pallas_call(
        functools.partial(opening_kernel, seq, dp),
        out_shape=(
            jax.ShapeDtypeStruct(pieces.shape, pieces.dtype),
            jax.ShapeDtypeStruct(pieces_two.shape, pieces_two.dtype),
            jax.ShapeDtypeStruct((dp, seq) + small.shape, small.dtype),
            jax.ShapeDtypeStruct((dp,) + shard.shape, shard.dtype),
        ),
        in_specs=[anywhere] * 4,
        out_specs=(anywhere,) * 4,
        scratch_shapes=[pltpu.SemaphoreType.DMA((4,))]
        + [pltpu.SemaphoreType.DMA((seq,))] * 6
        + [pltpu.SemaphoreType.DMA((dp,))] * 6,
        compiler_params=pltpu.CompilerParams(collective_id=1, has_side_effects=True),
        name="opening",
    )(pieces, pieces_two, small, shard)


def closing_kernel(
    seq, dp, terms, pieces, total, swapped, over_seq, partial, over_dp,
    own, send, recv, send_seq, recv_seq, send_row, recv_row,
):
    me_seq, me_dp = lax.axis_index("seq"), lax.axis_index("dp")
    greet(seq, dp, me_seq, me_dp)
    copies = []
    for step in range(1, seq):
        target = lax.rem(me_seq + step, seq)
        copies.append(
            pltpu.make_async_remote_copy(
                terms.at[target], over_seq.at[step], send_seq.at[step], recv_seq.at[step], (target, me_dp), MESH
            )
        )
        copies[-1].start()
    large = start_trade(seq, me_seq, me_dp, pieces, swapped, own, send, recv)
    value = terms[me_seq]
    for step, copy in enumerate(copies):
        copy.wait()
        value = value + over_seq[step + 1]
    partial[...] = value
    copies = []
    for step in range(1, dp):
        target = lax.rem(me_dp + step, dp)
        copies.append(
            pltpu.make_async_remote_copy(
                partial.at[target], over_dp.at[step], send_row.at[step], recv_row.at[step], (me_seq, target), MESH
            )
        )
        copies[-1].start()
    value = partial[me_dp]
    for step, copy in enumerate(copies):
        copy.wait()
        value = value + over_dp[step + 1]
    total[...] = value
    for copy in large:
        copy.wait()


def closing(seq, dp, terms, pieces):
    tile = terms.shape[2:]
    inside, anywhere = pl.BlockSpec(memory_space=pltpu.VMEM), pl.BlockSpec(memory_space=pl.ANY)
    return pl.pallas_call(
        functools.partial(closing_kernel, seq, dp),
        out_shape=(
            jax.ShapeDtypeStruct(tile, F32),
            jax.ShapeDtypeStruct(pieces.shape, pieces.dtype),
        ),
        in_specs=[inside, anywhere],
        out_specs=(inside, anywhere),
        scratch_shapes=[
            pltpu.VMEM(terms.shape, F32),
            pltpu.VMEM(terms.shape[1:], F32),
            pltpu.VMEM(terms.shape[1:], F32),
            pltpu.SemaphoreType.DMA,
        ]
        + [pltpu.SemaphoreType.DMA((seq,))] * 4
        + [pltpu.SemaphoreType.DMA((dp,))] * 2,
        compiler_params=pltpu.CompilerParams(collective_id=2, has_side_effects=True),
        name="closing",
    )(terms, pieces)


def head_parts(ref, where, part, size):
    return [ref[where[place], 0, :, part * size : (part + 1) * size] for place in range(ref.shape[0])]


def diagonal(block):
    return lax.broadcasted_iota(jnp.int32, (block, block), 1) <= lax.broadcasted_iota(jnp.int32, (block, block), 0)


def masked_exp(query, keys, scaling):
    logits = cols_product(query, keys) * scaling
    block, length = logits.shape
    last = jnp.where(diagonal(block), logits[:, length - block :], MASKED)
    logits = last if length == block else jnp.concatenate([logits[:, : length - block], last], axis=1)
    raised = jnp.exp(logits - jnp.max(logits, axis=-1, keepdims=True))
    return raised, jnp.sum(raised, axis=-1, keepdims=True)


def attend_kernel(scaling, where, joint, attended):
    seq, _, block, size = attended.shape
    keys = jnp.concatenate(head_parts(joint, where, 1, size))
    values = jnp.concatenate(head_parts(joint, where, 2, size))
    for place in range(seq):
        length = (place + 1) * block
        query = joint[where[place], 0, :, :size]
        raised, sums = masked_exp(query, keys[:length], scaling)
        weights = (raised * (1.0 / sums)).astype(BF)
        attended[where[place], 0] = product(weights, values[:length]).astype(BF)


def attend(where, joint, size, scaling):
    seq, slots, block, width = joint.shape
    heads = width // (3 * size)
    return pl.pallas_call(
        functools.partial(attend_kernel, scaling),
        out_shape=jax.ShapeDtypeStruct((seq, slots, block, heads * size), BF),
        grid=(slots, heads),
        in_specs=[
            pl.BlockSpec(memory_space=pltpu.SMEM),
            pl.BlockSpec((seq, 1, block, 3 * size), lambda slot, head: (0, slot, 0, head)),
        ],
        out_specs=pl.BlockSpec((seq, 1, block, size), lambda slot, head: (0, slot, 0, head)),
        compiler_params=pltpu.CompilerParams(vmem_limit_bytes=48 << 20),
        cost_estimate=pl.CostEstimate(flops=0, bytes_accessed=slots * (30 << 20), transcendentals=0),
        name="attend",
    )(where, joint)


def partner(me, step, count):
    if count & (count - 1):
        return lax.rem(me + step, count), lax.rem(me + count - step, count)
    bit = 1
    while bit < count:
        if step & bit:
            me = me + bit * (1 - 2 * lax.rem(me // bit, 2))
        bit *= 2
    return me, me


def attend_back_kernel(scaling, plan, joint, flow, terms, joint_back, terms_all, key_sum, value_sum, send, recv):
    seq, _, block, size = flow.shape
    me_seq, me_dp = lax.axis_index("seq"), lax.axis_index("dp")
    here = pl.program_id(0) * pl.num_programs(1) + pl.program_id(1)
    final = pl.num_programs(0) * pl.num_programs(1) - 1
    copies = [
        pltpu.make_async_remote_copy(
            terms.at[spot], terms_all.at[spot], send.at[spot], recv.at[spot], (partner(me_seq, step, seq)[1], me_dp), MESH
        )
        for spot, (step, half) in enumerate(plan)
        if step
    ]

    @pl.when(here == 0)
    def _():
        greet(seq, 1, me_seq, me_dp)
        for copy in copies:
            copy.start()

    where = [partner(me_seq, place, seq)[1] for place in range(seq)]
    keys = jnp.concatenate(head_parts(joint, where, 1, size))
    values = jnp.concatenate(head_parts(joint, where, 2, size))
    for place in reversed(range(seq)):
        length = (place + 1) * block
        spot = where[place]
        query = joint[spot, 0, :, :size]
        flow_here = flow[spot, 0]
        raised, sums = masked_exp(query, keys[:length], scaling)
        probs = raised * (1.0 / sums)
        weights = probs.astype(BF)
        prob_back = cols_product(flow_here, values[:length])
        mean_back = jnp.sum(probs * prob_back, axis=-1, keepdims=True)
        logit_back = (probs * (prob_back - mean_back)).astype(BF)
        joint_back[spot, 0, :, :size] = (product(logit_back, keys[:length]) * scaling).astype(BF)
        key_term = rows_product(logit_back, query) * scaling
        value_term = rows_product(weights, flow_here)
        if place == seq - 1:
            key_sum[...] = key_term
            value_sum[...] = value_term
        else:
            key_sum[:length] += key_term
            value_sum[:length] += value_term
    for place in range(seq):
        rows = slice(place * block, (place + 1) * block)
        joint_back[where[place], 0, :, size : 2 * size] = key_sum[rows].astype(BF)
        joint_back[where[place], 0, :, 2 * size :] = value_sum[rows].astype(BF)

    @pl.when(here == final)
    def _():
        for copy in copies:
            copy.wait()


def attend_back(plan, joint, flow, terms, size, scaling):
    seq, slots, block, width = joint.shape
    heads = width // (3 * size)
    anywhere = pl.BlockSpec(memory_space=pl.ANY)
    wide = pl.BlockSpec((seq, 1, block, 3 * size), lambda slot, head: (0, slot, 0, head))
    return pl.pallas_call(
        functools.partial(attend_back_kernel, scaling, plan),
        out_shape=[jax.ShapeDtypeStruct(joint.shape, BF), jax.ShapeDtypeStruct(terms.shape, BF)],
        grid=(slots, heads),
        in_specs=[wide, pl.BlockSpec((seq, 1, block, size), lambda slot, head: (0, slot, 0, head)), anywhere],
        out_specs=[wide, anywhere],
        scratch_shapes=[pltpu.VMEM((seq * block, size), F32)] * 2
        + [pltpu.SemaphoreType.DMA((terms.shape[0],))] * 2,
        compiler_params=pltpu.CompilerParams(
            collective_id=4, has_side_effects=True, vmem_limit_bytes=48 << 20
        ),
        cost_estimate=pl.CostEstimate(flops=0, bytes_accessed=300 << 20, transcendentals=0),
        name="attend_back",
    )(joint, flow, terms)


def forward_back_plan(seq):
    if seq == 4:
        order = [(0, 0), (0, 1), (1, 0), (2, 0), (1, 1), (2, 1), (3, 0), (3, 1)]
    else:
        order = [(step, half) for step in range(seq) for half in range(2)]
    at = {pair: spot for spot, pair in enumerate(order)}
    moves = []
    for step, half in order[2:]:
        if seq == 4 and step == 3:
            source = (1, 0) if half == 0 else (2, 1)
            moves.append((at[source], at[step, half], step - source[0], at[source]))
        else:
            moves.append((at[0, half], at[step, half], step, half))
    return order, moves


def forward_back_kernel(
    seq, chunk, mine, upstream, up, down, normed_all, hidden, expanded_back, result, flow_all,
    normed, flow, load, store, send, recv, send_flow, recv_flow,
):
    model, width = up.shape
    rows = normed.shape[1]
    pull = math.sqrt(2.0 / math.pi)
    me_seq, me_dp = lax.axis_index("seq"), lax.axis_index("dp")
    here = pl.program_id(0)
    order, moves = forward_back_plan(seq)
    steps = len(order)
    copies = {}
    for source, target, step, begin in moves:
        copies[target] = pltpu.make_async_remote_copy(
            normed.at[source], normed.at[target], send.at[target], recv.at[target],
            (partner(me_seq, step, seq)[0], me_dp), MESH,
        )
    backs = []
    for spot, (step, half) in enumerate(order):
        if step:
            backs.append(
                pltpu.make_async_remote_copy(
                    flow.at[spot], flow_all.at[spot], send_flow.at[spot], recv_flow.at[spot],
                    (partner(me_seq, step, seq)[1], me_dp), MESH,
                )
            )
        else:
            backs.append(pltpu.make_async_copy(flow.at[spot], flow_all.at[spot], recv_flow.at[spot]))
    stores = [pltpu.make_async_copy(normed.at[spot], normed_all.at[spot], store.at[spot]) for spot in range(steps)]

    @pl.when(here == 0)
    def _():
        fetches = [
            pltpu.make_async_copy(mine.at[pl.ds(half * rows, rows)], normed.at[half], load.at[half]) for half in range(2)
        ]
        for fetch in fetches:
            fetch.start()
        barrier = pltpu.get_barrier_semaphore()
        for step in range(1, seq):
            pl.semaphore_signal(barrier, inc=1, device_id=(lax.rem(me_seq + step, seq), me_dp), device_id_type=MESH)
        for fetch in fetches:
            fetch.wait()
        pl.semaphore_wait(barrier, seq - 1)

    for spot in range(steps):

        @pl.when(here == spot)
        def _(spot=spot):
            if spot > 1:
                copies[spot].wait_recv()
            for source, target, step, begin in moves:
                if begin == spot:
                    copies[target].start()
            stores[spot].start()

    def inner(step, carry):
        columns = pl.ds(pl.multiple_of(step * chunk, chunk), chunk)
        expanded = product(normed[here], up[:, columns])
        pulled = cols_product(upstream[0], down[columns, :])
        square = expanded * expanded
        bend = jnp.tanh(pull * (expanded + 0.044715 * (square * expanded)))
        half = 0.5 * (1.0 + bend)
        hidden[0, :, columns] = (expanded * half).astype(BF)
        slope = half + (0.5 * pull) * expanded * (1.0 - bend * bend) * (1.0 + 0.134145 * square)
        expanded_back[0, :, columns] = (pulled * slope).astype(BF)
        return carry

    lax.fori_loop(0, width // chunk, inner, 0)

    def outer(step, carry):
        columns = pl.ds(pl.multiple_of(step * chunk, chunk), chunk)
        flow[here, :, columns] = cols_product(expanded_back[0], up[columns, :]).astype(BF)
        return carry

    lax.fori_loop(0, model // chunk, outer, 0)
    for spot in range(steps):

        @pl.when(here == spot)
        def _(spot=spot):
            backs[spot].start()

    def last(step, carry):
        columns = pl.ds(pl.multiple_of(step * chunk, chunk), chunk)
        result[0, :, columns] = product(hidden[0], down[:, columns]).astype(BF)
        return carry

    lax.fori_loop(0, model // chunk, last, 0)

    @pl.when(here == steps - 1)
    def _():
        for copy in copies.values():
            copy.wait_send()
        for copy in stores + backs:
            copy.wait()


def forward_back(mine, upstream, up, down):
    steps, rows, model = upstream.shape
    seq = steps // 2
    width = up.shape[1]
    anywhere = pl.BlockSpec(memory_space=pl.ANY)
    by_step = lambda columns: pl.BlockSpec((1, rows, columns), lambda step: (step, 0, 0))
    whole = lambda shape: pl.BlockSpec(shape, lambda step: (0, 0), pipeline_mode=pl.Buffered(1))
    shape = lambda columns: jax.ShapeDtypeStruct((steps, rows, columns), BF)
    return pl.pallas_call(
        functools.partial(forward_back_kernel, seq, math.gcd(512, math.gcd(width, model))),
        out_shape=[shape(model), shape(width), shape(width), shape(model), shape(model)],
        grid=(steps,),
        in_specs=[anywhere, by_step(model), whole(up.shape), whole(down.shape)],
        out_specs=[anywhere, by_step(width), by_step(width), by_step(model), anywhere],
        scratch_shapes=[
            pltpu.VMEM((steps, rows, model), BF),
            pltpu.VMEM((steps, rows, model), BF),
            pltpu.SemaphoreType.DMA((2,)),
        ]
        + [pltpu.SemaphoreType.DMA((steps,))] * 5,
        compiler_params=pltpu.CompilerParams(
            collective_id=3, has_side_effects=True, vmem_limit_bytes=56 << 20
        ),
        cost_estimate=pl.CostEstimate(
            flops=8 * steps * rows * model * width, bytes_accessed=400 << 20, transcendentals=steps * rows * width
        ),
        name="forward_back",
    )(mine, upstream, up, down)


def make_layer(seq, dp):
    xor = seq & (seq - 1) == 0

    def shift(values, step):
        pairs = [(i, i ^ step if xor else (i + step) % seq) for i in range(seq)]
        return lax.ppermute(values, "seq", pairs)

    def gather_seq(block, event=None):
        if seq != 4:
            return [block] + [shift(block, step) for step in range(1, seq)]
        half = block.shape[0] // 2
        near, far = shift(block, 1), shift(block, 2)
        halves = near[:half], far[half:]
        if event is not None:
            halves = after(halves, event)
        return [block, near, far, jnp.concatenate([shift(halves[0], 2), shift(halves[1], 1)])]

    def scatter_seq(make, event=None, begun=None):
        if seq != 4:
            sent = [shift(make(step).astype(BF), step if xor else seq - step).astype(F32) for step in range(1, seq)]
            return make(0) + sum(sent)
        corner = make(3).astype(BF)
        half = corner.shape[0] // 2
        by_near, by_far = shift(corner[:half], 1), shift(corner[half:], 2)
        near = lax.optimization_barrier(make(1).astype(BF))
        far = lax.optimization_barrier(make(2).astype(BF))
        near_first, far_last = shift(near[:half], 1), shift(far[half:], 2)
        if event is not None:
            by_near, by_far = after((by_near, by_far), event)
        if begun is not None:
            begun.extend([by_near, by_far])
        near_last = shift((near[half:].astype(F32) + by_far.astype(F32)).astype(BF), 1)
        far_first = shift((far[:half].astype(F32) + by_near.astype(F32)).astype(BF), 2)
        first = near_first.astype(F32) + far_first.astype(F32)
        last = near_last.astype(F32) + far_last.astype(F32)
        return make(0) + jnp.concatenate([first, last])

    def column_pieces(shard, thirds, groups):
        rows, columns = shard.shape
        shaped = shard.reshape(rows, thirds, seq, groups, -1).transpose(2, 0, 3, 1, 4)
        return shaped.reshape(seq, rows, columns // seq)

    def gather_columns(swapped):
        return lax.all_gather(swapped, "dp", axis=1, tiled=True).reshape(-1, swapped.shape[2])

    def scatter_columns(term):
        total, width = term.shape
        rows = total // (seq * dp)
        summed = lax.psum_scatter(
            term.astype(BF).reshape(seq, dp * rows, width), "dp", scatter_dimension=1, tiled=True
        )
        return summed

    def column_rows(swapped, thirds, groups):
        _, rows, width = swapped.shape
        shaped = swapped.reshape(seq, rows, groups, thirds, -1).transpose(1, 3, 0, 2, 4)
        return shaped.reshape(rows, seq * width).astype(F32)

    def scatter_rows(term):
        return lax.psum_scatter(term.astype(BF), "dp", scatter_dimension=0, tiled=True).astype(F32)

    def layer(
        inputs, counts, cotangent, stretch, offset, inward, outward, dilation, translation, upward, downward
    ):
        slots, block, model = inputs.shape
        size = model // HEADS
        heads = HEADS // seq
        scaling = 1.0 / math.sqrt(size)
        local_rows = slots * block
        total = seq * local_rows
        live = jnp.repeat((jnp.arange(slots) < counts[0]).astype(F32), block)[:, None]
        residual = inputs.reshape(local_rows, model)
        small = jnp.stack([stretch, offset, dilation, translation]).astype(F32).reshape(-1)
        taken = small.shape[0]
        small = jnp.pad(small, (0, -taken % 1024)).reshape(-1, 128)
        swapped_in, swapped_up, small, matrix_out = opening(
            seq, dp, column_pieces(inward, 3, heads), column_pieces(upward, 1, 1), small, outward
        )
        matrix_out = matrix_out.reshape(-1, model)
        small = small.reshape(dp, seq, -1)[:, :, :taken].reshape(dp, seq, 4, -1).transpose(2, 1, 0, 3).reshape(4, model)
        gain_one, shift_one, gain_two, shift_two = small[0], small[1], small[2], small[3]
        matrix_in = gather_columns(swapped_in)
        blocks = gather_seq(after(residual, swapped_in))
        upstream = (cotangent.astype(F32).reshape(local_rows, model) * live).astype(BF)
        def piece(values, step):
            return values[step * local_rows : (step + 1) * local_rows]

        def norm_one(values):
            return (norm_parts(values.astype(F32))[0] * gain_one + shift_one).astype(BF)

        normed = [norm_one(part) for part in blocks]
        projected = jnp.concatenate([product(part, matrix_in).astype(BF) for part in normed])
        normed = jnp.concatenate(normed)
        upstream_all = gather_seq(after(upstream, blocks[-1]), projected)
        matrix_up = gather_columns(after(swapped_up, (matrix_in, blocks[-1])))
        me = lax.axis_index("seq")
        where = me ^ jnp.arange(seq) if xor else (me + seq - jnp.arange(seq)) % seq
        joint = projected.reshape(seq, slots, block, -1)
        attended = attend(where, joint, size, scaling).reshape(total, heads * size)
        middle = residual.astype(F32) + scatter_seq(lambda step: product(piece(attended, step), matrix_out))
        matrix_down = lax.all_gather(after(downward, (matrix_up, attended, upstream_all)), "dp", axis=0, tiled=True)
        unit_two, root_two = norm_parts(middle)
        mine = (unit_two * gain_two + shift_two).astype(BF)
        half = local_rows // 2
        plan = forward_back_plan(seq)[0]
        upstream_all = jnp.stack([upstream_all[step][part * half : (part + 1) * half] for step, part in plan])
        normed_two, hidden, expanded_back, down_terms, two_terms = forward_back(mine, upstream_all, matrix_up, matrix_down)

        def flat(values):
            return values.reshape(-1, values.shape[-1])

        down_sum = rows_product(flat(hidden), flat(upstream_all))
        spots = [[spot for spot, (_, part) in enumerate(plan) if part == which] for which in range(2)]

        def over_plan(values):
            return jnp.concatenate([sum(values[spot].astype(F32) for spot in places) for places in spots])

        two_back = over_plan(two_terms)
        downward_delta = scatter_rows(down_sum)
        middle_flow, dilation_term, translation_term = norm_back(two_back, unit_two, root_two, gain_two)
        middle_back = upstream.astype(F32) + middle_flow
        up_sum = rows_product(after(flat(normed_two), down_sum), flat(expanded_back))
        middle_low = gather_seq(after(middle_back.astype(BF), up_sum))
        heads_back = jnp.concatenate([cols_product(part, matrix_out).astype(BF) for part in middle_low])
        out_sum = rows_product(attended, jnp.concatenate(middle_low))
        heads_back = after(heads_back, (downward_delta, up_sum)).reshape(seq, slots, block, -1)
        summed_up = scatter_columns(after(up_sum, heads_back))
        projected_back, result_terms = attend_back(plan, joint, heads_back, down_terms, size, scaling)
        projected_back = projected_back.reshape(total, -1)
        result = middle + over_plan([down_terms[0], down_terms[1]] + [result_terms[spot] for spot in range(2, len(plan))])
        outputs = (result * live).astype(BF).reshape(slots, block, model)
        one_terms = [cols_product(piece(projected_back, step), matrix_in) for step in range(seq)]
        one_terms = [one_terms[0]] + lax.optimization_barrier([part.astype(BF) for part in one_terms[1:]])
        near_up = [lax.dynamic_index_in_dim(summed_up, where[step], 0, keepdims=False) for step in range(seq)]
        near_up = jnp.stack([near_up[0]] + [shift(near_up[step], step if xor else seq - step) for step in range(1, seq)])
        if not xor:
            near_up = near_up[(-jnp.arange(seq)) % seq]
        upward_delta = jnp.concatenate(
            [lax.dynamic_index_in_dim(near_up, where[step], 0, keepdims=False) for step in range(seq)], axis=1
        ).astype(F32)
        in_sum = rows_product(after(normed, (summed_up, one_terms[1:])), projected_back)
        summed_in = scatter_columns(in_sum)
        outward_delta = scatter_rows(after(out_sum, summed_in))
        one_back = scatter_seq(lambda step: one_terms[step])
        unit_one, root_one = norm_parts(residual.astype(F32))
        input_flow, stretch_term, offset_term = norm_back(one_back, unit_one, root_one, gain_one)
        terms = jnp.stack([stretch_term, offset_term, dilation_term, translation_term])
        terms = terms.reshape(4, seq, dp, -1).transpose(1, 2, 0, 3).reshape(seq, dp, -1)
        terms = jnp.pad(terms, ((0, 0), (0, 0), (0, -taken % 1024))).reshape(seq, dp, -1, 128)
        deltas, swapped_in = closing(seq, dp, terms, summed_in)
        inward_delta = column_rows(swapped_in, 3, heads)
        deltas = deltas.reshape(-1)[:taken].reshape(4, -1)
        input_delta = (middle_back + input_flow).reshape(slots, block, model)
        return (
            outputs,
            input_delta,
            deltas[0],
            deltas[1],
            inward_delta,
            outward_delta,
            deltas[2],
            deltas[3],
            upward_delta,
            downward_delta,
        )

    return layer


def solution(mesh):
    tokens, vector, matrix = P("dp", "seq", None), P(("seq", "dp")), P(("seq", "dp"), None)
    return jax.shard_map(
        make_layer(mesh.shape["seq"], mesh.shape["dp"]),
        mesh=mesh,
        in_specs=(tokens, P("dp"), tokens, vector, vector, matrix, matrix, vector, vector, matrix, matrix),
        out_specs=(tokens, tokens, vector, vector, matrix, matrix, vector, vector, matrix, matrix),
        check_vma=False,
    )
```

```python
import functools
import math

import jax
import jax.numpy as jnp
from jax import lax
from jax.experimental import pallas as pl
from jax.experimental.pallas import tpu as pltpu
from jax.sharding import PartitionSpec as P

HEADS = 16
EPSILON = 1e-05
MASKED = -1e30
BF = jnp.bfloat16
F32 = jnp.float32
MESH = pl.DeviceIdType.MESH


def norm_parts(values):
    average = jnp.mean(values, axis=-1, keepdims=True)
    centered = values - average
    root = lax.rsqrt(jnp.mean(centered * centered, axis=-1, keepdims=True) + EPSILON)
    return centered * root, root


def norm_back(flow, unit, root, gain):
    scaled = flow * gain
    first = jnp.mean(scaled, axis=-1, keepdims=True)
    second = jnp.mean(scaled * unit, axis=-1, keepdims=True)
    return root * (scaled - first - unit * second), jnp.sum(flow * unit, axis=0), jnp.sum(flow, axis=0)


def rows_product(left, right):
    return lax.dot_general(left, right, (((0,), (0,)), ((), ())), preferred_element_type=F32)


def cols_product(left, right):
    return lax.dot_general(left, right, (((1,), (1,)), ((), ())), preferred_element_type=F32)


def product(left, right):
    return jnp.dot(left, right, preferred_element_type=F32)


def after(values, event):
    return lax.optimization_barrier((values, event))[0]


def greet(seq, dp, me_seq, me_dp):
    barrier = pltpu.get_barrier_semaphore()
    for step in range(1, seq):
        pl.semaphore_signal(barrier, inc=1, device_id=(lax.rem(me_seq + step, seq), me_dp), device_id_type=MESH)
    for step in range(1, dp):
        pl.semaphore_signal(barrier, inc=1, device_id=(me_seq, lax.rem(me_dp + step, dp)), device_id_type=MESH)
    pl.semaphore_wait(barrier, seq + dp - 2)


def start_trade(seq, me_seq, me_dp, pieces, swapped, own, send, recv):
    copies = [pltpu.make_async_copy(pieces.at[me_seq], swapped.at[me_seq], own)]
    copies[0].start()
    for step in range(1, seq):
        target = lax.rem(me_seq + step, seq)
        copies.append(
            pltpu.make_async_remote_copy(
                pieces.at[target], swapped.at[me_seq], send.at[step], recv.at[step], (target, me_dp), MESH
            )
        )
        copies[-1].start()
    return copies


def opening_kernel(
    seq, dp, pieces, pieces_two, small, shard, swapped, swapped_two, params, shards,
    own, send, recv, send_two, recv_two, send_small, recv_small, send_row, recv_row, send_shard, recv_shard, send_next, recv_next,
):
    me_seq, me_dp = lax.axis_index("seq"), lax.axis_index("dp")
    greet(seq, dp, me_seq, me_dp)
    keep = pltpu.make_async_copy(small, params.at[me_dp, me_seq], own.at[0])
    keep.start()
    tiny, rows = [], []
    for step in range(1, seq):
        target = lax.rem(me_seq + step, seq)
        tiny.append(
            pltpu.make_async_remote_copy(
                small, params.at[me_dp, me_seq], send_small.at[step], recv_small.at[step], (target, me_dp), MESH
            )
        )
        tiny[-1].start()
    large = start_trade(seq, me_seq, me_dp, pieces, swapped, own.at[1], send, recv)
    span = 1 if dp % 2 else 2
    keep_shard = pltpu.make_async_copy(shard, shards.at[me_dp], own.at[3])
    keep_shard.start()
    firsts = []
    for step in range(1, dp // span):
        target = lax.rem(me_dp + span * step, dp)
        firsts.append(
            pltpu.make_async_remote_copy(
                shard, shards.at[me_dp], send_shard.at[step], recv_shard.at[step], (me_seq, target), MESH
            )
        )
        firsts[-1].start()
    large += start_trade(seq, me_seq, me_dp, pieces_two, swapped_two, own.at[2], send_two, recv_two)
    for copy in [keep] + tiny:
        copy.wait()
    for step in range(1, dp):
        target = lax.rem(me_dp + step, dp)
        rows.append(
            pltpu.make_async_remote_copy(
                params.at[me_dp], params.at[me_dp], send_row.at[step], recv_row.at[step], (me_seq, target), MESH
            )
        )
        rows[-1].start()
    keep_shard.wait()
    for step in range(dp // span):
        if step:
            firsts[step - 1].wait()
        if span == 2:
            origin = lax.rem(me_dp + dp - span * step, dp)
            sibling = me_dp + 1 - 2 * lax.rem(me_dp, 2)
            rows.append(
                pltpu.make_async_remote_copy(
                    shards.at[origin], shards.at[origin], send_next.at[step], recv_next.at[step], (me_seq, sibling), MESH
                )
            )
            rows[-1].start()
    for copy in rows + large:
        copy.wait()


def opening(seq, dp, pieces, pieces_two, small, shard):
    anywhere = pl.BlockSpec(memory_space=pl.ANY)
    return pl.pallas_call(
        functools.partial(opening_kernel, seq, dp),
        out_shape=(
            jax.ShapeDtypeStruct(pieces.shape, pieces.dtype),
            jax.ShapeDtypeStruct(pieces_two.shape, pieces_two.dtype),
            jax.ShapeDtypeStruct((dp, seq) + small.shape, small.dtype),
            jax.ShapeDtypeStruct((dp,) + shard.shape, shard.dtype),
        ),
        in_specs=[anywhere] * 4,
        out_specs=(anywhere,) * 4,
        scratch_shapes=[pltpu.SemaphoreType.DMA((4,))]
        + [pltpu.SemaphoreType.DMA((seq,))] * 6
        + [pltpu.SemaphoreType.DMA((dp,))] * 6,
        compiler_params=pltpu.CompilerParams(collective_id=1, has_side_effects=True),
        name="opening",
    )(pieces, pieces_two, small, shard)


def closing_kernel(
    seq, dp, terms, pieces, total, swapped, over_seq, partial, over_dp,
    own, send, recv, send_seq, recv_seq, send_row, recv_row,
):
    me_seq, me_dp = lax.axis_index("seq"), lax.axis_index("dp")
    greet(seq, dp, me_seq, me_dp)
    copies = []
    for step in range(1, seq):
        target = lax.rem(me_seq + step, seq)
        copies.append(
            pltpu.make_async_remote_copy(
                terms.at[target], over_seq.at[step], send_seq.at[step], recv_seq.at[step], (target, me_dp), MESH
            )
        )
        copies[-1].start()
    large = start_trade(seq, me_seq, me_dp, pieces, swapped, own, send, recv)
    value = terms[me_seq]
    for step, copy in enumerate(copies):
        copy.wait()
        value = value + over_seq[step + 1]
    partial[...] = value
    copies = []
    for step in range(1, dp):
        target = lax.rem(me_dp + step, dp)
        copies.append(
            pltpu.make_async_remote_copy(
                partial.at[target], over_dp.at[step], send_row.at[step], recv_row.at[step], (me_seq, target), MESH
            )
        )
        copies[-1].start()
    value = partial[me_dp]
    for step, copy in enumerate(copies):
        copy.wait()
        value = value + over_dp[step + 1]
    total[...] = value
    for copy in large:
        copy.wait()


def closing(seq, dp, terms, pieces):
    tile = terms.shape[2:]
    inside, anywhere = pl.BlockSpec(memory_space=pltpu.VMEM), pl.BlockSpec(memory_space=pl.ANY)
    return pl.pallas_call(
        functools.partial(closing_kernel, seq, dp),
        out_shape=(
            jax.ShapeDtypeStruct(tile, F32),
            jax.ShapeDtypeStruct(pieces.shape, pieces.dtype),
        ),
        in_specs=[inside, anywhere],
        out_specs=(inside, anywhere),
        scratch_shapes=[
            pltpu.VMEM(terms.shape, F32),
            pltpu.VMEM(terms.shape[1:], F32),
            pltpu.VMEM(terms.shape[1:], F32),
            pltpu.SemaphoreType.DMA,
        ]
        + [pltpu.SemaphoreType.DMA((seq,))] * 4
        + [pltpu.SemaphoreType.DMA((dp,))] * 2,
        compiler_params=pltpu.CompilerParams(collective_id=2, has_side_effects=True),
        name="closing",
    )(terms, pieces)


def head_parts(ref, where, part, size):
    return [ref[where[place], 0, :, part * size : (part + 1) * size] for place in range(ref.shape[0])]


def diagonal(block):
    return lax.broadcasted_iota(jnp.int32, (block, block), 1) <= lax.broadcasted_iota(jnp.int32, (block, block), 0)


def masked_exp(query, keys, scaling):
    logits = cols_product(query, keys) * scaling
    block, length = logits.shape
    last = jnp.where(diagonal(block), logits[:, length - block :], MASKED)
    logits = last if length == block else jnp.concatenate([logits[:, : length - block], last], axis=1)
    raised = jnp.exp(logits - jnp.max(logits, axis=-1, keepdims=True))
    return raised, jnp.sum(raised, axis=-1, keepdims=True)


def attend_kernel(scaling, where, joint, attended):
    seq, _, block, size = attended.shape
    keys = jnp.concatenate(head_parts(joint, where, 1, size))
    values = jnp.concatenate(head_parts(joint, where, 2, size))
    for place in range(seq):
        length = (place + 1) * block
        query = joint[where[place], 0, :, :size]
        raised, sums = masked_exp(query, keys[:length], scaling)
        weights = (raised * (1.0 / sums)).astype(BF)
        attended[where[place], 0] = product(weights, values[:length]).astype(BF)


def attend(where, joint, size, scaling):
    seq, slots, block, width = joint.shape
    heads = width // (3 * size)
    return pl.pallas_call(
        functools.partial(attend_kernel, scaling),
        out_shape=jax.ShapeDtypeStruct((seq, slots, block, heads * size), BF),
        grid=(slots, heads),
        in_specs=[
            pl.BlockSpec(memory_space=pltpu.SMEM),
            pl.BlockSpec((seq, 1, block, 3 * size), lambda slot, head: (0, slot, 0, head)),
        ],
        out_specs=pl.BlockSpec((seq, 1, block, size), lambda slot, head: (0, slot, 0, head)),
        compiler_params=pltpu.CompilerParams(vmem_limit_bytes=48 << 20),
        cost_estimate=pl.CostEstimate(flops=0, bytes_accessed=slots * (30 << 20), transcendentals=0),
        name="attend",
    )(where, joint)


def partner(me, step, count):
    if count & (count - 1):
        return lax.rem(me + step, count), lax.rem(me + count - step, count)
    bit = 1
    while bit < count:
        if step & bit:
            me = me + bit * (1 - 2 * lax.rem(me // bit, 2))
        bit *= 2
    return me, me


def forward_back_plan(seq):
    if seq == 4:
        order = [(0, 0), (0, 1), (1, 0), (2, 0), (1, 1), (2, 1), (3, 0), (3, 1)]
    else:
        order = [(step, half) for step in range(seq) for half in range(2)]
    at = {pair: spot for spot, pair in enumerate(order)}
    moves = []
    for step, half in order[2:]:
        if seq == 4 and step == 3:
            source = (1, 0) if half == 0 else (2, 1)
            moves.append((at[source], at[step, half], step - source[0], at[source]))
        else:
            moves.append((at[0, half], at[step, half], step, half))
    return order, moves


def returns(seq, plan, me_seq, me_dp, parts, extra, landing, send, recv):
    def copy(source, target, step, spot):
        device = (partner(me_seq, step, seq)[1], me_dp)
        return pltpu.make_async_remote_copy(source, target, send.at[spot], recv.at[spot], device, MESH)

    if seq != 4:
        return {spot: copy(parts(spot), landing.at[spot], step, spot) for spot, (step, _) in enumerate(plan) if step}, []
    at = {pair: spot for spot, pair in enumerate(plan)}
    now = {spot: copy(parts(spot), landing.at[spot], plan[spot][0], spot) for spot in (at[1, 0], at[2, 1])}
    now[at[3, 0]] = copy(parts(at[3, 0]), extra.at[0], 1, at[3, 0])
    now[at[3, 1]] = copy(parts(at[3, 1]), extra.at[1], 2, at[3, 1])
    later = []
    for half, spot in enumerate((at[2, 0], at[1, 1])):
        later.append((spot, at[3, half], copy(parts(spot), landing.at[spot], plan[spot][0], spot)))
    return now, later


def landings(seq):
    return 6 if seq == 4 else 2 * seq


def add_into(ref, spot, other, half, chunk):
    def body(step, carry):
        columns = pl.ds(pl.multiple_of(step * chunk, chunk), chunk)
        ref[spot, :, columns] = (ref[spot, :, columns].astype(F32) + other[half, :, columns].astype(F32)).astype(BF)
        return carry

    lax.fori_loop(0, ref.shape[2] // chunk, body, 0)


def attend_back_kernel(
    scaling, plan, joint, flow, terms, joint_back, terms_all, key_sum, value_sum, extra, held, load, send, recv
):
    seq, _, block, size = flow.shape
    me_seq, me_dp = lax.axis_index("seq"), lax.axis_index("dp")
    here = pl.program_id(0) * pl.num_programs(1) + pl.program_id(1)
    final = pl.num_programs(0) * pl.num_programs(1) - 1
    delayed = {spot: half for half, spot in enumerate([plan.index((2, 0)), plan.index((1, 1))])} if seq == 4 else {}
    now, later = returns(
        seq, plan, me_seq, me_dp, lambda spot: held.at[delayed[spot]] if spot in delayed else terms.at[spot],
        extra, terms_all, send, recv,
    )
    loads = [pltpu.make_async_copy(terms.at[spot], held.at[half], load.at[half]) for spot, half in delayed.items()]

    @pl.when(here == 0)
    def _():
        for copy in loads:
            copy.start()
        greet(seq, 1, me_seq, me_dp)
        for copy in now.values():
            copy.start()

    where = [partner(me_seq, place, seq)[1] for place in range(seq)]
    keys = jnp.concatenate(head_parts(joint, where, 1, size))
    values = jnp.concatenate(head_parts(joint, where, 2, size))
    for place in reversed(range(seq)):
        length = (place + 1) * block
        spot = where[place]
        query = joint[spot, 0, :, :size]
        flow_here = flow[spot, 0]
        raised, sums = masked_exp(query, keys[:length], scaling)
        probs = raised * (1.0 / sums)
        weights = probs.astype(BF)
        prob_back = cols_product(flow_here, values[:length])
        mean_back = jnp.sum(probs * prob_back, axis=-1, keepdims=True)
        logit_back = (probs * (prob_back - mean_back)).astype(BF)
        joint_back[spot, 0, :, :size] = (product(logit_back, keys[:length]) * scaling).astype(BF)
        key_term = rows_product(logit_back, query) * scaling
        value_term = rows_product(weights, flow_here)
        if place == seq - 1:
            key_sum[...] = key_term
            value_sum[...] = value_term
        else:
            key_sum[:length] += key_term
            value_sum[:length] += value_term
    for place in range(seq):
        rows = slice(place * block, (place + 1) * block)
        joint_back[where[place], 0, :, size : 2 * size] = key_sum[rows].astype(BF)
        joint_back[where[place], 0, :, 2 * size :] = value_sum[rows].astype(BF)

    @pl.when(here == final)
    def _():
        for copy in loads:
            copy.wait()
        for half, (spot, corner, copy) in enumerate(later):
            now[corner].wait_recv()
            add_into(held, half, extra, half, 256)
            copy.start()
        for spot, copy in now.items():
            copy.wait_send()
            if spot not in [corner for _, corner, _ in later]:
                copy.wait_recv()
        for _, _, copy in later:
            copy.wait()


def attend_back(plan, joint, flow, terms, size, scaling):
    seq, slots, block, width = joint.shape
    heads = width // (3 * size)
    anywhere = pl.BlockSpec(memory_space=pl.ANY)
    wide = pl.BlockSpec((seq, 1, block, 3 * size), lambda slot, head: (0, slot, 0, head))
    return pl.pallas_call(
        functools.partial(attend_back_kernel, scaling, plan),
        out_shape=[
            jax.ShapeDtypeStruct(joint.shape, BF),
            jax.ShapeDtypeStruct((landings(seq),) + terms.shape[1:], BF),
        ],
        grid=(slots, heads),
        in_specs=[wide, pl.BlockSpec((seq, 1, block, size), lambda slot, head: (0, slot, 0, head)), anywhere],
        out_specs=[wide, anywhere],
        scratch_shapes=[pltpu.VMEM((seq * block, size), F32)] * 2
        + [pltpu.VMEM((2,) + terms.shape[1:], BF)] * 2
        + [pltpu.SemaphoreType.DMA((2,))]
        + [pltpu.SemaphoreType.DMA((terms.shape[0],))] * 2,
        compiler_params=pltpu.CompilerParams(
            collective_id=4, has_side_effects=True, vmem_limit_bytes=48 << 20
        ),
        cost_estimate=pl.CostEstimate(flops=0, bytes_accessed=240 << 20, transcendentals=0),
        name="attend_back",
    )(joint, flow, terms)


def forward_back_kernel(
    seq, chunk, mine, upstream, up, down, normed_all, hidden, expanded_back, result, flow_all,
    normed, flow, extra, load, store, send, recv, send_flow, recv_flow,
):
    model, width = up.shape
    rows = normed.shape[1]
    pull = math.sqrt(2.0 / math.pi)
    me_seq, me_dp = lax.axis_index("seq"), lax.axis_index("dp")
    here = pl.program_id(0)
    order, moves = forward_back_plan(seq)
    steps = len(order)
    copies = {}
    for source, target, step, begin in moves:
        copies[target] = pltpu.make_async_remote_copy(
            normed.at[source], normed.at[target], send.at[target], recv.at[target],
            (partner(me_seq, step, seq)[0], me_dp), MESH,
        )
    backs, later = returns(seq, order, me_seq, me_dp, lambda spot: flow.at[spot], extra, flow_all, send_flow, recv_flow)
    owns = [pltpu.make_async_copy(flow.at[spot], flow_all.at[spot], recv_flow.at[spot]) for spot in range(2)]
    stores = [pltpu.make_async_copy(normed.at[spot], normed_all.at[spot], store.at[spot]) for spot in range(steps)]

    @pl.when(here == 0)
    def _():
        fetches = [
            pltpu.make_async_copy(mine.at[pl.ds(half * rows, rows)], normed.at[half], load.at[half]) for half in range(2)
        ]
        for fetch in fetches:
            fetch.start()
        barrier = pltpu.get_barrier_semaphore()
        for step in range(1, seq):
            pl.semaphore_signal(barrier, inc=1, device_id=(lax.rem(me_seq + step, seq), me_dp), device_id_type=MESH)
        for fetch in fetches:
            fetch.wait()
        pl.semaphore_wait(barrier, seq - 1)

    for spot in range(steps):

        @pl.when(here == spot)
        def _(spot=spot):
            if spot > 1:
                copies[spot].wait_recv()
            for source, target, step, begin in moves:
                if begin == spot:
                    copies[target].start()
            stores[spot].start()

    def inner(step, carry):
        columns = pl.ds(pl.multiple_of(step * chunk, chunk), chunk)
        expanded = product(normed[here], up[:, columns])
        pulled = cols_product(upstream[0], down[columns, :])
        square = expanded * expanded
        bend = jnp.tanh(pull * (expanded + 0.044715 * (square * expanded)))
        half = 0.5 * (1.0 + bend)
        hidden[0, :, columns] = (expanded * half).astype(BF)
        slope = half + (0.5 * pull) * expanded * (1.0 - bend * bend) * (1.0 + 0.134145 * square)
        expanded_back[0, :, columns] = (pulled * slope).astype(BF)
        return carry

    lax.fori_loop(0, width // chunk, inner, 0)

    def outer(step, carry):
        columns = pl.ds(pl.multiple_of(step * chunk, chunk), chunk)
        flow[here, :, columns] = cols_product(expanded_back[0], up[columns, :]).astype(BF)
        return carry

    lax.fori_loop(0, model // chunk, outer, 0)
    for spot in range(steps):

        @pl.when(here == spot)
        def _(spot=spot):
            if spot in backs:
                backs[spot].start()
            elif spot < 2:
                owns[spot].start()

    def last(step, carry):
        columns = pl.ds(pl.multiple_of(step * chunk, chunk), chunk)
        result[0, :, columns] = product(hidden[0], down[:, columns]).astype(BF)
        return carry

    lax.fori_loop(0, model // chunk, last, 0)

    @pl.when(here == steps - 1)
    def _():
        for half, (spot, corner, copy) in enumerate(later):
            backs[corner].wait_recv()
            add_into(flow, spot, extra, half, chunk)
            copy.start()
        for copy in copies.values():
            copy.wait_send()
        for spot, copy in backs.items():
            copy.wait_send()
            if spot not in [corner for _, corner, _ in later]:
                copy.wait_recv()
        for _, _, copy in later:
            copy.wait()
        for copy in stores + owns:
            copy.wait()


def forward_back(mine, upstream, up, down):
    steps, rows, model = upstream.shape
    seq = steps // 2
    width = up.shape[1]
    anywhere = pl.BlockSpec(memory_space=pl.ANY)
    by_step = lambda columns: pl.BlockSpec((1, rows, columns), lambda step: (step, 0, 0))
    whole = lambda shape: pl.BlockSpec(shape, lambda step: (0, 0), pipeline_mode=pl.Buffered(1))
    shape = lambda columns: jax.ShapeDtypeStruct((steps, rows, columns), BF)
    return pl.pallas_call(
        functools.partial(forward_back_kernel, seq, math.gcd(512, math.gcd(width, model))),
        out_shape=[shape(model), shape(width), shape(width), shape(model)]
        + [jax.ShapeDtypeStruct((landings(seq), rows, model), BF)],
        grid=(steps,),
        in_specs=[anywhere, by_step(model), whole(up.shape), whole(down.shape)],
        out_specs=[anywhere, by_step(width), by_step(width), by_step(model), anywhere],
        scratch_shapes=[
            pltpu.VMEM((steps, rows, model), BF),
            pltpu.VMEM((steps, rows, model), BF),
            pltpu.VMEM((2, rows, model), BF),
            pltpu.SemaphoreType.DMA((2,)),
        ]
        + [pltpu.SemaphoreType.DMA((steps,))] * 5,
        compiler_params=pltpu.CompilerParams(
            collective_id=3, has_side_effects=True, vmem_limit_bytes=56 << 20
        ),
        cost_estimate=pl.CostEstimate(
            flops=8 * steps * rows * model * width, bytes_accessed=400 << 20, transcendentals=steps * rows * width
        ),
        name="forward_back",
    )(mine, upstream, up, down)


def make_layer(seq, dp):
    xor = seq & (seq - 1) == 0

    def shift(values, step):
        pairs = [(i, i ^ step if xor else (i + step) % seq) for i in range(seq)]
        return lax.ppermute(values, "seq", pairs)

    def gather_seq(block, event=None):
        if seq != 4:
            return [block] + [shift(block, step) for step in range(1, seq)]
        half = block.shape[0] // 2
        near, far = shift(block, 1), shift(block, 2)
        halves = near[:half], far[half:]
        if event is not None:
            halves = after(halves, event)
        return [block, near, far, jnp.concatenate([shift(halves[0], 2), shift(halves[1], 1)])]

    def scatter_seq(make, event=None, begun=None):
        if seq != 4:
            sent = [shift(make(step).astype(BF), step if xor else seq - step).astype(F32) for step in range(1, seq)]
            return make(0) + sum(sent)
        corner = make(3).astype(BF)
        half = corner.shape[0] // 2
        by_near, by_far = shift(corner[:half], 1), shift(corner[half:], 2)
        near = lax.optimization_barrier(make(1).astype(BF))
        far = lax.optimization_barrier(make(2).astype(BF))
        near_first, far_last = shift(near[:half], 1), shift(far[half:], 2)
        if event is not None:
            by_near, by_far = after((by_near, by_far), event)
        if begun is not None:
            begun.extend([by_near, by_far])
        near_last = shift((near[half:].astype(F32) + by_far.astype(F32)).astype(BF), 1)
        far_first = shift((far[:half].astype(F32) + by_near.astype(F32)).astype(BF), 2)
        first = near_first.astype(F32) + far_first.astype(F32)
        last = near_last.astype(F32) + far_last.astype(F32)
        return make(0) + jnp.concatenate([first, last])

    def column_pieces(shard, thirds, groups):
        rows, columns = shard.shape
        shaped = shard.reshape(rows, thirds, seq, groups, -1).transpose(2, 0, 3, 1, 4)
        return shaped.reshape(seq, rows, columns // seq)

    def gather_columns(swapped):
        return lax.all_gather(swapped, "dp", axis=1, tiled=True).reshape(-1, swapped.shape[2])

    def scatter_columns(term):
        total, width = term.shape
        rows = total // (seq * dp)
        summed = lax.psum_scatter(
            term.astype(BF).reshape(seq, dp * rows, width), "dp", scatter_dimension=1, tiled=True
        )
        return summed

    def column_rows(swapped, thirds, groups):
        _, rows, width = swapped.shape
        shaped = swapped.reshape(seq, rows, groups, thirds, -1).transpose(1, 3, 0, 2, 4)
        return shaped.reshape(rows, seq * width).astype(F32)

    def scatter_rows(term):
        return lax.psum_scatter(term.astype(BF), "dp", scatter_dimension=0, tiled=True).astype(F32)

    def layer(
        inputs, counts, cotangent, stretch, offset, inward, outward, dilation, translation, upward, downward
    ):
        slots, block, model = inputs.shape
        size = model // HEADS
        heads = HEADS // seq
        scaling = 1.0 / math.sqrt(size)
        local_rows = slots * block
        total = seq * local_rows
        live = jnp.repeat((jnp.arange(slots) < counts[0]).astype(F32), block)[:, None]
        residual = inputs.reshape(local_rows, model)
        small = jnp.stack([stretch, offset, dilation, translation]).astype(F32).reshape(-1)
        taken = small.shape[0]
        small = jnp.pad(small, (0, -taken % 1024)).reshape(-1, 128)
        swapped_in, swapped_up, small, matrix_out = opening(
            seq, dp, column_pieces(inward, 3, heads), column_pieces(upward, 1, 1), small, outward
        )
        matrix_out = matrix_out.reshape(-1, model)
        small = small.reshape(dp, seq, -1)[:, :, :taken].reshape(dp, seq, 4, -1).transpose(2, 1, 0, 3).reshape(4, model)
        gain_one, shift_one, gain_two, shift_two = small[0], small[1], small[2], small[3]
        matrix_in = gather_columns(swapped_in)
        blocks = gather_seq(after(residual, swapped_in))
        upstream = (cotangent.astype(F32).reshape(local_rows, model) * live).astype(BF)
        def piece(values, step):
            return values[step * local_rows : (step + 1) * local_rows]

        def norm_one(values):
            return (norm_parts(values.astype(F32))[0] * gain_one + shift_one).astype(BF)

        normed = [norm_one(part) for part in blocks]
        projected = jnp.concatenate([product(part, matrix_in).astype(BF) for part in normed])
        normed = jnp.concatenate(normed)
        upstream_all = gather_seq(after(upstream, blocks[-1]), projected)
        matrix_up = gather_columns(after(swapped_up, (matrix_in, blocks[-1])))
        me = lax.axis_index("seq")
        where = me ^ jnp.arange(seq) if xor else (me + seq - jnp.arange(seq)) % seq
        joint = projected.reshape(seq, slots, block, -1)
        attended = attend(where, joint, size, scaling).reshape(total, heads * size)
        begun = []
        middle = residual.astype(F32) + scatter_seq(lambda step: product(piece(attended, step), matrix_out), None, begun)
        matrix_down = lax.all_gather(after(downward, (matrix_up, begun, upstream_all[1:3])), "dp", axis=0, tiled=True)
        unit_two, root_two = norm_parts(middle)
        mine = (unit_two * gain_two + shift_two).astype(BF)
        half = local_rows // 2
        plan = forward_back_plan(seq)[0]
        upstream_all = jnp.stack([upstream_all[step][part * half : (part + 1) * half] for step, part in plan])
        normed_two, hidden, expanded_back, down_terms, two_terms = forward_back(mine, upstream_all, matrix_up, matrix_down)

        def flat(values):
            return values.reshape(-1, values.shape[-1])

        down_sum = rows_product(flat(hidden), flat(upstream_all))
        spots = [[spot for spot, (_, part) in enumerate(plan) if part == which and spot < landings(seq)] for which in range(2)]

        def over_plan(values):
            return jnp.concatenate([sum(values[spot].astype(F32) for spot in places) for places in spots])

        two_back = over_plan(two_terms)
        downward_delta = scatter_rows(down_sum)
        middle_flow, dilation_term, translation_term = norm_back(two_back, unit_two, root_two, gain_two)
        middle_back = upstream.astype(F32) + middle_flow
        up_sum = rows_product(after(flat(normed_two), down_sum), flat(expanded_back))
        middle_low = gather_seq(after(middle_back.astype(BF), up_sum))
        heads_back = jnp.concatenate([cols_product(part, matrix_out).astype(BF) for part in middle_low])
        out_sum = rows_product(attended, jnp.concatenate(middle_low))
        heads_back = after(heads_back, (downward_delta, up_sum)).reshape(seq, slots, block, -1)
        summed_up = scatter_columns(after(up_sum, heads_back))
        projected_back, result_terms = attend_back(plan, joint, heads_back, down_terms, size, scaling)
        projected_back = projected_back.reshape(total, -1)
        result = middle + over_plan([down_terms[0], down_terms[1]] + [result_terms[spot] for spot in range(2, landings(seq))])
        outputs = (result * live).astype(BF).reshape(slots, block, model)
        one_terms = [cols_product(piece(projected_back, step), matrix_in) for step in range(seq)]
        one_terms = [one_terms[0]] + lax.optimization_barrier([part.astype(BF) for part in one_terms[1:]])
        near_up = [lax.dynamic_index_in_dim(summed_up, where[step], 0, keepdims=False) for step in range(seq)]
        near_up = jnp.stack([near_up[0]] + [shift(near_up[step], step if xor else seq - step) for step in range(1, seq)])
        if not xor:
            near_up = near_up[(-jnp.arange(seq)) % seq]
        upward_delta = jnp.concatenate(
            [lax.dynamic_index_in_dim(near_up, where[step], 0, keepdims=False) for step in range(seq)], axis=1
        ).astype(F32)
        in_sum = rows_product(after(normed, (summed_up, one_terms[1:])), projected_back)
        summed_in = scatter_columns(in_sum)
        outward_delta = scatter_rows(after(out_sum, summed_in))
        one_back = scatter_seq(lambda step: one_terms[step])
        unit_one, root_one = norm_parts(residual.astype(F32))
        input_flow, stretch_term, offset_term = norm_back(one_back, unit_one, root_one, gain_one)
        terms = jnp.stack([stretch_term, offset_term, dilation_term, translation_term])
        terms = terms.reshape(4, seq, dp, -1).transpose(1, 2, 0, 3).reshape(seq, dp, -1)
        terms = jnp.pad(terms, ((0, 0), (0, 0), (0, -taken % 1024))).reshape(seq, dp, -1, 128)
        deltas, swapped_in = closing(seq, dp, terms, summed_in)
        inward_delta = column_rows(swapped_in, 3, heads)
        deltas = deltas.reshape(-1)[:taken].reshape(4, -1)
        input_delta = (middle_back + input_flow).reshape(slots, block, model)
        return (
            outputs,
            input_delta,
            deltas[0],
            deltas[1],
            inward_delta,
            outward_delta,
            deltas[2],
            deltas[3],
            upward_delta,
            downward_delta,
        )

    return layer


def solution(mesh):
    tokens, vector, matrix = P("dp", "seq", None), P(("seq", "dp")), P(("seq", "dp"), None)
    return jax.shard_map(
        make_layer(mesh.shape["seq"], mesh.shape["dp"]),
        mesh=mesh,
        in_specs=(tokens, P("dp"), tokens, vector, vector, matrix, matrix, vector, vector, matrix, matrix),
        out_specs=(tokens, tokens, vector, vector, matrix, matrix, vector, vector, matrix, matrix),
        check_vma=False,
    )
```

```python
import functools
import math

import jax
import jax.numpy as jnp
from jax import lax
from jax.experimental import pallas as pl
from jax.experimental.pallas import tpu as pltpu
from jax.sharding import PartitionSpec as P

HEADS = 16
EPSILON = 1e-05
MASKED = -1e30
BF = jnp.bfloat16
F32 = jnp.float32
MESH = pl.DeviceIdType.MESH


def norm_parts(values):
    average = jnp.mean(values, axis=-1, keepdims=True)
    centered = values - average
    root = lax.rsqrt(jnp.mean(centered * centered, axis=-1, keepdims=True) + EPSILON)
    return centered * root, root


def norm_back(flow, unit, root, gain):
    scaled = flow * gain
    first = jnp.mean(scaled, axis=-1, keepdims=True)
    second = jnp.mean(scaled * unit, axis=-1, keepdims=True)
    return root * (scaled - first - unit * second), jnp.sum(flow * unit, axis=0), jnp.sum(flow, axis=0)


def rows_product(left, right):
    return lax.dot_general(left, right, (((0,), (0,)), ((), ())), preferred_element_type=F32)


def cols_product(left, right):
    return lax.dot_general(left, right, (((1,), (1,)), ((), ())), preferred_element_type=F32)


def product(left, right):
    return jnp.dot(left, right, preferred_element_type=F32)


def after(values, event):
    return lax.optimization_barrier((values, event))[0]


def greet(seq, dp, me_seq, me_dp):
    barrier = pltpu.get_barrier_semaphore()
    for step in range(1, seq):
        pl.semaphore_signal(barrier, inc=1, device_id=(lax.rem(me_seq + step, seq), me_dp), device_id_type=MESH)
    for step in range(1, dp):
        pl.semaphore_signal(barrier, inc=1, device_id=(me_seq, lax.rem(me_dp + step, dp)), device_id_type=MESH)
    pl.semaphore_wait(barrier, seq + dp - 2)


def start_trade(seq, me_seq, me_dp, pieces, swapped, own, send, recv):
    copies = [pltpu.make_async_copy(pieces.at[me_seq], swapped.at[me_seq], own)]
    copies[0].start()
    for step in range(1, seq):
        target = lax.rem(me_seq + step, seq)
        copies.append(
            pltpu.make_async_remote_copy(
                pieces.at[target], swapped.at[me_seq], send.at[step], recv.at[step], (target, me_dp), MESH
            )
        )
        copies[-1].start()
    return copies


def opening_kernel(
    seq, dp, pieces, pieces_two, small, shard, swapped, swapped_two, params, shards,
    own, send, recv, send_two, recv_two, send_small, recv_small, send_row, recv_row, send_shard, recv_shard, send_next, recv_next,
):
    me_seq, me_dp = lax.axis_index("seq"), lax.axis_index("dp")
    greet(seq, dp, me_seq, me_dp)
    keep = pltpu.make_async_copy(small, params.at[me_dp, me_seq], own.at[0])
    keep.start()
    tiny, rows = [], []
    for step in range(1, seq):
        target = lax.rem(me_seq + step, seq)
        tiny.append(
            pltpu.make_async_remote_copy(
                small, params.at[me_dp, me_seq], send_small.at[step], recv_small.at[step], (target, me_dp), MESH
            )
        )
        tiny[-1].start()
    large = start_trade(seq, me_seq, me_dp, pieces, swapped, own.at[1], send, recv)
    span = 1 if dp % 2 else 2
    keep_shard = pltpu.make_async_copy(shard, shards.at[me_dp], own.at[3])
    keep_shard.start()
    firsts = []
    for step in range(1, dp // span):
        target = lax.rem(me_dp + span * step, dp)
        firsts.append(
            pltpu.make_async_remote_copy(
                shard, shards.at[me_dp], send_shard.at[step], recv_shard.at[step], (me_seq, target), MESH
            )
        )
        firsts[-1].start()
    large += start_trade(seq, me_seq, me_dp, pieces_two, swapped_two, own.at[2], send_two, recv_two)
    for copy in [keep] + tiny:
        copy.wait()
    for step in range(1, dp):
        target = lax.rem(me_dp + step, dp)
        rows.append(
            pltpu.make_async_remote_copy(
                params.at[me_dp], params.at[me_dp], send_row.at[step], recv_row.at[step], (me_seq, target), MESH
            )
        )
        rows[-1].start()
    keep_shard.wait()
    for step in range(dp // span):
        if step:
            firsts[step - 1].wait()
        if span == 2:
            origin = lax.rem(me_dp + dp - span * step, dp)
            sibling = me_dp + 1 - 2 * lax.rem(me_dp, 2)
            rows.append(
                pltpu.make_async_remote_copy(
                    shards.at[origin], shards.at[origin], send_next.at[step], recv_next.at[step], (me_seq, sibling), MESH
                )
            )
            rows[-1].start()
    for copy in rows + large:
        copy.wait()


def opening(seq, dp, pieces, pieces_two, small, shard):
    anywhere = pl.BlockSpec(memory_space=pl.ANY)
    return pl.pallas_call(
        functools.partial(opening_kernel, seq, dp),
        out_shape=(
            jax.ShapeDtypeStruct(pieces.shape, pieces.dtype),
            jax.ShapeDtypeStruct(pieces_two.shape, pieces_two.dtype),
            jax.ShapeDtypeStruct((dp, seq) + small.shape, small.dtype),
            jax.ShapeDtypeStruct((dp,) + shard.shape, shard.dtype),
        ),
        in_specs=[anywhere] * 4,
        out_specs=(anywhere,) * 4,
        scratch_shapes=[pltpu.SemaphoreType.DMA((4,))]
        + [pltpu.SemaphoreType.DMA((seq,))] * 6
        + [pltpu.SemaphoreType.DMA((dp,))] * 6,
        compiler_params=pltpu.CompilerParams(collective_id=1, has_side_effects=True),
        name="opening",
    )(pieces, pieces_two, small, shard)


def closing_kernel(
    seq, dp, groups, terms, pieces, total, whole, swapped, over_seq, partial, over_dp,
    own, send, recv, send_seq, recv_seq, send_row, recv_row,
):
    me_seq, me_dp = lax.axis_index("seq"), lax.axis_index("dp")
    greet(seq, dp, me_seq, me_dp)
    copies = []
    for step in range(1, seq):
        target = lax.rem(me_seq + step, seq)
        copies.append(
            pltpu.make_async_remote_copy(
                terms.at[target], over_seq.at[step], send_seq.at[step], recv_seq.at[step], (target, me_dp), MESH
            )
        )
        copies[-1].start()
    large = start_trade(seq, me_seq, me_dp, pieces, swapped, own, send, recv)
    value = terms[me_seq]
    for step, copy in enumerate(copies):
        copy.wait()
        value = value + over_seq[step + 1]
    partial[...] = value
    copies = []
    for step in range(1, dp):
        target = lax.rem(me_dp + step, dp)
        copies.append(
            pltpu.make_async_remote_copy(
                partial.at[target], over_dp.at[step], send_row.at[step], recv_row.at[step], (me_seq, target), MESH
            )
        )
        copies[-1].start()
    value = partial[me_dp]
    for step, copy in enumerate(copies):
        copy.wait()
        value = value + over_dp[step + 1]
    total[...] = value
    for copy in large:
        copy.wait()
    size = whole.shape[1] // (3 * seq * groups)
    for source in range(seq):
        for group in range(groups):
            for third in range(3):
                place = ((third * seq + source) * groups + group) * size
                piece = swapped[source, :, (group * 3 + third) * size : (group * 3 + third + 1) * size]
                whole[:, place : place + size] = piece.astype(F32)


def closing(seq, dp, groups, terms, pieces):
    tile = terms.shape[2:]
    inside, anywhere = pl.BlockSpec(memory_space=pltpu.VMEM), pl.BlockSpec(memory_space=pl.ANY)
    return pl.pallas_call(
        functools.partial(closing_kernel, seq, dp, groups),
        out_shape=(
            jax.ShapeDtypeStruct(tile, F32),
            jax.ShapeDtypeStruct((pieces.shape[1], seq * pieces.shape[2]), F32),
        ),
        in_specs=[inside, anywhere],
        out_specs=(inside, inside),
        scratch_shapes=[
            pltpu.VMEM(pieces.shape, BF),
            pltpu.VMEM(terms.shape, F32),
            pltpu.VMEM(terms.shape[1:], F32),
            pltpu.VMEM(terms.shape[1:], F32),
            pltpu.SemaphoreType.DMA,
        ]
        + [pltpu.SemaphoreType.DMA((seq,))] * 4
        + [pltpu.SemaphoreType.DMA((dp,))] * 2,
        compiler_params=pltpu.CompilerParams(collective_id=2, has_side_effects=True),
        name="closing",
    )(terms, pieces)


def head_parts(ref, where, part, size):
    return [ref[where[place], 0, :, part * size : (part + 1) * size] for place in range(ref.shape[0])]


def diagonal(block):
    return lax.broadcasted_iota(jnp.int32, (block, block), 1) <= lax.broadcasted_iota(jnp.int32, (block, block), 0)


def masked_exp(query, keys, scaling):
    logits = cols_product(query, keys) * scaling
    block, length = logits.shape
    last = jnp.where(diagonal(block), logits[:, length - block :], MASKED)
    logits = last if length == block else jnp.concatenate([logits[:, : length - block], last], axis=1)
    raised = jnp.exp(logits - jnp.max(logits, axis=-1, keepdims=True))
    return raised, jnp.sum(raised, axis=-1, keepdims=True)


def attend_kernel(scaling, where, joint, attended):
    seq, _, block, size = attended.shape
    keys = jnp.concatenate(head_parts(joint, where, 1, size))
    values = jnp.concatenate(head_parts(joint, where, 2, size))
    for place in range(seq):
        length = (place + 1) * block
        query = joint[where[place], 0, :, :size]
        raised, sums = masked_exp(query, keys[:length], scaling)
        weights = (raised * (1.0 / sums)).astype(BF)
        attended[where[place], 0] = product(weights, values[:length]).astype(BF)


def attend(where, joint, size, scaling):
    seq, slots, block, width = joint.shape
    heads = width // (3 * size)
    return pl.pallas_call(
        functools.partial(attend_kernel, scaling),
        out_shape=jax.ShapeDtypeStruct((seq, slots, block, heads * size), BF),
        grid=(slots, heads),
        in_specs=[
            pl.BlockSpec(memory_space=pltpu.SMEM),
            pl.BlockSpec((seq, 1, block, 3 * size), lambda slot, head: (0, slot, 0, head)),
        ],
        out_specs=pl.BlockSpec((seq, 1, block, size), lambda slot, head: (0, slot, 0, head)),
        compiler_params=pltpu.CompilerParams(vmem_limit_bytes=48 << 20),
        cost_estimate=pl.CostEstimate(flops=0, bytes_accessed=slots * (30 << 20), transcendentals=0),
        name="attend",
    )(where, joint)


def partner(me, step, count):
    if count & (count - 1):
        return lax.rem(me + step, count), lax.rem(me + count - step, count)
    bit = 1
    while bit < count:
        if step & bit:
            me = me + bit * (1 - 2 * lax.rem(me // bit, 2))
        bit *= 2
    return me, me


def forward_back_plan(seq):
    if seq == 4:
        order = [(0, 0), (0, 1), (1, 0), (2, 0), (1, 1), (2, 1), (3, 0), (3, 1)]
    else:
        order = [(step, half) for step in range(seq) for half in range(2)]
    at = {pair: spot for spot, pair in enumerate(order)}
    moves = []
    for step, half in order[2:]:
        if seq == 4 and step == 3:
            source = (1, 0) if half == 0 else (2, 1)
            moves.append((at[source], at[step, half], step - source[0], at[source]))
        else:
            moves.append((at[0, half], at[step, half], step, half))
    return order, moves


def returns(seq, plan, me_seq, me_dp, parts, extra, landing, send, recv):
    def copy(source, target, step, spot):
        device = (partner(me_seq, step, seq)[1], me_dp)
        return pltpu.make_async_remote_copy(source, target, send.at[spot], recv.at[spot], device, MESH)

    if seq != 4:
        return {spot: copy(parts(spot), landing.at[spot], step, spot) for spot, (step, _) in enumerate(plan) if step}, []
    at = {pair: spot for spot, pair in enumerate(plan)}
    now = {spot: copy(parts(spot), landing.at[spot], plan[spot][0], spot) for spot in (at[1, 0], at[2, 1])}
    now[at[3, 0]] = copy(parts(at[3, 0]), extra.at[0], 1, at[3, 0])
    now[at[3, 1]] = copy(parts(at[3, 1]), extra.at[1], 2, at[3, 1])
    later = []
    for half, spot in enumerate((at[2, 0], at[1, 1])):
        later.append((spot, at[3, half], copy(parts(spot), landing.at[spot], plan[spot][0], spot)))
    return now, later


def landings(seq):
    return 6 if seq == 4 else 2 * seq


def add_into(ref, spot, other, half, chunk):
    def body(step, carry):
        columns = pl.ds(pl.multiple_of(step * chunk, chunk), chunk)
        ref[spot, :, columns] = (ref[spot, :, columns].astype(F32) + other[half, :, columns].astype(F32)).astype(BF)
        return carry

    lax.fori_loop(0, ref.shape[2] // chunk, body, 0)


def attend_back_kernel(
    scaling, plan, joint, flow, terms, joint_back, terms_all, key_sum, value_sum, extra, held, load, send, recv
):
    seq, _, block, size = flow.shape
    me_seq, me_dp = lax.axis_index("seq"), lax.axis_index("dp")
    here = pl.program_id(0) * pl.num_programs(1) + pl.program_id(1)
    final = pl.num_programs(0) * pl.num_programs(1) - 1
    delayed = {spot: half for half, spot in enumerate([plan.index((2, 0)), plan.index((1, 1))])} if seq == 4 else {}
    now, later = returns(
        seq, plan, me_seq, me_dp, lambda spot: held.at[delayed[spot]] if spot in delayed else terms.at[spot],
        extra, terms_all, send, recv,
    )
    loads = [pltpu.make_async_copy(terms.at[spot], held.at[half], load.at[half]) for spot, half in delayed.items()]

    @pl.when(here == 0)
    def _():
        for copy in loads:
            copy.start()
        greet(seq, 1, me_seq, me_dp)
        for copy in now.values():
            copy.start()

    where = [partner(me_seq, place, seq)[1] for place in range(seq)]
    keys = jnp.concatenate(head_parts(joint, where, 1, size))
    values = jnp.concatenate(head_parts(joint, where, 2, size))
    for place in reversed(range(seq)):
        length = (place + 1) * block
        spot = where[place]
        query = joint[spot, 0, :, :size]
        flow_here = flow[spot, 0]
        raised, sums = masked_exp(query, keys[:length], scaling)
        probs = raised * (1.0 / sums)
        weights = probs.astype(BF)
        prob_back = cols_product(flow_here, values[:length])
        mean_back = jnp.sum(probs * prob_back, axis=-1, keepdims=True)
        logit_back = (probs * (prob_back - mean_back)).astype(BF)
        joint_back[spot, 0, :, :size] = (product(logit_back, keys[:length]) * scaling).astype(BF)
        key_term = rows_product(logit_back, query) * scaling
        value_term = rows_product(weights, flow_here)
        if place == seq - 1:
            key_sum[...] = key_term
            value_sum[...] = value_term
        else:
            key_sum[:length] += key_term
            value_sum[:length] += value_term
    for place in range(seq):
        rows = slice(place * block, (place + 1) * block)
        joint_back[where[place], 0, :, size : 2 * size] = key_sum[rows].astype(BF)
        joint_back[where[place], 0, :, 2 * size :] = value_sum[rows].astype(BF)

    @pl.when(here == final)
    def _():
        for copy in loads:
            copy.wait()
        for half, (spot, corner, copy) in enumerate(later):
            now[corner].wait_recv()
            add_into(held, half, extra, half, 256)
            copy.start()
        for spot, copy in now.items():
            copy.wait_send()
            if spot not in [corner for _, corner, _ in later]:
                copy.wait_recv()
        for _, _, copy in later:
            copy.wait()


def attend_back(plan, joint, flow, terms, size, scaling):
    seq, slots, block, width = joint.shape
    heads = width // (3 * size)
    anywhere = pl.BlockSpec(memory_space=pl.ANY)
    wide = pl.BlockSpec((seq, 1, block, 3 * size), lambda slot, head: (0, slot, 0, head))
    return pl.pallas_call(
        functools.partial(attend_back_kernel, scaling, plan),
        out_shape=[
            jax.ShapeDtypeStruct(joint.shape, BF),
            jax.ShapeDtypeStruct((landings(seq),) + terms.shape[1:], BF),
        ],
        grid=(slots, heads),
        in_specs=[wide, pl.BlockSpec((seq, 1, block, size), lambda slot, head: (0, slot, 0, head)), anywhere],
        out_specs=[wide, anywhere],
        scratch_shapes=[pltpu.VMEM((seq * block, size), F32)] * 2
        + [pltpu.VMEM((2,) + terms.shape[1:], BF)] * 2
        + [pltpu.SemaphoreType.DMA((2,))]
        + [pltpu.SemaphoreType.DMA((terms.shape[0],))] * 2,
        compiler_params=pltpu.CompilerParams(
            collective_id=4, has_side_effects=True, vmem_limit_bytes=48 << 20
        ),
        cost_estimate=pl.CostEstimate(flops=0, bytes_accessed=240 << 20, transcendentals=0),
        name="attend_back",
    )(joint, flow, terms)


def forward_back_kernel(
    seq, chunk, mine, upstream, up, down, normed_all, hidden, expanded_back, result, flow_all,
    normed, flow, extra, load, store, send, recv, send_flow, recv_flow,
):
    model, width = up.shape
    rows = normed.shape[1]
    pull = math.sqrt(2.0 / math.pi)
    me_seq, me_dp = lax.axis_index("seq"), lax.axis_index("dp")
    here = pl.program_id(0)
    order, moves = forward_back_plan(seq)
    steps = len(order)
    copies = {}
    for source, target, step, begin in moves:
        copies[target] = pltpu.make_async_remote_copy(
            normed.at[source], normed.at[target], send.at[target], recv.at[target],
            (partner(me_seq, step, seq)[0], me_dp), MESH,
        )
    backs, later = returns(seq, order, me_seq, me_dp, lambda spot: flow.at[spot], extra, flow_all, send_flow, recv_flow)
    owns = [pltpu.make_async_copy(flow.at[spot], flow_all.at[spot], recv_flow.at[spot]) for spot in range(2)]
    stores = [pltpu.make_async_copy(normed.at[spot], normed_all.at[spot], store.at[spot]) for spot in range(steps)]

    @pl.when(here == 0)
    def _():
        fetches = [
            pltpu.make_async_copy(mine.at[pl.ds(half * rows, rows)], normed.at[half], load.at[half]) for half in range(2)
        ]
        for fetch in fetches:
            fetch.start()
        barrier = pltpu.get_barrier_semaphore()
        for step in range(1, seq):
            pl.semaphore_signal(barrier, inc=1, device_id=(lax.rem(me_seq + step, seq), me_dp), device_id_type=MESH)
        for fetch in fetches:
            fetch.wait()
        pl.semaphore_wait(barrier, seq - 1)

    for spot in range(steps):

        @pl.when(here == spot)
        def _(spot=spot):
            if spot > 1:
                copies[spot].wait_recv()
            for source, target, step, begin in moves:
                if begin == spot:
                    copies[target].start()
            stores[spot].start()

    def inner(step, carry):
        columns = pl.ds(pl.multiple_of(step * chunk, chunk), chunk)
        expanded = product(normed[here], up[:, columns])
        pulled = cols_product(upstream[0], down[columns, :])
        square = expanded * expanded
        bend = jnp.tanh(pull * (expanded + 0.044715 * (square * expanded)))
        half = 0.5 * (1.0 + bend)
        hidden[0, :, columns] = (expanded * half).astype(BF)
        slope = half + (0.5 * pull) * expanded * (1.0 - bend * bend) * (1.0 + 0.134145 * square)
        expanded_back[0, :, columns] = (pulled * slope).astype(BF)
        return carry

    lax.fori_loop(0, width // chunk, inner, 0)

    def outer(step, carry):
        columns = pl.ds(pl.multiple_of(step * chunk, chunk), chunk)
        flow[here, :, columns] = cols_product(expanded_back[0], up[columns, :]).astype(BF)
        return carry

    lax.fori_loop(0, model // chunk, outer, 0)
    for spot in range(steps):

        @pl.when(here == spot)
        def _(spot=spot):
            if spot in backs:
                backs[spot].start()
            elif spot < 2:
                owns[spot].start()

    def last(step, carry):
        columns = pl.ds(pl.multiple_of(step * chunk, chunk), chunk)
        result[0, :, columns] = product(hidden[0], down[:, columns]).astype(BF)
        return carry

    lax.fori_loop(0, model // chunk, last, 0)

    @pl.when(here == steps - 1)
    def _():
        for half, (spot, corner, copy) in enumerate(later):
            backs[corner].wait_recv()
            add_into(flow, spot, extra, half, chunk)
            copy.start()
        for copy in copies.values():
            copy.wait_send()
        for spot, copy in backs.items():
            copy.wait_send()
            if spot not in [corner for _, corner, _ in later]:
                copy.wait_recv()
        for _, _, copy in later:
            copy.wait()
        for copy in stores + owns:
            copy.wait()


def forward_back(mine, upstream, up, down):
    steps, rows, model = upstream.shape
    seq = steps // 2
    width = up.shape[1]
    anywhere = pl.BlockSpec(memory_space=pl.ANY)
    by_step = lambda columns: pl.BlockSpec((1, rows, columns), lambda step: (step, 0, 0))
    whole = lambda shape: pl.BlockSpec(shape, lambda step: (0, 0), pipeline_mode=pl.Buffered(1))
    shape = lambda columns: jax.ShapeDtypeStruct((steps, rows, columns), BF)
    return pl.pallas_call(
        functools.partial(forward_back_kernel, seq, math.gcd(512, math.gcd(width, model))),
        out_shape=[shape(model), shape(width), shape(width), shape(model)]
        + [jax.ShapeDtypeStruct((landings(seq), rows, model), BF)],
        grid=(steps,),
        in_specs=[anywhere, by_step(model), whole(up.shape), whole(down.shape)],
        out_specs=[anywhere, by_step(width), by_step(width), by_step(model), anywhere],
        scratch_shapes=[
            pltpu.VMEM((steps, rows, model), BF),
            pltpu.VMEM((steps, rows, model), BF),
            pltpu.VMEM((2, rows, model), BF),
            pltpu.SemaphoreType.DMA((2,)),
        ]
        + [pltpu.SemaphoreType.DMA((steps,))] * 5,
        compiler_params=pltpu.CompilerParams(
            collective_id=3, has_side_effects=True, vmem_limit_bytes=56 << 20
        ),
        cost_estimate=pl.CostEstimate(
            flops=8 * steps * rows * model * width, bytes_accessed=400 << 20, transcendentals=steps * rows * width
        ),
        name="forward_back",
    )(mine, upstream, up, down)


def send_back_kernel(
    seq, plan, chunk, left, right, pieces, landing, swapped, flow, extra, keep, send, recv, own, send_piece, recv_piece
):
    me_seq, me_dp = lax.axis_index("seq"), lax.axis_index("dp")
    model = right.shape[0]
    now, later = returns(seq, plan, me_seq, me_dp, lambda spot: flow.at[spot], extra, landing, send, recv)
    owns = [pltpu.make_async_copy(flow.at[spot], landing.at[spot], keep.at[spot]) for spot in range(2)]
    greet(seq, 1, me_seq, me_dp)

    def work(spot):
        def body(step, carry):
            columns = pl.ds(pl.multiple_of(step * chunk, chunk), chunk)
            flow[spot, :, columns] = cols_product(left[plan[spot][0] * 2 + plan[spot][1]], right[columns, :]).astype(BF)
            return carry

        lax.fori_loop(0, model // chunk, body, 0)

    corners = [corner for _, corner, _ in later]
    for spot in corners + [spot for spot in now if spot not in corners]:
        work(spot)
        now[spot].start()
    for spot, _, _ in later:
        work(spot)
    for spot in range(2):
        work(spot)
        owns[spot].start()
    for half, (spot, corner, copy) in enumerate(later):
        now[corner].wait_recv()
        add_into(flow, spot, extra, half, chunk)
        copy.start()
    for copy in start_trade(seq, me_seq, me_dp, pieces, swapped, own, send_piece, recv_piece):
        copy.wait()
    for spot, copy in now.items():
        copy.wait_send()
        if spot not in corners:
            copy.wait_recv()
    for _, _, copy in later:
        copy.wait()
    for copy in owns:
        copy.wait()


def send_back(seq, plan, left, right, pieces):
    steps = len(plan)
    model, depth = right.shape
    left = left.reshape(steps, -1, depth)
    rows = left.shape[1]
    inside, anywhere = pl.BlockSpec(memory_space=pltpu.VMEM), pl.BlockSpec(memory_space=pl.ANY)
    return pl.pallas_call(
        functools.partial(send_back_kernel, seq, plan, math.gcd(512, model)),
        out_shape=[
            jax.ShapeDtypeStruct((landings(seq), rows, model), BF),
            jax.ShapeDtypeStruct(pieces.shape, pieces.dtype),
        ],
        in_specs=[inside, inside, anywhere],
        out_specs=[anywhere, anywhere],
        scratch_shapes=[
            pltpu.VMEM((steps, rows, model), BF),
            pltpu.VMEM((2, rows, model), BF),
            pltpu.SemaphoreType.DMA((2,)),
        ]
        + [pltpu.SemaphoreType.DMA((steps,))] * 2
        + [pltpu.SemaphoreType.DMA]
        + [pltpu.SemaphoreType.DMA((seq,))] * 2,
        compiler_params=pltpu.CompilerParams(
            collective_id=5, has_side_effects=True, vmem_limit_bytes=44 << 20
        ),
        cost_estimate=pl.CostEstimate(
            flops=2 * steps * rows * model * depth, bytes_accessed=240 << 20, transcendentals=0
        ),
        name="send_back",
    )(left, right, pieces)


def make_layer(seq, dp):
    xor = seq & (seq - 1) == 0

    def shift(values, step):
        pairs = [(i, i ^ step if xor else (i + step) % seq) for i in range(seq)]
        return lax.ppermute(values, "seq", pairs)

    def gather_seq(block, event=None):
        if seq != 4:
            return [block] + [shift(block, step) for step in range(1, seq)]
        half = block.shape[0] // 2
        near, far = shift(block, 1), shift(block, 2)
        halves = near[:half], far[half:]
        if event is not None:
            halves = after(halves, event)
        return [block, near, far, jnp.concatenate([shift(halves[0], 2), shift(halves[1], 1)])]

    def scatter_seq(make, event=None, begun=None):
        if seq != 4:
            sent = [shift(make(step).astype(BF), step if xor else seq - step).astype(F32) for step in range(1, seq)]
            return make(0) + sum(sent)
        corner = make(3).astype(BF)
        half = corner.shape[0] // 2
        by_near, by_far = shift(corner[:half], 1), shift(corner[half:], 2)
        near = lax.optimization_barrier(make(1).astype(BF))
        far = lax.optimization_barrier(make(2).astype(BF))
        near_first, far_last = shift(near[:half], 1), shift(far[half:], 2)
        if event is not None:
            by_near, by_far = after((by_near, by_far), event)
        if begun is not None:
            begun.extend([by_near, by_far])
        near_last = shift((near[half:].astype(F32) + by_far.astype(F32)).astype(BF), 1)
        far_first = shift((far[:half].astype(F32) + by_near.astype(F32)).astype(BF), 2)
        first = near_first.astype(F32) + far_first.astype(F32)
        last = near_last.astype(F32) + far_last.astype(F32)
        return make(0) + jnp.concatenate([first, last])

    def column_pieces(shard, thirds, groups):
        rows, columns = shard.shape
        shaped = shard.reshape(rows, thirds, seq, groups, -1).transpose(2, 0, 3, 1, 4)
        return shaped.reshape(seq, rows, columns // seq)

    def gather_columns(swapped):
        return lax.all_gather(swapped, "dp", axis=1, tiled=True).reshape(-1, swapped.shape[2])

    def scatter_columns(term):
        total, width = term.shape
        rows = total // (seq * dp)
        summed = lax.psum_scatter(
            term.astype(BF).reshape(seq, dp * rows, width), "dp", scatter_dimension=1, tiled=True
        )
        return summed

    def scatter_rows(term):
        return lax.psum_scatter(term.astype(BF), "dp", scatter_dimension=0, tiled=True).astype(F32)

    def layer(
        inputs, counts, cotangent, stretch, offset, inward, outward, dilation, translation, upward, downward
    ):
        slots, block, model = inputs.shape
        size = model // HEADS
        heads = HEADS // seq
        scaling = 1.0 / math.sqrt(size)
        local_rows = slots * block
        total = seq * local_rows
        live = jnp.repeat((jnp.arange(slots) < counts[0]).astype(F32), block)[:, None]
        residual = inputs.reshape(local_rows, model)
        small = jnp.stack([stretch, offset, dilation, translation]).astype(F32).reshape(-1)
        taken = small.shape[0]
        small = jnp.pad(small, (0, -taken % 1024)).reshape(-1, 128)
        swapped_in, swapped_up, small, matrix_out = opening(
            seq, dp, column_pieces(inward, 3, heads), column_pieces(upward, 1, 1), small, outward
        )
        matrix_out = matrix_out.reshape(-1, model)
        small = small.reshape(dp, seq, -1)[:, :, :taken].reshape(dp, seq, 4, -1).transpose(2, 1, 0, 3).reshape(4, model)
        gain_one, shift_one, gain_two, shift_two = small[0], small[1], small[2], small[3]
        matrix_in = gather_columns(swapped_in)
        blocks = gather_seq(after(residual, swapped_in))
        upstream = (cotangent.astype(F32).reshape(local_rows, model) * live).astype(BF)
        def piece(values, step):
            return values[step * local_rows : (step + 1) * local_rows]

        def norm_one(values):
            return (norm_parts(values.astype(F32))[0] * gain_one + shift_one).astype(BF)

        normed = [norm_one(part) for part in blocks]
        projected = jnp.concatenate([product(part, matrix_in).astype(BF) for part in normed])
        normed = jnp.concatenate(normed)
        upstream_all = gather_seq(after(upstream, blocks[-1]), projected)
        matrix_up = gather_columns(after(swapped_up, (matrix_in, blocks[-1])))
        me = lax.axis_index("seq")
        where = me ^ jnp.arange(seq) if xor else (me + seq - jnp.arange(seq)) % seq
        joint = projected.reshape(seq, slots, block, -1)
        attended = attend(where, joint, size, scaling).reshape(total, heads * size)
        begun = []
        middle = residual.astype(F32) + scatter_seq(lambda step: product(piece(attended, step), matrix_out), None, begun)
        matrix_down = lax.all_gather(after(downward, (matrix_up, begun, upstream_all[1:3])), "dp", axis=0, tiled=True)
        unit_two, root_two = norm_parts(middle)
        mine = (unit_two * gain_two + shift_two).astype(BF)
        half = local_rows // 2
        plan = forward_back_plan(seq)[0]
        upstream_all = jnp.stack([upstream_all[step][part * half : (part + 1) * half] for step, part in plan])
        normed_two, hidden, expanded_back, down_terms, two_terms = forward_back(mine, upstream_all, matrix_up, matrix_down)

        def flat(values):
            return values.reshape(-1, values.shape[-1])

        down_sum = rows_product(flat(hidden), flat(upstream_all))
        spots = [[spot for spot, (_, part) in enumerate(plan) if part == which and spot < landings(seq)] for which in range(2)]

        def over_plan(values):
            return jnp.concatenate([sum(values[spot].astype(F32) for spot in places) for places in spots])

        two_back = over_plan(two_terms)
        downward_delta = scatter_rows(down_sum)
        middle_flow, dilation_term, translation_term = norm_back(two_back, unit_two, root_two, gain_two)
        middle_back = upstream.astype(F32) + middle_flow
        up_sum = rows_product(after(flat(normed_two), down_sum), flat(expanded_back))
        middle_low = gather_seq(after(middle_back.astype(BF), up_sum))
        heads_back = jnp.concatenate([cols_product(part, matrix_out).astype(BF) for part in middle_low])
        out_sum = rows_product(attended, jnp.concatenate(middle_low))
        heads_back = after(heads_back, (downward_delta, up_sum)).reshape(seq, slots, block, -1)
        summed_up = scatter_columns(after(up_sum, heads_back))
        projected_back, result_terms = attend_back(plan, joint, heads_back, down_terms, size, scaling)
        projected_back = projected_back.reshape(total, -1)
        result = middle + over_plan([down_terms[0], down_terms[1]] + [result_terms[spot] for spot in range(2, landings(seq))])
        outputs = (result * live).astype(BF).reshape(slots, block, model)
        in_sum = rows_product(after(normed, (summed_up, outputs)), projected_back)
        summed_in = scatter_columns(in_sum)
        one_terms, swapped_up = send_back(seq, plan, after(projected_back, in_sum), matrix_in, summed_up)
        upward_delta = jnp.concatenate([swapped_up[step] for step in range(seq)], axis=1).astype(F32)
        one_back = over_plan(one_terms)
        outward_delta = scatter_rows(after(out_sum, (summed_in, one_terms)))
        unit_one, root_one = norm_parts(residual.astype(F32))
        input_flow, stretch_term, offset_term = norm_back(one_back, unit_one, root_one, gain_one)
        terms = jnp.stack([stretch_term, offset_term, dilation_term, translation_term])
        terms = terms.reshape(4, seq, dp, -1).transpose(1, 2, 0, 3).reshape(seq, dp, -1)
        terms = jnp.pad(terms, ((0, 0), (0, 0), (0, -taken % 1024))).reshape(seq, dp, -1, 128)
        deltas, inward_delta = closing(seq, dp, heads, terms, summed_in)
        deltas = deltas.reshape(-1)[:taken].reshape(4, -1)
        input_delta = (middle_back + input_flow).reshape(slots, block, model)
        return (
            outputs,
            input_delta,
            deltas[0],
            deltas[1],
            inward_delta,
            outward_delta,
            deltas[2],
            deltas[3],
            upward_delta,
            downward_delta,
        )

    return layer


def solution(mesh):
    tokens, vector, matrix = P("dp", "seq", None), P(("seq", "dp")), P(("seq", "dp"), None)
    return jax.shard_map(
        make_layer(mesh.shape["seq"], mesh.shape["dp"]),
        mesh=mesh,
        in_specs=(tokens, P("dp"), tokens, vector, vector, matrix, matrix, vector, vector, matrix, matrix),
        out_specs=(tokens, tokens, vector, vector, matrix, matrix, vector, vector, matrix, matrix),
        check_vma=False,
    )
```

```python
import functools
import math

import jax
import jax.numpy as jnp
from jax import lax
from jax.experimental import pallas as pl
from jax.experimental.pallas import tpu as pltpu
from jax.sharding import PartitionSpec as P

HEADS = 16
EPSILON = 1e-05
MASKED = -1e30
BF = jnp.bfloat16
F32 = jnp.float32
MESH = pl.DeviceIdType.MESH


def norm_parts(values):
    average = jnp.mean(values, axis=-1, keepdims=True)
    centered = values - average
    root = lax.rsqrt(jnp.mean(centered * centered, axis=-1, keepdims=True) + EPSILON)
    return centered * root, root


def norm_back(flow, unit, root, gain):
    scaled = flow * gain
    first = jnp.mean(scaled, axis=-1, keepdims=True)
    second = jnp.mean(scaled * unit, axis=-1, keepdims=True)
    return root * (scaled - first - unit * second), jnp.sum(flow * unit, axis=0), jnp.sum(flow, axis=0)


def rows_product(left, right):
    return lax.dot_general(left, right, (((0,), (0,)), ((), ())), preferred_element_type=F32)


def cols_product(left, right):
    return lax.dot_general(left, right, (((1,), (1,)), ((), ())), preferred_element_type=F32)


def product(left, right):
    return jnp.dot(left, right, preferred_element_type=F32)


def after(values, event):
    return lax.optimization_barrier((values, event))[0]


def greet(seq, dp, me_seq, me_dp):
    barrier = pltpu.get_barrier_semaphore()
    for step in range(1, seq):
        pl.semaphore_signal(barrier, inc=1, device_id=(lax.rem(me_seq + step, seq), me_dp), device_id_type=MESH)
    for step in range(1, dp):
        pl.semaphore_signal(barrier, inc=1, device_id=(me_seq, lax.rem(me_dp + step, dp)), device_id_type=MESH)
    pl.semaphore_wait(barrier, seq + dp - 2)


def start_trade(seq, me_seq, me_dp, pieces, swapped, own, send, recv):
    copies = [pltpu.make_async_copy(pieces.at[me_seq], swapped.at[me_seq], own)]
    copies[0].start()
    for step in range(1, seq):
        target = lax.rem(me_seq + step, seq)
        copies.append(
            pltpu.make_async_remote_copy(
                pieces.at[target], swapped.at[me_seq], send.at[step], recv.at[step], (target, me_dp), MESH
            )
        )
        copies[-1].start()
    return copies


def opening_kernel(
    seq, dp, pieces, pieces_two, small, shard, swapped, swapped_two, params, shards,
    own, send, recv, send_two, recv_two, send_small, recv_small, send_row, recv_row, send_shard, recv_shard, send_next, recv_next,
):
    me_seq, me_dp = lax.axis_index("seq"), lax.axis_index("dp")
    greet(seq, dp, me_seq, me_dp)
    keep = pltpu.make_async_copy(small, params.at[me_dp, me_seq], own.at[0])
    keep.start()
    tiny, rows = [], []
    for step in range(1, seq):
        target = lax.rem(me_seq + step, seq)
        tiny.append(
            pltpu.make_async_remote_copy(
                small, params.at[me_dp, me_seq], send_small.at[step], recv_small.at[step], (target, me_dp), MESH
            )
        )
        tiny[-1].start()
    large = start_trade(seq, me_seq, me_dp, pieces, swapped, own.at[1], send, recv)
    span = 1 if dp % 2 else 2
    keep_shard = pltpu.make_async_copy(shard, shards.at[me_dp], own.at[3])
    keep_shard.start()
    firsts = []
    for step in range(1, dp // span):
        target = lax.rem(me_dp + span * step, dp)
        firsts.append(
            pltpu.make_async_remote_copy(
                shard, shards.at[me_dp], send_shard.at[step], recv_shard.at[step], (me_seq, target), MESH
            )
        )
        firsts[-1].start()
    large += start_trade(seq, me_seq, me_dp, pieces_two, swapped_two, own.at[2], send_two, recv_two)
    for copy in [keep] + tiny:
        copy.wait()
    for step in range(1, dp):
        target = lax.rem(me_dp + step, dp)
        rows.append(
            pltpu.make_async_remote_copy(
                params.at[me_dp], params.at[me_dp], send_row.at[step], recv_row.at[step], (me_seq, target), MESH
            )
        )
        rows[-1].start()
    keep_shard.wait()
    for step in range(dp // span):
        if step:
            firsts[step - 1].wait()
        if span == 2:
            origin = lax.rem(me_dp + dp - span * step, dp)
            sibling = me_dp + 1 - 2 * lax.rem(me_dp, 2)
            rows.append(
                pltpu.make_async_remote_copy(
                    shards.at[origin], shards.at[origin], send_next.at[step], recv_next.at[step], (me_seq, sibling), MESH
                )
            )
            rows[-1].start()
    for copy in rows + large:
        copy.wait()


def opening(seq, dp, pieces, pieces_two, small, shard):
    anywhere = pl.BlockSpec(memory_space=pl.ANY)
    return pl.pallas_call(
        functools.partial(opening_kernel, seq, dp),
        out_shape=(
            jax.ShapeDtypeStruct(pieces.shape, pieces.dtype),
            jax.ShapeDtypeStruct(pieces_two.shape, pieces_two.dtype),
            jax.ShapeDtypeStruct((dp, seq) + small.shape, small.dtype),
            jax.ShapeDtypeStruct((dp,) + shard.shape, shard.dtype),
        ),
        in_specs=[anywhere] * 4,
        out_specs=(anywhere,) * 4,
        scratch_shapes=[pltpu.SemaphoreType.DMA((4,))]
        + [pltpu.SemaphoreType.DMA((seq,))] * 6
        + [pltpu.SemaphoreType.DMA((dp,))] * 6,
        compiler_params=pltpu.CompilerParams(collective_id=1, has_side_effects=True),
        name="opening",
    )(pieces, pieces_two, small, shard)


def closing_kernel(
    seq, dp, groups, terms, pieces, total, whole, swapped, over_seq, partial, over_dp,
    own, send, recv, send_seq, recv_seq, send_row, recv_row,
):
    me_seq, me_dp = lax.axis_index("seq"), lax.axis_index("dp")
    greet(seq, dp, me_seq, me_dp)
    copies = []
    for step in range(1, seq):
        target = lax.rem(me_seq + step, seq)
        copies.append(
            pltpu.make_async_remote_copy(
                terms.at[target], over_seq.at[step], send_seq.at[step], recv_seq.at[step], (target, me_dp), MESH
            )
        )
        copies[-1].start()
    large = start_trade(seq, me_seq, me_dp, pieces, swapped, own, send, recv)
    value = terms[me_seq]
    for step, copy in enumerate(copies):
        copy.wait()
        value = value + over_seq[step + 1]
    partial[...] = value
    copies = []
    for step in range(1, dp):
        target = lax.rem(me_dp + step, dp)
        copies.append(
            pltpu.make_async_remote_copy(
                partial.at[target], over_dp.at[step], send_row.at[step], recv_row.at[step], (me_seq, target), MESH
            )
        )
        copies[-1].start()
    value = partial[me_dp]
    for step, copy in enumerate(copies):
        copy.wait()
        value = value + over_dp[step + 1]
    total[...] = value
    for copy in large:
        copy.wait()
    size = whole.shape[1] // (3 * seq * groups)
    for source in range(seq):
        for group in range(groups):
            for third in range(3):
                place = ((third * seq + source) * groups + group) * size
                piece = swapped[source, :, (group * 3 + third) * size : (group * 3 + third + 1) * size]
                whole[:, place : place + size] = piece.astype(F32)


def closing(seq, dp, groups, terms, pieces):
    tile = terms.shape[2:]
    inside, anywhere = pl.BlockSpec(memory_space=pltpu.VMEM), pl.BlockSpec(memory_space=pl.ANY)
    return pl.pallas_call(
        functools.partial(closing_kernel, seq, dp, groups),
        out_shape=(
            jax.ShapeDtypeStruct(tile, F32),
            jax.ShapeDtypeStruct((pieces.shape[1], seq * pieces.shape[2]), F32),
        ),
        in_specs=[inside, anywhere],
        out_specs=(inside, inside),
        scratch_shapes=[
            pltpu.VMEM(pieces.shape, BF),
            pltpu.VMEM(terms.shape, F32),
            pltpu.VMEM(terms.shape[1:], F32),
            pltpu.VMEM(terms.shape[1:], F32),
            pltpu.SemaphoreType.DMA,
        ]
        + [pltpu.SemaphoreType.DMA((seq,))] * 4
        + [pltpu.SemaphoreType.DMA((dp,))] * 2,
        compiler_params=pltpu.CompilerParams(collective_id=2, has_side_effects=True),
        name="closing",
    )(terms, pieces)


def head_parts(ref, where, part, size):
    return [ref[where[place], 0, :, part * size : (part + 1) * size] for place in range(ref.shape[0])]


def diagonal(block):
    return lax.broadcasted_iota(jnp.int32, (block, block), 1) <= lax.broadcasted_iota(jnp.int32, (block, block), 0)


def masked_exp(query, keys, scaling):
    logits = cols_product(query, keys) * scaling
    block, length = logits.shape
    last = jnp.where(diagonal(block), logits[:, length - block :], MASKED)
    logits = last if length == block else jnp.concatenate([logits[:, : length - block], last], axis=1)
    raised = jnp.exp(logits - jnp.max(logits, axis=-1, keepdims=True))
    return raised, jnp.sum(raised, axis=-1, keepdims=True)


def attend_kernel(scaling, where, joint, attended):
    seq, _, block, size = attended.shape
    keys = jnp.concatenate(head_parts(joint, where, 1, size))
    values = jnp.concatenate(head_parts(joint, where, 2, size))
    for place in range(seq):
        length = (place + 1) * block
        query = joint[where[place], 0, :, :size]
        raised, sums = masked_exp(query, keys[:length], scaling)
        weights = (raised * (1.0 / sums)).astype(BF)
        attended[where[place], 0] = product(weights, values[:length]).astype(BF)


def attend(where, joint, size, scaling):
    seq, slots, block, width = joint.shape
    heads = width // (3 * size)
    return pl.pallas_call(
        functools.partial(attend_kernel, scaling),
        out_shape=jax.ShapeDtypeStruct((seq, slots, block, heads * size), BF),
        grid=(slots, heads),
        in_specs=[
            pl.BlockSpec(memory_space=pltpu.SMEM),
            pl.BlockSpec((seq, 1, block, 3 * size), lambda slot, head: (0, slot, 0, head)),
        ],
        out_specs=pl.BlockSpec((seq, 1, block, size), lambda slot, head: (0, slot, 0, head)),
        compiler_params=pltpu.CompilerParams(vmem_limit_bytes=48 << 20),
        cost_estimate=pl.CostEstimate(flops=0, bytes_accessed=slots * (30 << 20), transcendentals=0),
        name="attend",
    )(where, joint)


def partner(me, step, count):
    if count & (count - 1):
        return lax.rem(me + step, count), lax.rem(me + count - step, count)
    bit = 1
    while bit < count:
        if step & bit:
            me = me + bit * (1 - 2 * lax.rem(me // bit, 2))
        bit *= 2
    return me, me


def forward_back_plan(seq):
    if seq == 4:
        order = [(0, 0), (0, 1), (1, 0), (2, 0), (1, 1), (2, 1), (3, 0), (3, 1)]
    else:
        order = [(step, half) for step in range(seq) for half in range(2)]
    at = {pair: spot for spot, pair in enumerate(order)}
    moves = []
    for step, half in order[2:]:
        if seq == 4 and step == 3:
            source = (1, 0) if half == 0 else (2, 1)
            moves.append((at[source], at[step, half], step - source[0], at[source]))
        else:
            moves.append((at[0, half], at[step, half], step, half))
    return order, moves


def returns(seq, plan, me_seq, me_dp, parts, extra, landing, send, recv):
    def copy(source, target, step, spot):
        device = (partner(me_seq, step, seq)[1], me_dp)
        return pltpu.make_async_remote_copy(source, target, send.at[spot], recv.at[spot], device, MESH)

    if seq != 4:
        return {spot: copy(parts(spot), landing.at[spot], step, spot) for spot, (step, _) in enumerate(plan) if step}, []
    at = {pair: spot for spot, pair in enumerate(plan)}
    now = {spot: copy(parts(spot), landing.at[spot], plan[spot][0], spot) for spot in (at[1, 0], at[2, 1])}
    now[at[3, 0]] = copy(parts(at[3, 0]), extra.at[0], 1, at[3, 0])
    now[at[3, 1]] = copy(parts(at[3, 1]), extra.at[1], 2, at[3, 1])
    later = []
    for half, spot in enumerate((at[2, 0], at[1, 1])):
        later.append((spot, at[3, half], copy(parts(spot), landing.at[spot], plan[spot][0], spot)))
    return now, later


def landings(seq):
    return 6 if seq == 4 else 2 * seq


def add_into(ref, spot, other, half, chunk):
    def body(step, carry):
        columns = pl.ds(pl.multiple_of(step * chunk, chunk), chunk)
        ref[spot, :, columns] = (ref[spot, :, columns].astype(F32) + other[half, :, columns].astype(F32)).astype(BF)
        return carry

    lax.fori_loop(0, ref.shape[2] // chunk, body, 0)


def attend_back_kernel(
    scaling, plan, joint, flow, terms, joint_back, terms_all, key_sum, value_sum, extra, held, load, send, recv
):
    seq, _, block, size = flow.shape
    me_seq, me_dp = lax.axis_index("seq"), lax.axis_index("dp")
    here = pl.program_id(0) * pl.num_programs(1) + pl.program_id(1)
    final = pl.num_programs(0) * pl.num_programs(1) - 1
    delayed = {spot: half for half, spot in enumerate([plan.index((2, 0)), plan.index((1, 1))])} if seq == 4 else {}
    now, later = returns(
        seq, plan, me_seq, me_dp, lambda spot: held.at[delayed[spot]] if spot in delayed else terms.at[spot],
        extra, terms_all, send, recv,
    )
    loads = [pltpu.make_async_copy(terms.at[spot], held.at[half], load.at[half]) for spot, half in delayed.items()]

    @pl.when(here == 0)
    def _():
        for copy in loads:
            copy.start()
        greet(seq, 1, me_seq, me_dp)
        for copy in now.values():
            copy.start()

    where = [partner(me_seq, place, seq)[1] for place in range(seq)]
    keys = jnp.concatenate(head_parts(joint, where, 1, size))
    values = jnp.concatenate(head_parts(joint, where, 2, size))
    for place in reversed(range(seq)):
        length = (place + 1) * block
        spot = where[place]
        query = joint[spot, 0, :, :size]
        flow_here = flow[spot, 0]
        raised, sums = masked_exp(query, keys[:length], scaling)
        probs = raised * (1.0 / sums)
        weights = probs.astype(BF)
        prob_back = cols_product(flow_here, values[:length])
        mean_back = jnp.sum(probs * prob_back, axis=-1, keepdims=True)
        logit_back = (probs * (prob_back - mean_back)).astype(BF)
        joint_back[spot, 0, :, :size] = (product(logit_back, keys[:length]) * scaling).astype(BF)
        key_term = rows_product(logit_back, query) * scaling
        value_term = rows_product(weights, flow_here)
        if place == seq - 1:
            key_sum[...] = key_term
            value_sum[...] = value_term
        else:
            key_sum[:length] += key_term
            value_sum[:length] += value_term
    for place in range(seq):
        rows = slice(place * block, (place + 1) * block)
        joint_back[where[place], 0, :, size : 2 * size] = key_sum[rows].astype(BF)
        joint_back[where[place], 0, :, 2 * size :] = value_sum[rows].astype(BF)

    @pl.when(here == final)
    def _():
        for copy in loads:
            copy.wait()
        for half, (spot, corner, copy) in enumerate(later):
            now[corner].wait_recv()
            add_into(held, half, extra, half, 256)
            copy.start()
        for spot, copy in now.items():
            copy.wait_send()
            if spot not in [corner for _, corner, _ in later]:
                copy.wait_recv()
        for _, _, copy in later:
            copy.wait()


def attend_back(plan, joint, flow, terms, size, scaling):
    seq, slots, block, width = joint.shape
    heads = width // (3 * size)
    anywhere = pl.BlockSpec(memory_space=pl.ANY)
    wide = pl.BlockSpec((seq, 1, block, 3 * size), lambda slot, head: (0, slot, 0, head))
    return pl.pallas_call(
        functools.partial(attend_back_kernel, scaling, plan),
        out_shape=[
            jax.ShapeDtypeStruct(joint.shape, BF),
            jax.ShapeDtypeStruct((landings(seq),) + terms.shape[1:], BF),
        ],
        grid=(slots, heads),
        in_specs=[wide, pl.BlockSpec((seq, 1, block, size), lambda slot, head: (0, slot, 0, head)), anywhere],
        out_specs=[wide, anywhere],
        scratch_shapes=[pltpu.VMEM((seq * block, size), F32)] * 2
        + [pltpu.VMEM((2,) + terms.shape[1:], BF)] * 2
        + [pltpu.SemaphoreType.DMA((2,))]
        + [pltpu.SemaphoreType.DMA((terms.shape[0],))] * 2,
        compiler_params=pltpu.CompilerParams(
            collective_id=4, has_side_effects=True, vmem_limit_bytes=48 << 20
        ),
        cost_estimate=pl.CostEstimate(flops=0, bytes_accessed=240 << 20, transcendentals=0),
        name="attend_back",
    )(joint, flow, terms)


def forward_back_kernel(
    seq, chunk, mine, upstream, up, down, normed_all, hidden, expanded_back, result, flow_all,
    normed, flow, extra, load, store, send, recv, send_flow, recv_flow,
):
    model, width = up.shape
    rows = normed.shape[1]
    pull = math.sqrt(2.0 / math.pi)
    me_seq, me_dp = lax.axis_index("seq"), lax.axis_index("dp")
    here = pl.program_id(0)
    order, moves = forward_back_plan(seq)
    steps = len(order)
    copies = {}
    for source, target, step, begin in moves:
        copies[target] = pltpu.make_async_remote_copy(
            normed.at[source], normed.at[target], send.at[target], recv.at[target],
            (partner(me_seq, step, seq)[0], me_dp), MESH,
        )
    backs, later = returns(seq, order, me_seq, me_dp, lambda spot: flow.at[spot], extra, flow_all, send_flow, recv_flow)
    owns = [pltpu.make_async_copy(flow.at[spot], flow_all.at[spot], recv_flow.at[spot]) for spot in range(2)]
    stores = [pltpu.make_async_copy(normed.at[spot], normed_all.at[spot], store.at[spot]) for spot in range(steps)]

    @pl.when(here == 0)
    def _():
        fetches = [
            pltpu.make_async_copy(mine.at[pl.ds(half * rows, rows)], normed.at[half], load.at[half]) for half in range(2)
        ]
        for fetch in fetches:
            fetch.start()
        barrier = pltpu.get_barrier_semaphore()
        for step in range(1, seq):
            pl.semaphore_signal(barrier, inc=1, device_id=(lax.rem(me_seq + step, seq), me_dp), device_id_type=MESH)
        for fetch in fetches:
            fetch.wait()
        pl.semaphore_wait(barrier, seq - 1)

    for spot in range(steps):

        @pl.when(here == spot)
        def _(spot=spot):
            if spot > 1:
                copies[spot].wait_recv()
            for source, target, step, begin in moves:
                if begin == spot:
                    copies[target].start()
            stores[spot].start()

    def inner(step, carry):
        columns = pl.ds(pl.multiple_of(step * chunk, chunk), chunk)
        expanded = product(normed[here], up[:, columns])
        pulled = cols_product(upstream[0], down[columns, :])
        square = expanded * expanded
        bend = jnp.tanh(pull * (expanded + 0.044715 * (square * expanded)))
        half = 0.5 * (1.0 + bend)
        hidden[0, :, columns] = (expanded * half).astype(BF)
        slope = half + (0.5 * pull) * expanded * (1.0 - bend * bend) * (1.0 + 0.134145 * square)
        expanded_back[0, :, columns] = (pulled * slope).astype(BF)
        return carry

    lax.fori_loop(0, width // chunk, inner, 0)

    def outer(step, carry):
        columns = pl.ds(pl.multiple_of(step * chunk, chunk), chunk)
        flow[here, :, columns] = cols_product(expanded_back[0], up[columns, :]).astype(BF)
        return carry

    lax.fori_loop(0, model // chunk, outer, 0)
    for spot in range(steps):

        @pl.when(here == spot)
        def _(spot=spot):
            if spot in backs:
                backs[spot].start()
            elif spot < 2:
                owns[spot].start()

    def last(step, carry):
        columns = pl.ds(pl.multiple_of(step * chunk, chunk), chunk)
        result[0, :, columns] = product(hidden[0], down[:, columns]).astype(BF)
        return carry

    lax.fori_loop(0, model // chunk, last, 0)

    @pl.when(here == steps - 1)
    def _():
        for half, (spot, corner, copy) in enumerate(later):
            backs[corner].wait_recv()
            add_into(flow, spot, extra, half, chunk)
            copy.start()
        for copy in copies.values():
            copy.wait_send()
        for spot, copy in backs.items():
            copy.wait_send()
            if spot not in [corner for _, corner, _ in later]:
                copy.wait_recv()
        for _, _, copy in later:
            copy.wait()
        for copy in stores + owns:
            copy.wait()


def forward_back(mine, upstream, up, down):
    steps, rows, model = upstream.shape
    seq = steps // 2
    width = up.shape[1]
    anywhere = pl.BlockSpec(memory_space=pl.ANY)
    by_step = lambda columns: pl.BlockSpec((1, rows, columns), lambda step: (step, 0, 0))
    whole = lambda shape: pl.BlockSpec(shape, lambda step: (0, 0), pipeline_mode=pl.Buffered(1))
    shape = lambda columns: jax.ShapeDtypeStruct((steps, rows, columns), BF)
    return pl.pallas_call(
        functools.partial(forward_back_kernel, seq, math.gcd(512, math.gcd(width, model))),
        out_shape=[shape(model), shape(width), shape(width), shape(model)]
        + [jax.ShapeDtypeStruct((landings(seq), rows, model), BF)],
        grid=(steps,),
        in_specs=[anywhere, by_step(model), whole(up.shape), whole(down.shape)],
        out_specs=[anywhere, by_step(width), by_step(width), by_step(model), anywhere],
        scratch_shapes=[
            pltpu.VMEM((steps, rows, model), BF),
            pltpu.VMEM((steps, rows, model), BF),
            pltpu.VMEM((2, rows, model), BF),
            pltpu.SemaphoreType.DMA((2,)),
        ]
        + [pltpu.SemaphoreType.DMA((steps,))] * 5,
        compiler_params=pltpu.CompilerParams(
            collective_id=3, has_side_effects=True, vmem_limit_bytes=56 << 20
        ),
        cost_estimate=pl.CostEstimate(
            flops=8 * steps * rows * model * width, bytes_accessed=400 << 20, transcendentals=steps * rows * width
        ),
        name="forward_back",
    )(mine, upstream, up, down)


def send_back_kernel(
    seq, plan, chunk, left, right, pieces, landing, swapped, flow, extra, keep, send, recv, own, send_piece, recv_piece
):
    me_seq, me_dp = lax.axis_index("seq"), lax.axis_index("dp")
    model = right.shape[0]
    now, later = returns(seq, plan, me_seq, me_dp, lambda spot: flow.at[spot], extra, landing, send, recv)
    owns = [pltpu.make_async_copy(flow.at[spot], landing.at[spot], keep.at[spot]) for spot in range(2)]
    greet(seq, 1, me_seq, me_dp)

    def work(spot):
        def body(step, carry):
            columns = pl.ds(pl.multiple_of(step * chunk, chunk), chunk)
            flow[spot, :, columns] = cols_product(left[plan[spot][0] * 2 + plan[spot][1]], right[columns, :]).astype(BF)
            return carry

        lax.fori_loop(0, model // chunk, body, 0)

    corners = [corner for _, corner, _ in later]
    for spot in corners + [spot for spot in now if spot not in corners]:
        work(spot)
        now[spot].start()
    for spot, _, _ in later:
        work(spot)
    for spot in range(2):
        work(spot)
        owns[spot].start()
    for half, (spot, corner, copy) in enumerate(later):
        now[corner].wait_recv()
        add_into(flow, spot, extra, half, chunk)
        copy.start()
    for copy in start_trade(seq, me_seq, me_dp, pieces, swapped, own, send_piece, recv_piece):
        copy.wait()
    for spot, copy in now.items():
        copy.wait_send()
        if spot not in corners:
            copy.wait_recv()
    for _, _, copy in later:
        copy.wait()
    for copy in owns:
        copy.wait()


def send_back(seq, plan, left, right, pieces):
    steps = len(plan)
    model, depth = right.shape
    left = left.reshape(steps, -1, depth)
    rows = left.shape[1]
    inside, anywhere = pl.BlockSpec(memory_space=pltpu.VMEM), pl.BlockSpec(memory_space=pl.ANY)
    return pl.pallas_call(
        functools.partial(send_back_kernel, seq, plan, math.gcd(512, model)),
        out_shape=[
            jax.ShapeDtypeStruct((landings(seq), rows, model), BF),
            jax.ShapeDtypeStruct(pieces.shape, pieces.dtype),
        ],
        in_specs=[inside, inside, anywhere],
        out_specs=[anywhere, anywhere],
        scratch_shapes=[
            pltpu.VMEM((steps, rows, model), BF),
            pltpu.VMEM((2, rows, model), BF),
            pltpu.SemaphoreType.DMA((2,)),
        ]
        + [pltpu.SemaphoreType.DMA((steps,))] * 2
        + [pltpu.SemaphoreType.DMA]
        + [pltpu.SemaphoreType.DMA((seq,))] * 2,
        compiler_params=pltpu.CompilerParams(
            collective_id=5, has_side_effects=True, vmem_limit_bytes=44 << 20
        ),
        cost_estimate=pl.CostEstimate(
            flops=2 * steps * rows * model * depth, bytes_accessed=240 << 20, transcendentals=0
        ),
        name="send_back",
    )(left, right, pieces)


def make_layer(seq, dp):
    xor = seq & (seq - 1) == 0

    def shift(values, step):
        pairs = [(i, i ^ step if xor else (i + step) % seq) for i in range(seq)]
        return lax.ppermute(values, "seq", pairs)

    def gather_seq(block, event=None):
        if seq != 4:
            return [block] + [shift(block, step) for step in range(1, seq)]
        half = block.shape[0] // 2
        near, far = shift(block, 1), shift(block, 2)
        halves = near[:half], far[half:]
        if event is not None:
            halves = after(halves, event)
        return [block, near, far, jnp.concatenate([shift(halves[0], 2), shift(halves[1], 1)])]

    def scatter_seq(make, event=None, begun=None):
        if seq != 4:
            sent = [shift(make(step).astype(BF), step if xor else seq - step).astype(F32) for step in range(1, seq)]
            return make(0) + sum(sent)
        corner = make(3).astype(BF)
        half = corner.shape[0] // 2
        by_near, by_far = shift(corner[:half], 1), shift(corner[half:], 2)
        near = lax.optimization_barrier(make(1).astype(BF))
        far = lax.optimization_barrier(make(2).astype(BF))
        near_first, far_last = shift(near[:half], 1), shift(far[half:], 2)
        if event is not None:
            by_near, by_far = after((by_near, by_far), event)
        if begun is not None:
            begun.extend([by_near, by_far])
        near_last = shift((near[half:].astype(F32) + by_far.astype(F32)).astype(BF), 1)
        far_first = shift((far[:half].astype(F32) + by_near.astype(F32)).astype(BF), 2)
        first = near_first.astype(F32) + far_first.astype(F32)
        last = near_last.astype(F32) + far_last.astype(F32)
        return make(0) + jnp.concatenate([first, last])

    def column_pieces(shard, thirds, groups):
        rows, columns = shard.shape
        shaped = shard.reshape(rows, thirds, seq, groups, -1).transpose(2, 0, 3, 1, 4)
        return shaped.reshape(seq, rows, columns // seq)

    def gather_columns(swapped):
        return lax.all_gather(swapped, "dp", axis=1, tiled=True).reshape(-1, swapped.shape[2])

    def scatter_columns(term):
        total, width = term.shape
        rows = total // (seq * dp)
        summed = lax.psum_scatter(
            term.astype(BF).reshape(seq, dp * rows, width), "dp", scatter_dimension=1, tiled=True
        )
        return summed

    def scatter_rows(term):
        return lax.psum_scatter(term.astype(BF), "dp", scatter_dimension=0, tiled=True).astype(F32)

    def layer(
        inputs, counts, cotangent, stretch, offset, inward, outward, dilation, translation, upward, downward
    ):
        slots, block, model = inputs.shape
        size = model // HEADS
        heads = HEADS // seq
        scaling = 1.0 / math.sqrt(size)
        local_rows = slots * block
        total = seq * local_rows
        live = jnp.repeat((jnp.arange(slots) < counts[0]).astype(F32), block)[:, None]
        residual = inputs.reshape(local_rows, model)
        small = jnp.stack([stretch, offset, dilation, translation]).astype(F32).reshape(-1)
        taken = small.shape[0]
        small = jnp.pad(small, (0, -taken % 1024)).reshape(-1, 128)
        swapped_in, swapped_up, small, matrix_out = opening(
            seq, dp, column_pieces(inward, 3, heads), column_pieces(upward, 1, 1), small, outward
        )
        matrix_out = matrix_out.reshape(-1, model)
        small = small.reshape(dp, seq, -1)[:, :, :taken].reshape(dp, seq, 4, -1).transpose(2, 1, 0, 3).reshape(4, model)
        gain_one, shift_one, gain_two, shift_two = small[0], small[1], small[2], small[3]
        matrix_in = gather_columns(swapped_in)
        blocks = gather_seq(after(residual, swapped_in))
        upstream = (cotangent.astype(F32).reshape(local_rows, model) * live).astype(BF)
        def piece(values, step):
            return values[step * local_rows : (step + 1) * local_rows]

        def norm_one(values):
            return (norm_parts(values.astype(F32))[0] * gain_one + shift_one).astype(BF)

        normed = [norm_one(part) for part in blocks]
        projected = jnp.concatenate([product(part, matrix_in).astype(BF) for part in normed])
        normed = jnp.concatenate(normed)
        upstream_all = gather_seq(after(upstream, blocks[-1]), projected)
        matrix_up = gather_columns(after(swapped_up, (matrix_in, blocks[-1])))
        me = lax.axis_index("seq")
        where = me ^ jnp.arange(seq) if xor else (me + seq - jnp.arange(seq)) % seq
        joint = projected.reshape(seq, slots, block, -1)
        attended = attend(where, joint, size, scaling).reshape(total, heads * size)
        begun = []
        middle = residual.astype(F32) + scatter_seq(lambda step: product(piece(attended, step), matrix_out), None, begun)
        matrix_down = lax.all_gather(after(downward, (matrix_up, begun, upstream_all[1:3])), "dp", axis=0, tiled=True)
        unit_two, root_two = norm_parts(middle)
        mine = (unit_two * gain_two + shift_two).astype(BF)
        half = local_rows // 2
        plan = forward_back_plan(seq)[0]
        upstream_all = jnp.stack([upstream_all[step][part * half : (part + 1) * half] for step, part in plan])
        normed_two, hidden, expanded_back, down_terms, two_terms = forward_back(mine, upstream_all, matrix_up, matrix_down)

        def flat(values):
            return values.reshape(-1, values.shape[-1])

        down_sum = rows_product(flat(hidden), flat(upstream_all))
        spots = [[spot for spot, (_, part) in enumerate(plan) if part == which and spot < landings(seq)] for which in range(2)]

        def over_plan(values):
            return jnp.concatenate([sum(values[spot].astype(F32) for spot in places) for places in spots])

        two_back = over_plan(two_terms)
        downward_delta = scatter_rows(down_sum)
        middle_flow, dilation_term, translation_term = norm_back(two_back, unit_two, root_two, gain_two)
        middle_back = upstream.astype(F32) + middle_flow
        up_sum = rows_product(after(flat(normed_two), down_sum), flat(expanded_back))
        middle_low = gather_seq(after(middle_back.astype(BF), up_sum))
        heads_back = jnp.concatenate([cols_product(part, matrix_out).astype(BF) for part in middle_low])
        out_sum = rows_product(attended, jnp.concatenate(middle_low))
        heads_back = after(heads_back, (downward_delta, up_sum)).reshape(seq, slots, block, -1)
        summed_up = scatter_columns(after(up_sum, heads_back))
        projected_back, result_terms = attend_back(plan, joint, heads_back, down_terms, size, scaling)
        projected_back = projected_back.reshape(total, -1)
        result = middle + over_plan([down_terms[0], down_terms[1]] + [result_terms[spot] for spot in range(2, landings(seq))])
        outputs = (result * live).astype(BF).reshape(slots, block, model)
        in_sum = rows_product(after(normed, outputs), projected_back)
        summed_in = scatter_columns(in_sum)
        one_terms, swapped_up = send_back(seq, plan, after(projected_back, in_sum), matrix_in, summed_up)
        upward_delta = jnp.concatenate([swapped_up[step] for step in range(seq)], axis=1).astype(F32)
        one_back = over_plan(one_terms)
        outward_delta = scatter_rows(after(out_sum, (summed_in, one_terms)))
        unit_one, root_one = norm_parts(residual.astype(F32))
        input_flow, stretch_term, offset_term = norm_back(one_back, unit_one, root_one, gain_one)
        terms = jnp.stack([stretch_term, offset_term, dilation_term, translation_term])
        terms = terms.reshape(4, seq, dp, -1).transpose(1, 2, 0, 3).reshape(seq, dp, -1)
        terms = jnp.pad(terms, ((0, 0), (0, 0), (0, -taken % 1024))).reshape(seq, dp, -1, 128)
        deltas, inward_delta = closing(seq, dp, heads, terms, summed_in)
        deltas = deltas.reshape(-1)[:taken].reshape(4, -1)
        input_delta = (middle_back + input_flow).reshape(slots, block, model)
        return (
            outputs,
            input_delta,
            deltas[0],
            deltas[1],
            inward_delta,
            outward_delta,
            deltas[2],
            deltas[3],
            upward_delta,
            downward_delta,
        )

    return layer


def solution(mesh):
    tokens, vector, matrix = P("dp", "seq", None), P(("seq", "dp")), P(("seq", "dp"), None)
    return jax.shard_map(
        make_layer(mesh.shape["seq"], mesh.shape["dp"]),
        mesh=mesh,
        in_specs=(tokens, P("dp"), tokens, vector, vector, matrix, matrix, vector, vector, matrix, matrix),
        out_specs=(tokens, tokens, vector, vector, matrix, matrix, vector, vector, matrix, matrix),
        check_vma=False,
    )
```

```python
import functools
import math

import jax
import jax.numpy as jnp
from jax import lax
from jax.experimental import pallas as pl
from jax.experimental.pallas import tpu as pltpu
from jax.sharding import PartitionSpec as P

HEADS = 16
EPSILON = 1e-05
MASKED = -1e30
BF = jnp.bfloat16
F32 = jnp.float32
MESH = pl.DeviceIdType.MESH


def norm_parts(values):
    average = jnp.mean(values, axis=-1, keepdims=True)
    centered = values - average
    root = lax.rsqrt(jnp.mean(centered * centered, axis=-1, keepdims=True) + EPSILON)
    return centered * root, root


def norm_back(flow, unit, root, gain):
    scaled = flow * gain
    first = jnp.mean(scaled, axis=-1, keepdims=True)
    second = jnp.mean(scaled * unit, axis=-1, keepdims=True)
    return root * (scaled - first - unit * second), jnp.sum(flow * unit, axis=0), jnp.sum(flow, axis=0)


def rows_product(left, right):
    return lax.dot_general(left, right, (((0,), (0,)), ((), ())), preferred_element_type=F32)


def cols_product(left, right):
    return lax.dot_general(left, right, (((1,), (1,)), ((), ())), preferred_element_type=F32)


def product(left, right):
    return jnp.dot(left, right, preferred_element_type=F32)


def after(values, event):
    return lax.optimization_barrier((values, event))[0]


def greet(seq, dp, me_seq, me_dp):
    barrier = pltpu.get_barrier_semaphore()
    for step in range(1, seq):
        pl.semaphore_signal(barrier, inc=1, device_id=(lax.rem(me_seq + step, seq), me_dp), device_id_type=MESH)
    for step in range(1, dp):
        pl.semaphore_signal(barrier, inc=1, device_id=(me_seq, lax.rem(me_dp + step, dp)), device_id_type=MESH)
    pl.semaphore_wait(barrier, seq + dp - 2)


def start_trade(seq, me_seq, me_dp, pieces, swapped, own, send, recv):
    copies = [pltpu.make_async_copy(pieces.at[me_seq], swapped.at[me_seq], own)]
    copies[0].start()
    for step in range(1, seq):
        target = lax.rem(me_seq + step, seq)
        copies.append(
            pltpu.make_async_remote_copy(
                pieces.at[target], swapped.at[me_seq], send.at[step], recv.at[step], (target, me_dp), MESH
            )
        )
        copies[-1].start()
    return copies


def opening_kernel(
    seq, dp, pieces, pieces_two, small, shard, swapped, swapped_two, params, shards,
    own, send, recv, send_two, recv_two, send_small, recv_small, send_row, recv_row, send_shard, recv_shard, send_next, recv_next,
):
    me_seq, me_dp = lax.axis_index("seq"), lax.axis_index("dp")
    greet(seq, dp, me_seq, me_dp)
    keep = pltpu.make_async_copy(small, params.at[me_dp, me_seq], own.at[0])
    keep.start()
    tiny, rows = [], []
    for step in range(1, seq):
        target = lax.rem(me_seq + step, seq)
        tiny.append(
            pltpu.make_async_remote_copy(
                small, params.at[me_dp, me_seq], send_small.at[step], recv_small.at[step], (target, me_dp), MESH
            )
        )
        tiny[-1].start()
    large = start_trade(seq, me_seq, me_dp, pieces, swapped, own.at[1], send, recv)
    span = 1 if dp % 2 else 2
    keep_shard = pltpu.make_async_copy(shard, shards.at[me_dp], own.at[3])
    keep_shard.start()
    firsts = []
    for step in range(1, dp // span):
        target = lax.rem(me_dp + span * step, dp)
        firsts.append(
            pltpu.make_async_remote_copy(
                shard, shards.at[me_dp], send_shard.at[step], recv_shard.at[step], (me_seq, target), MESH
            )
        )
        firsts[-1].start()
    large += start_trade(seq, me_seq, me_dp, pieces_two, swapped_two, own.at[2], send_two, recv_two)
    for copy in [keep] + tiny:
        copy.wait()
    for step in range(1, dp):
        target = lax.rem(me_dp + step, dp)
        rows.append(
            pltpu.make_async_remote_copy(
                params.at[me_dp], params.at[me_dp], send_row.at[step], recv_row.at[step], (me_seq, target), MESH
            )
        )
        rows[-1].start()
    keep_shard.wait()
    for step in range(dp // span):
        if step:
            firsts[step - 1].wait()
        if span == 2:
            origin = lax.rem(me_dp + dp - span * step, dp)
            sibling = me_dp + 1 - 2 * lax.rem(me_dp, 2)
            rows.append(
                pltpu.make_async_remote_copy(
                    shards.at[origin], shards.at[origin], send_next.at[step], recv_next.at[step], (me_seq, sibling), MESH
                )
            )
            rows[-1].start()
    for copy in rows + large:
        copy.wait()


def opening(seq, dp, pieces, pieces_two, small, shard):
    anywhere = pl.BlockSpec(memory_space=pl.ANY)
    return pl.pallas_call(
        functools.partial(opening_kernel, seq, dp),
        out_shape=(
            jax.ShapeDtypeStruct(pieces.shape, pieces.dtype),
            jax.ShapeDtypeStruct(pieces_two.shape, pieces_two.dtype),
            jax.ShapeDtypeStruct((dp, seq) + small.shape, small.dtype),
            jax.ShapeDtypeStruct((dp,) + shard.shape, shard.dtype),
        ),
        in_specs=[anywhere] * 4,
        out_specs=(anywhere,) * 4,
        scratch_shapes=[pltpu.SemaphoreType.DMA((4,))]
        + [pltpu.SemaphoreType.DMA((seq,))] * 6
        + [pltpu.SemaphoreType.DMA((dp,))] * 6,
        compiler_params=pltpu.CompilerParams(collective_id=1, has_side_effects=True),
        name="opening",
    )(pieces, pieces_two, small, shard)


def closing_kernel(
    seq, dp, groups, terms, pieces, total, whole, swapped, over_seq, partial, over_dp,
    own, send, recv, send_seq, recv_seq, send_row, recv_row,
):
    me_seq, me_dp = lax.axis_index("seq"), lax.axis_index("dp")
    greet(seq, dp, me_seq, me_dp)
    copies = []
    for step in range(1, seq):
        target = lax.rem(me_seq + step, seq)
        copies.append(
            pltpu.make_async_remote_copy(
                terms.at[target], over_seq.at[step], send_seq.at[step], recv_seq.at[step], (target, me_dp), MESH
            )
        )
        copies[-1].start()
    large = start_trade(seq, me_seq, me_dp, pieces, swapped, own, send, recv)
    value = terms[me_seq]
    for step, copy in enumerate(copies):
        copy.wait()
        value = value + over_seq[step + 1]
    partial[...] = value
    copies = []
    for step in range(1, dp):
        target = lax.rem(me_dp + step, dp)
        copies.append(
            pltpu.make_async_remote_copy(
                partial.at[target], over_dp.at[step], send_row.at[step], recv_row.at[step], (me_seq, target), MESH
            )
        )
        copies[-1].start()
    value = partial[me_dp]
    for step, copy in enumerate(copies):
        copy.wait()
        value = value + over_dp[step + 1]
    total[...] = value
    for copy in large:
        copy.wait()
    size = whole.shape[1] // (3 * seq * groups)
    for source in range(seq):
        for group in range(groups):
            for third in range(3):
                place = ((third * seq + source) * groups + group) * size
                piece = swapped[source, :, (group * 3 + third) * size : (group * 3 + third + 1) * size]
                whole[:, place : place + size] = piece.astype(F32)


def closing(seq, dp, groups, terms, pieces):
    tile = terms.shape[2:]
    inside, anywhere = pl.BlockSpec(memory_space=pltpu.VMEM), pl.BlockSpec(memory_space=pl.ANY)
    return pl.pallas_call(
        functools.partial(closing_kernel, seq, dp, groups),
        out_shape=(
            jax.ShapeDtypeStruct(tile, F32),
            jax.ShapeDtypeStruct((pieces.shape[1], seq * pieces.shape[2]), F32),
        ),
        in_specs=[inside, anywhere],
        out_specs=(inside, inside),
        scratch_shapes=[
            pltpu.VMEM(pieces.shape, BF),
            pltpu.VMEM(terms.shape, F32),
            pltpu.VMEM(terms.shape[1:], F32),
            pltpu.VMEM(terms.shape[1:], F32),
            pltpu.SemaphoreType.DMA,
        ]
        + [pltpu.SemaphoreType.DMA((seq,))] * 4
        + [pltpu.SemaphoreType.DMA((dp,))] * 2,
        compiler_params=pltpu.CompilerParams(collective_id=2, has_side_effects=True),
        name="closing",
    )(terms, pieces)


def head_parts(ref, where, part, size):
    return [ref[where[place], 0, :, part * size : (part + 1) * size] for place in range(ref.shape[0])]


def diagonal(block):
    return lax.broadcasted_iota(jnp.int32, (block, block), 1) <= lax.broadcasted_iota(jnp.int32, (block, block), 0)


def masked_exp(query, keys, scaling):
    logits = cols_product(query, keys) * scaling
    block, length = logits.shape
    last = jnp.where(diagonal(block), logits[:, length - block :], MASKED)
    logits = last if length == block else jnp.concatenate([logits[:, : length - block], last], axis=1)
    raised = jnp.exp(logits - jnp.max(logits, axis=-1, keepdims=True))
    return raised, jnp.sum(raised, axis=-1, keepdims=True)


def attend_kernel(scaling, where, joint, attended):
    seq, _, block, size = attended.shape
    keys = jnp.concatenate(head_parts(joint, where, 1, size))
    values = jnp.concatenate(head_parts(joint, where, 2, size))
    for place in range(seq):
        length = (place + 1) * block
        query = joint[where[place], 0, :, :size]
        raised, sums = masked_exp(query, keys[:length], scaling)
        weights = (raised * (1.0 / sums)).astype(BF)
        attended[where[place], 0] = product(weights, values[:length]).astype(BF)


def attend(where, joint, size, scaling):
    seq, slots, block, width = joint.shape
    heads = width // (3 * size)
    return pl.pallas_call(
        functools.partial(attend_kernel, scaling),
        out_shape=jax.ShapeDtypeStruct((seq, slots, block, heads * size), BF),
        grid=(slots, heads),
        in_specs=[
            pl.BlockSpec(memory_space=pltpu.SMEM),
            pl.BlockSpec((seq, 1, block, 3 * size), lambda slot, head: (0, slot, 0, head)),
        ],
        out_specs=pl.BlockSpec((seq, 1, block, size), lambda slot, head: (0, slot, 0, head)),
        compiler_params=pltpu.CompilerParams(vmem_limit_bytes=48 << 20),
        cost_estimate=pl.CostEstimate(flops=0, bytes_accessed=slots * (30 << 20), transcendentals=0),
        name="attend",
    )(where, joint)


def partner(me, step, count):
    if count & (count - 1):
        return lax.rem(me + step, count), lax.rem(me + count - step, count)
    bit = 1
    while bit < count:
        if step & bit:
            me = me + bit * (1 - 2 * lax.rem(me // bit, 2))
        bit *= 2
    return me, me


def forward_back_plan(seq):
    if seq == 4:
        order = [(0, 0), (0, 1), (1, 0), (2, 0), (1, 1), (2, 1), (3, 0), (3, 1)]
    else:
        order = [(step, half) for step in range(seq) for half in range(2)]
    at = {pair: spot for spot, pair in enumerate(order)}
    moves = []
    for step, half in order[2:]:
        if seq == 4 and step == 3:
            source = (1, 0) if half == 0 else (2, 1)
            moves.append((at[source], at[step, half], step - source[0], at[source]))
        else:
            moves.append((at[0, half], at[step, half], step, half))
    return order, moves


def returns(seq, plan, me_seq, me_dp, parts, extra, landing, send, recv):
    def copy(source, target, step, spot):
        device = (partner(me_seq, step, seq)[1], me_dp)
        return pltpu.make_async_remote_copy(source, target, send.at[spot], recv.at[spot], device, MESH)

    if seq != 4:
        return {spot: copy(parts(spot), landing.at[spot], step, spot) for spot, (step, _) in enumerate(plan) if step}, []
    at = {pair: spot for spot, pair in enumerate(plan)}
    now = {spot: copy(parts(spot), landing.at[spot], plan[spot][0], spot) for spot in (at[1, 0], at[2, 1])}
    now[at[3, 0]] = copy(parts(at[3, 0]), extra.at[0], 1, at[3, 0])
    now[at[3, 1]] = copy(parts(at[3, 1]), extra.at[1], 2, at[3, 1])
    later = []
    for half, spot in enumerate((at[2, 0], at[1, 1])):
        later.append((spot, at[3, half], copy(parts(spot), landing.at[spot], plan[spot][0], spot)))
    return now, later


def landings(seq):
    return 6 if seq == 4 else 2 * seq


def add_into(ref, spot, other, half, chunk):
    def body(step, carry):
        columns = pl.ds(pl.multiple_of(step * chunk, chunk), chunk)
        ref[spot, :, columns] = (ref[spot, :, columns].astype(F32) + other[half, :, columns].astype(F32)).astype(BF)
        return carry

    lax.fori_loop(0, ref.shape[2] // chunk, body, 0)


def attend_back_kernel(
    scaling, plan, joint, flow, terms, joint_back, terms_all, key_sum, value_sum, extra, held, load, send, recv
):
    seq, _, block, size = flow.shape
    me_seq, me_dp = lax.axis_index("seq"), lax.axis_index("dp")
    here = pl.program_id(0) * pl.num_programs(1) + pl.program_id(1)
    final = pl.num_programs(0) * pl.num_programs(1) - 1
    delayed = {spot: half for half, spot in enumerate([plan.index((2, 0)), plan.index((1, 1))])} if seq == 4 else {}
    now, later = returns(
        seq, plan, me_seq, me_dp, lambda spot: held.at[delayed[spot]] if spot in delayed else terms.at[spot],
        extra, terms_all, send, recv,
    )
    loads = [pltpu.make_async_copy(terms.at[spot], held.at[half], load.at[half]) for spot, half in delayed.items()]

    @pl.when(here == 0)
    def _():
        for copy in loads:
            copy.start()
        greet(seq, 1, me_seq, me_dp)
        for copy in now.values():
            copy.start()

    where = [partner(me_seq, place, seq)[1] for place in range(seq)]
    keys = jnp.concatenate(head_parts(joint, where, 1, size))
    values = jnp.concatenate(head_parts(joint, where, 2, size))
    for place in reversed(range(seq)):
        length = (place + 1) * block
        spot = where[place]
        query = joint[spot, 0, :, :size]
        flow_here = flow[spot, 0]
        raised, sums = masked_exp(query, keys[:length], scaling)
        probs = raised * (1.0 / sums)
        weights = probs.astype(BF)
        prob_back = cols_product(flow_here, values[:length])
        mean_back = jnp.sum(probs * prob_back, axis=-1, keepdims=True)
        logit_back = (probs * (prob_back - mean_back)).astype(BF)
        joint_back[spot, 0, :, :size] = (product(logit_back, keys[:length]) * scaling).astype(BF)
        key_term = rows_product(logit_back, query) * scaling
        value_term = rows_product(weights, flow_here)
        if place == seq - 1:
            key_sum[...] = key_term
            value_sum[...] = value_term
        else:
            key_sum[:length] += key_term
            value_sum[:length] += value_term
    for place in range(seq):
        rows = slice(place * block, (place + 1) * block)
        joint_back[where[place], 0, :, size : 2 * size] = key_sum[rows].astype(BF)
        joint_back[where[place], 0, :, 2 * size :] = value_sum[rows].astype(BF)

    @pl.when(here == final)
    def _():
        for copy in loads:
            copy.wait()
        for half, (spot, corner, copy) in enumerate(later):
            now[corner].wait_recv()
            add_into(held, half, extra, half, 256)
            copy.start()
        for spot, copy in now.items():
            copy.wait_send()
            if spot not in [corner for _, corner, _ in later]:
                copy.wait_recv()
        for _, _, copy in later:
            copy.wait()


def attend_back(plan, joint, flow, terms, size, scaling):
    seq, slots, block, width = joint.shape
    heads = width // (3 * size)
    anywhere = pl.BlockSpec(memory_space=pl.ANY)
    wide = pl.BlockSpec((seq, 1, block, 3 * size), lambda slot, head: (0, slot, 0, head))
    return pl.pallas_call(
        functools.partial(attend_back_kernel, scaling, plan),
        out_shape=[
            jax.ShapeDtypeStruct(joint.shape, BF),
            jax.ShapeDtypeStruct((landings(seq),) + terms.shape[1:], BF),
        ],
        grid=(slots, heads),
        in_specs=[wide, pl.BlockSpec((seq, 1, block, size), lambda slot, head: (0, slot, 0, head)), anywhere],
        out_specs=[wide, anywhere],
        scratch_shapes=[pltpu.VMEM((seq * block, size), F32)] * 2
        + [pltpu.VMEM((2,) + terms.shape[1:], BF)] * 2
        + [pltpu.SemaphoreType.DMA((2,))]
        + [pltpu.SemaphoreType.DMA((terms.shape[0],))] * 2,
        compiler_params=pltpu.CompilerParams(
            collective_id=4, has_side_effects=True, vmem_limit_bytes=48 << 20
        ),
        cost_estimate=pl.CostEstimate(flops=0, bytes_accessed=240 << 20, transcendentals=0),
        name="attend_back",
    )(joint, flow, terms)


def forward_back_kernel(
    seq, chunk, mine, upstream, up, down, normed_all, hidden, expanded_back, result, flow_all,
    normed, flow, extra, load, store, send, recv, send_flow, recv_flow,
):
    model, width = up.shape
    rows = normed.shape[1]
    pull = math.sqrt(2.0 / math.pi)
    me_seq, me_dp = lax.axis_index("seq"), lax.axis_index("dp")
    here = pl.program_id(0)
    order, moves = forward_back_plan(seq)
    steps = len(order)
    copies = {}
    for source, target, step, begin in moves:
        copies[target] = pltpu.make_async_remote_copy(
            normed.at[source], normed.at[target], send.at[target], recv.at[target],
            (partner(me_seq, step, seq)[0], me_dp), MESH,
        )
    backs, later = returns(seq, order, me_seq, me_dp, lambda spot: flow.at[spot], extra, flow_all, send_flow, recv_flow)
    owns = [pltpu.make_async_copy(flow.at[spot], flow_all.at[spot], recv_flow.at[spot]) for spot in range(2)]
    stores = [pltpu.make_async_copy(normed.at[spot], normed_all.at[spot], store.at[spot]) for spot in range(steps)]

    @pl.when(here == 0)
    def _():
        fetches = [
            pltpu.make_async_copy(mine.at[pl.ds(half * rows, rows)], normed.at[half], load.at[half]) for half in range(2)
        ]
        for fetch in fetches:
            fetch.start()
        barrier = pltpu.get_barrier_semaphore()
        for step in range(1, seq):
            pl.semaphore_signal(barrier, inc=1, device_id=(lax.rem(me_seq + step, seq), me_dp), device_id_type=MESH)
        for fetch in fetches:
            fetch.wait()
        pl.semaphore_wait(barrier, seq - 1)

    for spot in range(steps):

        @pl.when(here == spot)
        def _(spot=spot):
            if spot > 1:
                copies[spot].wait_recv()
            for source, target, step, begin in moves:
                if begin == spot:
                    copies[target].start()
            stores[spot].start()

    def inner(step, carry):
        columns = pl.ds(pl.multiple_of(step * chunk, chunk), chunk)
        expanded = product(normed[here], up[:, columns])
        pulled = cols_product(upstream[0], down[columns, :])
        square = expanded * expanded
        bend = jnp.tanh(pull * (expanded + 0.044715 * (square * expanded)))
        half = 0.5 * (1.0 + bend)
        hidden[0, :, columns] = (expanded * half).astype(BF)
        slope = half + (0.5 * pull) * expanded * (1.0 - bend * bend) * (1.0 + 0.134145 * square)
        expanded_back[0, :, columns] = (pulled * slope).astype(BF)
        return carry

    lax.fori_loop(0, width // chunk, inner, 0)

    def outer(step, carry):
        columns = pl.ds(pl.multiple_of(step * chunk, chunk), chunk)
        flow[here, :, columns] = cols_product(expanded_back[0], up[columns, :]).astype(BF)
        return carry

    lax.fori_loop(0, model // chunk, outer, 0)
    for spot in range(steps):

        @pl.when(here == spot)
        def _(spot=spot):
            if spot in backs:
                backs[spot].start()
            elif spot < 2:
                owns[spot].start()

    def last(step, carry):
        columns = pl.ds(pl.multiple_of(step * chunk, chunk), chunk)
        result[0, :, columns] = product(hidden[0], down[:, columns]).astype(BF)
        return carry

    lax.fori_loop(0, model // chunk, last, 0)

    @pl.when(here == steps - 1)
    def _():
        for half, (spot, corner, copy) in enumerate(later):
            backs[corner].wait_recv()
            add_into(flow, spot, extra, half, chunk)
            copy.start()
        for copy in copies.values():
            copy.wait_send()
        for spot, copy in backs.items():
            copy.wait_send()
            if spot not in [corner for _, corner, _ in later]:
                copy.wait_recv()
        for _, _, copy in later:
            copy.wait()
        for copy in stores + owns:
            copy.wait()


def forward_back(mine, upstream, up, down):
    steps, rows, model = upstream.shape
    seq = steps // 2
    width = up.shape[1]
    anywhere = pl.BlockSpec(memory_space=pl.ANY)
    by_step = lambda columns: pl.BlockSpec((1, rows, columns), lambda step: (step, 0, 0))
    whole = lambda shape: pl.BlockSpec(shape, lambda step: (0, 0), pipeline_mode=pl.Buffered(1))
    shape = lambda columns: jax.ShapeDtypeStruct((steps, rows, columns), BF)
    return pl.pallas_call(
        functools.partial(forward_back_kernel, seq, math.gcd(1024, math.gcd(width, model))),
        out_shape=[shape(model), shape(width), shape(width), shape(model)]
        + [jax.ShapeDtypeStruct((landings(seq), rows, model), BF)],
        grid=(steps,),
        in_specs=[anywhere, by_step(model), whole(up.shape), whole(down.shape)],
        out_specs=[anywhere, by_step(width), by_step(width), by_step(model), anywhere],
        scratch_shapes=[
            pltpu.VMEM((steps, rows, model), BF),
            pltpu.VMEM((steps, rows, model), BF),
            pltpu.VMEM((2, rows, model), BF),
            pltpu.SemaphoreType.DMA((2,)),
        ]
        + [pltpu.SemaphoreType.DMA((steps,))] * 5,
        compiler_params=pltpu.CompilerParams(
            collective_id=3, has_side_effects=True, vmem_limit_bytes=56 << 20
        ),
        cost_estimate=pl.CostEstimate(
            flops=8 * steps * rows * model * width, bytes_accessed=400 << 20, transcendentals=steps * rows * width
        ),
        name="forward_back",
    )(mine, upstream, up, down)


def send_back_kernel(
    seq, plan, chunk, left, right, pieces, landing, swapped, flow, extra, keep, send, recv, own, send_piece, recv_piece
):
    me_seq, me_dp = lax.axis_index("seq"), lax.axis_index("dp")
    model = right.shape[0]
    now, later = returns(seq, plan, me_seq, me_dp, lambda spot: flow.at[spot], extra, landing, send, recv)
    owns = [pltpu.make_async_copy(flow.at[spot], landing.at[spot], keep.at[spot]) for spot in range(2)]
    greet(seq, 1, me_seq, me_dp)

    def work(spot):
        def body(step, carry):
            columns = pl.ds(pl.multiple_of(step * chunk, chunk), chunk)
            flow[spot, :, columns] = cols_product(left[plan[spot][0] * 2 + plan[spot][1]], right[columns, :]).astype(BF)
            return carry

        lax.fori_loop(0, model // chunk, body, 0)

    corners = [corner for _, corner, _ in later]
    for spot in corners + [spot for spot in now if spot not in corners]:
        work(spot)
        now[spot].start()
    for spot, _, _ in later:
        work(spot)
    for spot in range(2):
        work(spot)
        owns[spot].start()
    for half, (spot, corner, copy) in enumerate(later):
        now[corner].wait_recv()
        add_into(flow, spot, extra, half, chunk)
        copy.start()
    for copy in start_trade(seq, me_seq, me_dp, pieces, swapped, own, send_piece, recv_piece):
        copy.wait()
    for spot, copy in now.items():
        copy.wait_send()
        if spot not in corners:
            copy.wait_recv()
    for _, _, copy in later:
        copy.wait()
    for copy in owns:
        copy.wait()


def send_back(seq, plan, left, right, pieces):
    steps = len(plan)
    model, depth = right.shape
    left = left.reshape(steps, -1, depth)
    rows = left.shape[1]
    inside, anywhere = pl.BlockSpec(memory_space=pltpu.VMEM), pl.BlockSpec(memory_space=pl.ANY)
    return pl.pallas_call(
        functools.partial(send_back_kernel, seq, plan, math.gcd(512, model)),
        out_shape=[
            jax.ShapeDtypeStruct((landings(seq), rows, model), BF),
            jax.ShapeDtypeStruct(pieces.shape, pieces.dtype),
        ],
        in_specs=[inside, inside, anywhere],
        out_specs=[anywhere, anywhere],
        scratch_shapes=[
            pltpu.VMEM((steps, rows, model), BF),
            pltpu.VMEM((2, rows, model), BF),
            pltpu.SemaphoreType.DMA((2,)),
        ]
        + [pltpu.SemaphoreType.DMA((steps,))] * 2
        + [pltpu.SemaphoreType.DMA]
        + [pltpu.SemaphoreType.DMA((seq,))] * 2,
        compiler_params=pltpu.CompilerParams(
            collective_id=5, has_side_effects=True, vmem_limit_bytes=44 << 20
        ),
        cost_estimate=pl.CostEstimate(
            flops=2 * steps * rows * model * depth, bytes_accessed=240 << 20, transcendentals=0
        ),
        name="send_back",
    )(left, right, pieces)


def make_layer(seq, dp):
    xor = seq & (seq - 1) == 0

    def shift(values, step):
        pairs = [(i, i ^ step if xor else (i + step) % seq) for i in range(seq)]
        return lax.ppermute(values, "seq", pairs)

    def gather_seq(block, event=None):
        if seq != 4:
            return [block] + [shift(block, step) for step in range(1, seq)]
        half = block.shape[0] // 2
        near, far = shift(block, 1), shift(block, 2)
        halves = near[:half], far[half:]
        if event is not None:
            halves = after(halves, event)
        return [block, near, far, jnp.concatenate([shift(halves[0], 2), shift(halves[1], 1)])]

    def scatter_seq(make, event=None, begun=None):
        if seq != 4:
            sent = [shift(make(step).astype(BF), step if xor else seq - step).astype(F32) for step in range(1, seq)]
            return make(0) + sum(sent)
        corner = make(3).astype(BF)
        half = corner.shape[0] // 2
        by_near, by_far = shift(corner[:half], 1), shift(corner[half:], 2)
        near = lax.optimization_barrier(make(1).astype(BF))
        far = lax.optimization_barrier(make(2).astype(BF))
        near_first, far_last = shift(near[:half], 1), shift(far[half:], 2)
        if event is not None:
            by_near, by_far = after((by_near, by_far), event)
        if begun is not None:
            begun.extend([by_near, by_far])
        near_last = shift((near[half:].astype(F32) + by_far.astype(F32)).astype(BF), 1)
        far_first = shift((far[:half].astype(F32) + by_near.astype(F32)).astype(BF), 2)
        first = near_first.astype(F32) + far_first.astype(F32)
        last = near_last.astype(F32) + far_last.astype(F32)
        return make(0) + jnp.concatenate([first, last])

    def column_pieces(shard, thirds, groups):
        rows, columns = shard.shape
        shaped = shard.reshape(rows, thirds, seq, groups, -1).transpose(2, 0, 3, 1, 4)
        return shaped.reshape(seq, rows, columns // seq)

    def gather_columns(swapped):
        return lax.all_gather(swapped, "dp", axis=1, tiled=True).reshape(-1, swapped.shape[2])

    def scatter_columns(term):
        total, width = term.shape
        rows = total // (seq * dp)
        summed = lax.psum_scatter(
            term.astype(BF).reshape(seq, dp * rows, width), "dp", scatter_dimension=1, tiled=True
        )
        return summed

    def scatter_rows(term):
        return lax.psum_scatter(term.astype(BF), "dp", scatter_dimension=0, tiled=True).astype(F32)

    def layer(
        inputs, counts, cotangent, stretch, offset, inward, outward, dilation, translation, upward, downward
    ):
        slots, block, model = inputs.shape
        size = model // HEADS
        heads = HEADS // seq
        scaling = 1.0 / math.sqrt(size)
        local_rows = slots * block
        total = seq * local_rows
        live = jnp.repeat((jnp.arange(slots) < counts[0]).astype(F32), block)[:, None]
        residual = inputs.reshape(local_rows, model)
        small = jnp.stack([stretch, offset, dilation, translation]).astype(F32).reshape(-1)
        taken = small.shape[0]
        small = jnp.pad(small, (0, -taken % 1024)).reshape(-1, 128)
        swapped_in, swapped_up, small, matrix_out = opening(
            seq, dp, column_pieces(inward, 3, heads), column_pieces(upward, 1, 1), small, outward
        )
        matrix_out = matrix_out.reshape(-1, model)
        small = small.reshape(dp, seq, -1)[:, :, :taken].reshape(dp, seq, 4, -1).transpose(2, 1, 0, 3).reshape(4, model)
        gain_one, shift_one, gain_two, shift_two = small[0], small[1], small[2], small[3]
        matrix_in = gather_columns(swapped_in)
        blocks = gather_seq(after(residual, swapped_in))
        upstream = (cotangent.astype(F32).reshape(local_rows, model) * live).astype(BF)
        def piece(values, step):
            return values[step * local_rows : (step + 1) * local_rows]

        def norm_one(values):
            return (norm_parts(values.astype(F32))[0] * gain_one + shift_one).astype(BF)

        normed = [norm_one(part) for part in blocks]
        projected = jnp.concatenate([product(part, matrix_in).astype(BF) for part in normed])
        normed = jnp.concatenate(normed)
        upstream_all = gather_seq(after(upstream, blocks[-1]), projected)
        matrix_up = gather_columns(after(swapped_up, (matrix_in, blocks[-1])))
        me = lax.axis_index("seq")
        where = me ^ jnp.arange(seq) if xor else (me + seq - jnp.arange(seq)) % seq
        joint = projected.reshape(seq, slots, block, -1)
        attended = attend(where, joint, size, scaling).reshape(total, heads * size)
        begun = []
        middle = residual.astype(F32) + scatter_seq(lambda step: product(piece(attended, step), matrix_out), None, begun)
        matrix_down = lax.all_gather(after(downward, (matrix_up, begun, upstream_all[1:3])), "dp", axis=0, tiled=True)
        unit_two, root_two = norm_parts(middle)
        mine = (unit_two * gain_two + shift_two).astype(BF)
        half = local_rows // 2
        plan = forward_back_plan(seq)[0]
        upstream_all = jnp.stack([upstream_all[step][part * half : (part + 1) * half] for step, part in plan])
        normed_two, hidden, expanded_back, down_terms, two_terms = forward_back(mine, upstream_all, matrix_up, matrix_down)

        def flat(values):
            return values.reshape(-1, values.shape[-1])

        down_sum = rows_product(flat(hidden), flat(upstream_all))
        spots = [[spot for spot, (_, part) in enumerate(plan) if part == which and spot < landings(seq)] for which in range(2)]

        def over_plan(values):
            return jnp.concatenate([sum(values[spot].astype(F32) for spot in places) for places in spots])

        two_back = over_plan(two_terms)
        downward_delta = scatter_rows(down_sum)
        middle_flow, dilation_term, translation_term = norm_back(two_back, unit_two, root_two, gain_two)
        middle_back = upstream.astype(F32) + middle_flow
        up_sum = rows_product(after(flat(normed_two), down_sum), flat(expanded_back))
        middle_low = gather_seq(after(middle_back.astype(BF), up_sum))
        heads_back = jnp.concatenate([cols_product(part, matrix_out).astype(BF) for part in middle_low])
        out_sum = rows_product(attended, jnp.concatenate(middle_low))
        heads_back = after(heads_back, (downward_delta, up_sum)).reshape(seq, slots, block, -1)
        summed_up = scatter_columns(after(up_sum, heads_back))
        projected_back, result_terms = attend_back(plan, joint, heads_back, down_terms, size, scaling)
        projected_back = projected_back.reshape(total, -1)
        result = middle + over_plan([down_terms[0], down_terms[1]] + [result_terms[spot] for spot in range(2, landings(seq))])
        outputs = (result * live).astype(BF).reshape(slots, block, model)
        in_sum = rows_product(after(normed, outputs), projected_back)
        summed_in = scatter_columns(in_sum)
        one_terms, swapped_up = send_back(seq, plan, after(projected_back, in_sum), matrix_in, summed_up)
        upward_delta = jnp.concatenate([swapped_up[step] for step in range(seq)], axis=1).astype(F32)
        one_back = over_plan(one_terms)
        outward_delta = scatter_rows(after(out_sum, (summed_in, one_terms)))
        unit_one, root_one = norm_parts(residual.astype(F32))
        input_flow, stretch_term, offset_term = norm_back(one_back, unit_one, root_one, gain_one)
        terms = jnp.stack([stretch_term, offset_term, dilation_term, translation_term])
        terms = terms.reshape(4, seq, dp, -1).transpose(1, 2, 0, 3).reshape(seq, dp, -1)
        terms = jnp.pad(terms, ((0, 0), (0, 0), (0, -taken % 1024))).reshape(seq, dp, -1, 128)
        deltas, inward_delta = closing(seq, dp, heads, terms, summed_in)
        deltas = deltas.reshape(-1)[:taken].reshape(4, -1)
        input_delta = (middle_back + input_flow).reshape(slots, block, model)
        return (
            outputs,
            input_delta,
            deltas[0],
            deltas[1],
            inward_delta,
            outward_delta,
            deltas[2],
            deltas[3],
            upward_delta,
            downward_delta,
        )

    return layer


def solution(mesh):
    tokens, vector, matrix = P("dp", "seq", None), P(("seq", "dp")), P(("seq", "dp"), None)
    return jax.shard_map(
        make_layer(mesh.shape["seq"], mesh.shape["dp"]),
        mesh=mesh,
        in_specs=(tokens, P("dp"), tokens, vector, vector, matrix, matrix, vector, vector, matrix, matrix),
        out_specs=(tokens, tokens, vector, vector, matrix, matrix, vector, vector, matrix, matrix),
        check_vma=False,
    )
```

```python
import functools
import math

import jax
import jax.numpy as jnp
from jax import lax
from jax.experimental import pallas as pl
from jax.experimental.pallas import tpu as pltpu
from jax.sharding import PartitionSpec as P

HEADS = 16
EPSILON = 1e-05
MASKED = -1e30
BF = jnp.bfloat16
F32 = jnp.float32
MESH = pl.DeviceIdType.MESH


def norm_parts(values):
    average = jnp.mean(values, axis=-1, keepdims=True)
    centered = values - average
    root = lax.rsqrt(jnp.mean(centered * centered, axis=-1, keepdims=True) + EPSILON)
    return centered * root, root


def norm_back(flow, unit, root, gain):
    scaled = flow * gain
    first = jnp.mean(scaled, axis=-1, keepdims=True)
    second = jnp.mean(scaled * unit, axis=-1, keepdims=True)
    return root * (scaled - first - unit * second), jnp.sum(flow * unit, axis=0), jnp.sum(flow, axis=0)


def rows_product(left, right):
    return lax.dot_general(left, right, (((0,), (0,)), ((), ())), preferred_element_type=F32)


def cols_product(left, right):
    return lax.dot_general(left, right, (((1,), (1,)), ((), ())), preferred_element_type=F32)


def product(left, right):
    return jnp.dot(left, right, preferred_element_type=F32)


def after(values, event):
    return lax.optimization_barrier((values, event))[0]


def greet(seq, dp, me_seq, me_dp):
    barrier = pltpu.get_barrier_semaphore()
    for step in range(1, seq):
        pl.semaphore_signal(barrier, inc=1, device_id=(lax.rem(me_seq + step, seq), me_dp), device_id_type=MESH)
    for step in range(1, dp):
        pl.semaphore_signal(barrier, inc=1, device_id=(me_seq, lax.rem(me_dp + step, dp)), device_id_type=MESH)
    pl.semaphore_wait(barrier, seq + dp - 2)


def start_trade(seq, me_seq, me_dp, pieces, swapped, own, send, recv):
    copies = [pltpu.make_async_copy(pieces.at[me_seq], swapped.at[me_seq], own)]
    copies[0].start()
    for step in range(1, seq):
        target = lax.rem(me_seq + step, seq)
        copies.append(
            pltpu.make_async_remote_copy(
                pieces.at[target], swapped.at[me_seq], send.at[step], recv.at[step], (target, me_dp), MESH
            )
        )
        copies[-1].start()
    return copies


def opening_kernel(
    seq, dp, pieces, pieces_two, small, shard, swapped, swapped_two, params, shards,
    own, send, recv, send_two, recv_two, send_small, recv_small, send_row, recv_row, send_shard, recv_shard, send_next, recv_next,
):
    me_seq, me_dp = lax.axis_index("seq"), lax.axis_index("dp")
    greet(seq, dp, me_seq, me_dp)
    keep = pltpu.make_async_copy(small, params.at[me_dp, me_seq], own.at[0])
    keep.start()
    tiny, rows = [], []
    for step in range(1, seq):
        target = lax.rem(me_seq + step, seq)
        tiny.append(
            pltpu.make_async_remote_copy(
                small, params.at[me_dp, me_seq], send_small.at[step], recv_small.at[step], (target, me_dp), MESH
            )
        )
        tiny[-1].start()
    large = start_trade(seq, me_seq, me_dp, pieces, swapped, own.at[1], send, recv)
    span = 1 if dp % 2 else 2
    keep_shard = pltpu.make_async_copy(shard, shards.at[me_dp], own.at[3])
    keep_shard.start()
    firsts = []
    for step in range(1, dp // span):
        target = lax.rem(me_dp + span * step, dp)
        firsts.append(
            pltpu.make_async_remote_copy(
                shard, shards.at[me_dp], send_shard.at[step], recv_shard.at[step], (me_seq, target), MESH
            )
        )
        firsts[-1].start()
    large += start_trade(seq, me_seq, me_dp, pieces_two, swapped_two, own.at[2], send_two, recv_two)
    for copy in [keep] + tiny:
        copy.wait()
    for step in range(1, dp):
        target = lax.rem(me_dp + step, dp)
        rows.append(
            pltpu.make_async_remote_copy(
                params.at[me_dp], params.at[me_dp], send_row.at[step], recv_row.at[step], (me_seq, target), MESH
            )
        )
        rows[-1].start()
    keep_shard.wait()
    for step in range(dp // span):
        if step:
            firsts[step - 1].wait()
        if span == 2:
            origin = lax.rem(me_dp + dp - span * step, dp)
            sibling = me_dp + 1 - 2 * lax.rem(me_dp, 2)
            rows.append(
                pltpu.make_async_remote_copy(
                    shards.at[origin], shards.at[origin], send_next.at[step], recv_next.at[step], (me_seq, sibling), MESH
                )
            )
            rows[-1].start()
    for copy in rows + large:
        copy.wait()


def opening(seq, dp, pieces, pieces_two, small, shard):
    anywhere = pl.BlockSpec(memory_space=pl.ANY)
    return pl.pallas_call(
        functools.partial(opening_kernel, seq, dp),
        out_shape=(
            jax.ShapeDtypeStruct(pieces.shape, pieces.dtype),
            jax.ShapeDtypeStruct(pieces_two.shape, pieces_two.dtype),
            jax.ShapeDtypeStruct((dp, seq) + small.shape, small.dtype),
            jax.ShapeDtypeStruct((dp,) + shard.shape, shard.dtype),
        ),
        in_specs=[anywhere] * 4,
        out_specs=(anywhere,) * 4,
        scratch_shapes=[pltpu.SemaphoreType.DMA((4,))]
        + [pltpu.SemaphoreType.DMA((seq,))] * 6
        + [pltpu.SemaphoreType.DMA((dp,))] * 6,
        compiler_params=pltpu.CompilerParams(collective_id=1, has_side_effects=True),
        name="opening",
    )(pieces, pieces_two, small, shard)


def closing_kernel(
    seq, dp, groups, terms, pieces, total, whole, swapped, over_seq, partial, over_dp,
    own, send, recv, send_seq, recv_seq, send_row, recv_row,
):
    me_seq, me_dp = lax.axis_index("seq"), lax.axis_index("dp")
    greet(seq, dp, me_seq, me_dp)
    copies = []
    for step in range(1, seq):
        target = lax.rem(me_seq + step, seq)
        copies.append(
            pltpu.make_async_remote_copy(
                terms.at[target], over_seq.at[step], send_seq.at[step], recv_seq.at[step], (target, me_dp), MESH
            )
        )
        copies[-1].start()
    large = start_trade(seq, me_seq, me_dp, pieces, swapped, own, send, recv)
    value = terms[me_seq]
    for step, copy in enumerate(copies):
        copy.wait()
        value = value + over_seq[step + 1]
    partial[...] = value
    copies = []
    for step in range(1, dp):
        target = lax.rem(me_dp + step, dp)
        copies.append(
            pltpu.make_async_remote_copy(
                partial.at[target], over_dp.at[step], send_row.at[step], recv_row.at[step], (me_seq, target), MESH
            )
        )
        copies[-1].start()
    value = partial[me_dp]
    for step, copy in enumerate(copies):
        copy.wait()
        value = value + over_dp[step + 1]
    total[...] = value
    for copy in large:
        copy.wait()
    size = whole.shape[1] // (3 * seq * groups)
    for source in range(seq):
        for group in range(groups):
            for third in range(3):
                place = ((third * seq + source) * groups + group) * size
                piece = swapped[source, :, (group * 3 + third) * size : (group * 3 + third + 1) * size]
                whole[:, place : place + size] = piece.astype(F32)


def closing(seq, dp, groups, terms, pieces):
    tile = terms.shape[2:]
    inside, anywhere = pl.BlockSpec(memory_space=pltpu.VMEM), pl.BlockSpec(memory_space=pl.ANY)
    return pl.pallas_call(
        functools.partial(closing_kernel, seq, dp, groups),
        out_shape=(
            jax.ShapeDtypeStruct(tile, F32),
            jax.ShapeDtypeStruct((pieces.shape[1], seq * pieces.shape[2]), F32),
        ),
        in_specs=[inside, anywhere],
        out_specs=(inside, inside),
        scratch_shapes=[
            pltpu.VMEM(pieces.shape, BF),
            pltpu.VMEM(terms.shape, F32),
            pltpu.VMEM(terms.shape[1:], F32),
            pltpu.VMEM(terms.shape[1:], F32),
            pltpu.SemaphoreType.DMA,
        ]
        + [pltpu.SemaphoreType.DMA((seq,))] * 4
        + [pltpu.SemaphoreType.DMA((dp,))] * 2,
        compiler_params=pltpu.CompilerParams(collective_id=2, has_side_effects=True),
        name="closing",
    )(terms, pieces)


def head_parts(ref, where, part, size):
    return [ref[where[place], 0, :, part * size : (part + 1) * size] for place in range(ref.shape[0])]


def diagonal(block):
    return lax.broadcasted_iota(jnp.int32, (block, block), 1) <= lax.broadcasted_iota(jnp.int32, (block, block), 0)


def masked_exp(query, keys, scaling):
    logits = cols_product(query, keys) * scaling
    block, length = logits.shape
    last = jnp.where(diagonal(block), logits[:, length - block :], MASKED)
    logits = last if length == block else jnp.concatenate([logits[:, : length - block], last], axis=1)
    raised = jnp.exp(logits - jnp.max(logits, axis=-1, keepdims=True))
    return raised, jnp.sum(raised, axis=-1, keepdims=True)


def attend_kernel(scaling, where, joint, attended):
    seq, _, block, size = attended.shape
    keys = jnp.concatenate(head_parts(joint, where, 1, size))
    values = jnp.concatenate(head_parts(joint, where, 2, size))
    for place in range(seq):
        length = (place + 1) * block
        query = joint[where[place], 0, :, :size]
        raised, sums = masked_exp(query, keys[:length], scaling)
        weights = (raised * (1.0 / sums)).astype(BF)
        attended[where[place], 0] = product(weights, values[:length]).astype(BF)


def attend(where, joint, size, scaling):
    seq, slots, block, width = joint.shape
    heads = width // (3 * size)
    return pl.pallas_call(
        functools.partial(attend_kernel, scaling),
        out_shape=jax.ShapeDtypeStruct((seq, slots, block, heads * size), BF),
        grid=(slots, heads),
        in_specs=[
            pl.BlockSpec(memory_space=pltpu.SMEM),
            pl.BlockSpec((seq, 1, block, 3 * size), lambda slot, head: (0, slot, 0, head)),
        ],
        out_specs=pl.BlockSpec((seq, 1, block, size), lambda slot, head: (0, slot, 0, head)),
        compiler_params=pltpu.CompilerParams(vmem_limit_bytes=48 << 20),
        cost_estimate=pl.CostEstimate(flops=0, bytes_accessed=slots * (30 << 20), transcendentals=0),
        name="attend",
    )(where, joint)


def partner(me, step, count):
    if count & (count - 1):
        return lax.rem(me + step, count), lax.rem(me + count - step, count)
    bit = 1
    while bit < count:
        if step & bit:
            me = me + bit * (1 - 2 * lax.rem(me // bit, 2))
        bit *= 2
    return me, me


def forward_back_plan(seq):
    if seq == 4:
        order = [(0, 0), (0, 1), (1, 0), (2, 0), (1, 1), (2, 1), (3, 0), (3, 1)]
    else:
        order = [(step, half) for step in range(seq) for half in range(2)]
    at = {pair: spot for spot, pair in enumerate(order)}
    moves = []
    for step, half in order[2:]:
        if seq == 4 and step == 3:
            source = (1, 0) if half == 0 else (2, 1)
            moves.append((at[source], at[step, half], step - source[0], at[source]))
        else:
            moves.append((at[0, half], at[step, half], step, half))
    return order, moves


def returns(seq, plan, me_seq, me_dp, parts, extra, landing, send, recv):
    def copy(source, target, step, spot):
        device = (partner(me_seq, step, seq)[1], me_dp)
        return pltpu.make_async_remote_copy(source, target, send.at[spot], recv.at[spot], device, MESH)

    if seq != 4:
        return {spot: copy(parts(spot), landing.at[spot], step, spot) for spot, (step, _) in enumerate(plan) if step}, []
    at = {pair: spot for spot, pair in enumerate(plan)}
    now = {spot: copy(parts(spot), landing.at[spot], plan[spot][0], spot) for spot in (at[1, 0], at[2, 1])}
    now[at[3, 0]] = copy(parts(at[3, 0]), extra.at[0], 1, at[3, 0])
    now[at[3, 1]] = copy(parts(at[3, 1]), extra.at[1], 2, at[3, 1])
    later = []
    for half, spot in enumerate((at[2, 0], at[1, 1])):
        later.append((spot, at[3, half], copy(parts(spot), landing.at[spot], plan[spot][0], spot)))
    return now, later


def landings(seq):
    return 6 if seq == 4 else 2 * seq


def add_into(ref, spot, other, half, chunk):
    def body(step, carry):
        columns = pl.ds(pl.multiple_of(step * chunk, chunk), chunk)
        ref[spot, :, columns] = (ref[spot, :, columns].astype(F32) + other[half, :, columns].astype(F32)).astype(BF)
        return carry

    lax.fori_loop(0, ref.shape[2] // chunk, body, 0)


def attend_back_kernel(
    scaling, plan, joint, flow, terms, joint_back, terms_all, key_sum, value_sum, extra, held, load, send, recv
):
    seq, _, block, size = flow.shape
    me_seq, me_dp = lax.axis_index("seq"), lax.axis_index("dp")
    here = pl.program_id(0) * pl.num_programs(1) + pl.program_id(1)
    final = pl.num_programs(0) * pl.num_programs(1) - 1
    delayed = {spot: half for half, spot in enumerate([plan.index((2, 0)), plan.index((1, 1))])} if seq == 4 else {}
    now, later = returns(
        seq, plan, me_seq, me_dp, lambda spot: held.at[delayed[spot]] if spot in delayed else terms.at[spot],
        extra, terms_all, send, recv,
    )
    loads = [pltpu.make_async_copy(terms.at[spot], held.at[half], load.at[half]) for spot, half in delayed.items()]

    @pl.when(here == 0)
    def _():
        for copy in loads:
            copy.start()
        greet(seq, 1, me_seq, me_dp)
        for copy in now.values():
            copy.start()

    where = [partner(me_seq, place, seq)[1] for place in range(seq)]
    keys = jnp.concatenate(head_parts(joint, where, 1, size))
    values = jnp.concatenate(head_parts(joint, where, 2, size))
    for place in reversed(range(seq)):
        length = (place + 1) * block
        spot = where[place]
        query = joint[spot, 0, :, :size]
        flow_here = flow[spot, 0]
        raised, sums = masked_exp(query, keys[:length], scaling)
        probs = raised * (1.0 / sums)
        weights = probs.astype(BF)
        prob_back = cols_product(flow_here, values[:length])
        mean_back = jnp.sum(probs * prob_back, axis=-1, keepdims=True)
        logit_back = (probs * (prob_back - mean_back)).astype(BF)
        joint_back[spot, 0, :, :size] = (product(logit_back, keys[:length]) * scaling).astype(BF)
        key_term = rows_product(logit_back, query) * scaling
        value_term = rows_product(weights, flow_here)
        if place == seq - 1:
            key_sum[...] = key_term
            value_sum[...] = value_term
        else:
            key_sum[:length] += key_term
            value_sum[:length] += value_term
    for place in range(seq):
        rows = slice(place * block, (place + 1) * block)
        joint_back[where[place], 0, :, size : 2 * size] = key_sum[rows].astype(BF)
        joint_back[where[place], 0, :, 2 * size :] = value_sum[rows].astype(BF)

    @pl.when(here == final)
    def _():
        for copy in loads:
            copy.wait()
        for half, (spot, corner, copy) in enumerate(later):
            now[corner].wait_recv()
            add_into(held, half, extra, half, 256)
            copy.start()
        for spot, copy in now.items():
            copy.wait_send()
            if spot not in [corner for _, corner, _ in later]:
                copy.wait_recv()
        for _, _, copy in later:
            copy.wait()


def attend_back(plan, joint, flow, terms, size, scaling):
    seq, slots, block, width = joint.shape
    heads = width // (3 * size)
    anywhere = pl.BlockSpec(memory_space=pl.ANY)
    wide = pl.BlockSpec((seq, 1, block, 3 * size), lambda slot, head: (0, slot, 0, head))
    return pl.pallas_call(
        functools.partial(attend_back_kernel, scaling, plan),
        out_shape=[
            jax.ShapeDtypeStruct(joint.shape, BF),
            jax.ShapeDtypeStruct((landings(seq),) + terms.shape[1:], BF),
        ],
        grid=(slots, heads),
        in_specs=[wide, pl.BlockSpec((seq, 1, block, size), lambda slot, head: (0, slot, 0, head)), anywhere],
        out_specs=[wide, anywhere],
        scratch_shapes=[pltpu.VMEM((seq * block, size), F32)] * 2
        + [pltpu.VMEM((2,) + terms.shape[1:], BF)] * 2
        + [pltpu.SemaphoreType.DMA((2,))]
        + [pltpu.SemaphoreType.DMA((terms.shape[0],))] * 2,
        compiler_params=pltpu.CompilerParams(
            collective_id=4, has_side_effects=True, vmem_limit_bytes=48 << 20
        ),
        cost_estimate=pl.CostEstimate(flops=0, bytes_accessed=240 << 20, transcendentals=0),
        name="attend_back",
    )(joint, flow, terms)


def forward_back_kernel(
    seq, chunk, mine, upstream, up, down, normed_all, hidden, expanded_back, result, flow_all,
    normed, flow, extra, load, store, send, recv, send_flow, recv_flow,
):
    model, width = up.shape
    rows = normed.shape[1]
    pull = math.sqrt(2.0 / math.pi)
    me_seq, me_dp = lax.axis_index("seq"), lax.axis_index("dp")
    here = pl.program_id(0)
    order, moves = forward_back_plan(seq)
    steps = len(order)
    copies = {}
    for source, target, step, begin in moves:
        copies[target] = pltpu.make_async_remote_copy(
            normed.at[source], normed.at[target], send.at[target], recv.at[target],
            (partner(me_seq, step, seq)[0], me_dp), MESH,
        )
    backs, later = returns(seq, order, me_seq, me_dp, lambda spot: flow.at[spot], extra, flow_all, send_flow, recv_flow)
    owns = [pltpu.make_async_copy(flow.at[spot], flow_all.at[spot], recv_flow.at[spot]) for spot in range(2)]
    stores = [pltpu.make_async_copy(normed.at[spot], normed_all.at[spot], store.at[spot]) for spot in range(steps)]

    @pl.when(here == 0)
    def _():
        fetches = [
            pltpu.make_async_copy(mine.at[pl.ds(half * rows, rows)], normed.at[half], load.at[half]) for half in range(2)
        ]
        for fetch in fetches:
            fetch.start()
        barrier = pltpu.get_barrier_semaphore()
        for step in range(1, seq):
            pl.semaphore_signal(barrier, inc=1, device_id=(lax.rem(me_seq + step, seq), me_dp), device_id_type=MESH)
        for fetch in fetches:
            fetch.wait()
        pl.semaphore_wait(barrier, seq - 1)

    for spot in range(steps):

        @pl.when(here == spot)
        def _(spot=spot):
            if spot > 1:
                copies[spot].wait_recv()
            for source, target, step, begin in moves:
                if begin == spot:
                    copies[target].start()
            stores[spot].start()

    def inner(step, carry):
        columns = pl.ds(pl.multiple_of(step * chunk, chunk), chunk)
        expanded = product(normed[here], up[:, columns])
        pulled = cols_product(upstream[0], down[columns, :])
        square = expanded * expanded
        bend = jnp.tanh(pull * (expanded + 0.044715 * (square * expanded)))
        half = 0.5 * (1.0 + bend)
        hidden[0, :, columns] = (expanded * half).astype(BF)
        slope = half + (0.5 * pull) * expanded * (1.0 - bend * bend) * (1.0 + 0.134145 * square)
        expanded_back[0, :, columns] = (pulled * slope).astype(BF)
        return carry

    lax.fori_loop(0, width // chunk, inner, 0)

    def outer(step, carry):
        columns = pl.ds(pl.multiple_of(step * chunk, chunk), chunk)
        flow[here, :, columns] = cols_product(expanded_back[0], up[columns, :]).astype(BF)
        return carry

    lax.fori_loop(0, model // chunk, outer, 0)
    for spot in range(steps):

        @pl.when(here == spot)
        def _(spot=spot):
            if spot in backs:
                backs[spot].start()
            elif spot < 2:
                owns[spot].start()

    def last(step, carry):
        columns = pl.ds(pl.multiple_of(step * chunk, chunk), chunk)
        result[0, :, columns] = product(hidden[0], down[:, columns]).astype(BF)
        return carry

    lax.fori_loop(0, model // chunk, last, 0)

    @pl.when(here == steps - 1)
    def _():
        for half, (spot, corner, copy) in enumerate(later):
            backs[corner].wait_recv()
            add_into(flow, spot, extra, half, chunk)
            copy.start()
        for copy in copies.values():
            copy.wait_send()
        for spot, copy in backs.items():
            copy.wait_send()
            if spot not in [corner for _, corner, _ in later]:
                copy.wait_recv()
        for _, _, copy in later:
            copy.wait()
        for copy in stores + owns:
            copy.wait()


def forward_back(mine, upstream, up, down):
    steps, rows, model = upstream.shape
    seq = steps // 2
    width = up.shape[1]
    anywhere = pl.BlockSpec(memory_space=pl.ANY)
    by_step = lambda columns: pl.BlockSpec((1, rows, columns), lambda step: (step, 0, 0))
    whole = lambda shape: pl.BlockSpec(shape, lambda step: (0, 0), pipeline_mode=pl.Buffered(1))
    shape = lambda columns: jax.ShapeDtypeStruct((steps, rows, columns), BF)
    return pl.pallas_call(
        functools.partial(forward_back_kernel, seq, math.gcd(1024, math.gcd(width, model))),
        out_shape=[shape(model), shape(width), shape(width), shape(model)]
        + [jax.ShapeDtypeStruct((landings(seq), rows, model), BF)],
        grid=(steps,),
        in_specs=[anywhere, by_step(model), whole(up.shape), whole(down.shape)],
        out_specs=[anywhere, by_step(width), by_step(width), by_step(model), anywhere],
        scratch_shapes=[
            pltpu.VMEM((steps, rows, model), BF),
            pltpu.VMEM((steps, rows, model), BF),
            pltpu.VMEM((2, rows, model), BF),
            pltpu.SemaphoreType.DMA((2,)),
        ]
        + [pltpu.SemaphoreType.DMA((steps,))] * 5,
        compiler_params=pltpu.CompilerParams(
            collective_id=3, has_side_effects=True, vmem_limit_bytes=56 << 20
        ),
        cost_estimate=pl.CostEstimate(
            flops=8 * steps * rows * model * width, bytes_accessed=400 << 20, transcendentals=steps * rows * width
        ),
        name="forward_back",
    )(mine, upstream, up, down)


def send_back_kernel(
    seq, plan, chunk, left, right, pieces, landing, swapped, flow, extra, keep, send, recv, own, send_piece, recv_piece
):
    me_seq, me_dp = lax.axis_index("seq"), lax.axis_index("dp")
    model = right.shape[0]
    now, later = returns(seq, plan, me_seq, me_dp, lambda spot: flow.at[spot], extra, landing, send, recv)
    owns = [pltpu.make_async_copy(flow.at[spot], landing.at[spot], keep.at[spot]) for spot in range(2)]
    greet(seq, 1, me_seq, me_dp)

    def work(spot):
        def body(step, carry):
            columns = pl.ds(pl.multiple_of(step * chunk, chunk), chunk)
            flow[spot, :, columns] = cols_product(left[plan[spot][0] * 2 + plan[spot][1]], right[columns, :]).astype(BF)
            return carry

        lax.fori_loop(0, model // chunk, body, 0)

    corners = [corner for _, corner, _ in later]
    for spot in corners + [spot for spot in now if spot not in corners]:
        work(spot)
        now[spot].start()
    for spot, _, _ in later:
        work(spot)
    for spot in range(2):
        work(spot)
        owns[spot].start()
    for half, (spot, corner, copy) in enumerate(later):
        now[corner].wait_recv()
        add_into(flow, spot, extra, half, chunk)
        copy.start()
    for copy in start_trade(seq, me_seq, me_dp, pieces, swapped, own, send_piece, recv_piece):
        copy.wait()
    for spot, copy in now.items():
        copy.wait_send()
        if spot not in corners:
            copy.wait_recv()
    for _, _, copy in later:
        copy.wait()
    for copy in owns:
        copy.wait()


def send_back(seq, plan, left, right, pieces):
    steps = len(plan)
    model, depth = right.shape
    left = left.reshape(steps, -1, depth)
    rows = left.shape[1]
    inside, anywhere = pl.BlockSpec(memory_space=pltpu.VMEM), pl.BlockSpec(memory_space=pl.ANY)
    return pl.pallas_call(
        functools.partial(send_back_kernel, seq, plan, math.gcd(1024, model)),
        out_shape=[
            jax.ShapeDtypeStruct((landings(seq), rows, model), BF),
            jax.ShapeDtypeStruct(pieces.shape, pieces.dtype),
        ],
        in_specs=[inside, inside, anywhere],
        out_specs=[anywhere, anywhere],
        scratch_shapes=[
            pltpu.VMEM((steps, rows, model), BF),
            pltpu.VMEM((2, rows, model), BF),
            pltpu.SemaphoreType.DMA((2,)),
        ]
        + [pltpu.SemaphoreType.DMA((steps,))] * 2
        + [pltpu.SemaphoreType.DMA]
        + [pltpu.SemaphoreType.DMA((seq,))] * 2,
        compiler_params=pltpu.CompilerParams(
            collective_id=5, has_side_effects=True, vmem_limit_bytes=44 << 20
        ),
        cost_estimate=pl.CostEstimate(
            flops=2 * steps * rows * model * depth, bytes_accessed=240 << 20, transcendentals=0
        ),
        name="send_back",
    )(left, right, pieces)


def make_layer(seq, dp):
    xor = seq & (seq - 1) == 0

    def shift(values, step):
        pairs = [(i, i ^ step if xor else (i + step) % seq) for i in range(seq)]
        return lax.ppermute(values, "seq", pairs)

    def gather_seq(block, event=None):
        if seq != 4:
            return [block] + [shift(block, step) for step in range(1, seq)]
        half = block.shape[0] // 2
        near, far = shift(block, 1), shift(block, 2)
        halves = near[:half], far[half:]
        if event is not None:
            halves = after(halves, event)
        return [block, near, far, jnp.concatenate([shift(halves[0], 2), shift(halves[1], 1)])]

    def scatter_seq(make, event=None, begun=None):
        if seq != 4:
            sent = [shift(make(step).astype(BF), step if xor else seq - step).astype(F32) for step in range(1, seq)]
            return make(0) + sum(sent)
        corner = make(3).astype(BF)
        half = corner.shape[0] // 2
        by_near, by_far = shift(corner[:half], 1), shift(corner[half:], 2)
        near = lax.optimization_barrier(make(1).astype(BF))
        far = lax.optimization_barrier(make(2).astype(BF))
        near_first, far_last = shift(near[:half], 1), shift(far[half:], 2)
        if event is not None:
            by_near, by_far = after((by_near, by_far), event)
        if begun is not None:
            begun.extend([by_near, by_far])
        near_last = shift((near[half:].astype(F32) + by_far.astype(F32)).astype(BF), 1)
        far_first = shift((far[:half].astype(F32) + by_near.astype(F32)).astype(BF), 2)
        first = near_first.astype(F32) + far_first.astype(F32)
        last = near_last.astype(F32) + far_last.astype(F32)
        return make(0) + jnp.concatenate([first, last])

    def column_pieces(shard, thirds, groups):
        rows, columns = shard.shape
        shaped = shard.reshape(rows, thirds, seq, groups, -1).transpose(2, 0, 3, 1, 4)
        return shaped.reshape(seq, rows, columns // seq)

    def gather_columns(swapped):
        return lax.all_gather(swapped, "dp", axis=1, tiled=True).reshape(-1, swapped.shape[2])

    def scatter_columns(term):
        total, width = term.shape
        rows = total // (seq * dp)
        summed = lax.psum_scatter(
            term.astype(BF).reshape(seq, dp * rows, width), "dp", scatter_dimension=1, tiled=True
        )
        return summed

    def scatter_rows(term):
        return lax.psum_scatter(term.astype(BF), "dp", scatter_dimension=0, tiled=True).astype(F32)

    def layer(
        inputs, counts, cotangent, stretch, offset, inward, outward, dilation, translation, upward, downward
    ):
        slots, block, model = inputs.shape
        size = model // HEADS
        heads = HEADS // seq
        scaling = 1.0 / math.sqrt(size)
        local_rows = slots * block
        total = seq * local_rows
        live = jnp.repeat((jnp.arange(slots) < counts[0]).astype(F32), block)[:, None]
        residual = inputs.reshape(local_rows, model)
        small = jnp.stack([stretch, offset, dilation, translation]).astype(F32).reshape(-1)
        taken = small.shape[0]
        small = jnp.pad(small, (0, -taken % 1024)).reshape(-1, 128)
        swapped_in, swapped_up, small, matrix_out = opening(
            seq, dp, column_pieces(inward, 3, heads), column_pieces(upward, 1, 1), small, outward
        )
        matrix_out = matrix_out.reshape(-1, model)
        small = small.reshape(dp, seq, -1)[:, :, :taken].reshape(dp, seq, 4, -1).transpose(2, 1, 0, 3).reshape(4, model)
        gain_one, shift_one, gain_two, shift_two = small[0], small[1], small[2], small[3]
        matrix_in = gather_columns(swapped_in)
        blocks = gather_seq(after(residual, swapped_in))
        upstream = (cotangent.astype(F32).reshape(local_rows, model) * live).astype(BF)
        def piece(values, step):
            return values[step * local_rows : (step + 1) * local_rows]

        def norm_one(values):
            return (norm_parts(values.astype(F32))[0] * gain_one + shift_one).astype(BF)

        normed = [norm_one(part) for part in blocks]
        projected = jnp.concatenate([product(part, matrix_in).astype(BF) for part in normed])
        normed = jnp.concatenate(normed)
        upstream_all = gather_seq(after(upstream, blocks[-1]), projected)
        matrix_up = gather_columns(after(swapped_up, (matrix_in, blocks[-1])))
        me = lax.axis_index("seq")
        where = me ^ jnp.arange(seq) if xor else (me + seq - jnp.arange(seq)) % seq
        joint = projected.reshape(seq, slots, block, -1)
        attended = attend(where, joint, size, scaling).reshape(total, heads * size)
        begun = []
        middle = residual.astype(F32) + scatter_seq(lambda step: product(piece(attended, step), matrix_out), None, begun)
        matrix_down = lax.all_gather(after(downward, (matrix_up, begun, upstream_all[1:3])), "dp", axis=0, tiled=True)
        unit_two, root_two = norm_parts(middle)
        mine = (unit_two * gain_two + shift_two).astype(BF)
        half = local_rows // 2
        plan = forward_back_plan(seq)[0]
        upstream_all = jnp.stack([upstream_all[step][part * half : (part + 1) * half] for step, part in plan])
        normed_two, hidden, expanded_back, down_terms, two_terms = forward_back(mine, upstream_all, matrix_up, matrix_down)

        def flat(values):
            return values.reshape(-1, values.shape[-1])

        down_sum = rows_product(flat(hidden), flat(upstream_all))
        spots = [[spot for spot, (_, part) in enumerate(plan) if part == which and spot < landings(seq)] for which in range(2)]

        def over_plan(values):
            return jnp.concatenate([sum(values[spot].astype(F32) for spot in places) for places in spots])

        two_back = over_plan(two_terms)
        downward_delta = scatter_rows(down_sum)
        middle_flow, dilation_term, translation_term = norm_back(two_back, unit_two, root_two, gain_two)
        middle_back = upstream.astype(F32) + middle_flow
        up_sum = rows_product(after(flat(normed_two), down_sum), flat(expanded_back))
        middle_low = gather_seq(after(middle_back.astype(BF), up_sum))
        heads_back = jnp.concatenate([cols_product(part, matrix_out).astype(BF) for part in middle_low])
        out_sum = rows_product(attended, jnp.concatenate(middle_low))
        heads_back = after(heads_back, (downward_delta, up_sum)).reshape(seq, slots, block, -1)
        summed_up = scatter_columns(after(up_sum, heads_back))
        projected_back, result_terms = attend_back(plan, joint, heads_back, down_terms, size, scaling)
        projected_back = projected_back.reshape(total, -1)
        result = middle + over_plan([down_terms[0], down_terms[1]] + [result_terms[spot] for spot in range(2, landings(seq))])
        outputs = (result * live).astype(BF).reshape(slots, block, model)
        in_sum = rows_product(after(normed, outputs), projected_back)
        summed_in = scatter_columns(in_sum)
        one_terms, swapped_up = send_back(seq, plan, after(projected_back, in_sum), matrix_in, summed_up)
        upward_delta = jnp.concatenate([swapped_up[step] for step in range(seq)], axis=1).astype(F32)
        one_back = over_plan(one_terms)
        outward_delta = scatter_rows(after(out_sum, (summed_in, one_terms)))
        unit_one, root_one = norm_parts(residual.astype(F32))
        input_flow, stretch_term, offset_term = norm_back(one_back, unit_one, root_one, gain_one)
        terms = jnp.stack([stretch_term, offset_term, dilation_term, translation_term])
        terms = terms.reshape(4, seq, dp, -1).transpose(1, 2, 0, 3).reshape(seq, dp, -1)
        terms = jnp.pad(terms, ((0, 0), (0, 0), (0, -taken % 1024))).reshape(seq, dp, -1, 128)
        deltas, inward_delta = closing(seq, dp, heads, terms, summed_in)
        deltas = deltas.reshape(-1)[:taken].reshape(4, -1)
        input_delta = (middle_back + input_flow).reshape(slots, block, model)
        return (
            outputs,
            input_delta,
            deltas[0],
            deltas[1],
            inward_delta,
            outward_delta,
            deltas[2],
            deltas[3],
            upward_delta,
            downward_delta,
        )

    return layer


def solution(mesh):
    tokens, vector, matrix = P("dp", "seq", None), P(("seq", "dp")), P(("seq", "dp"), None)
    return jax.shard_map(
        make_layer(mesh.shape["seq"], mesh.shape["dp"]),
        mesh=mesh,
        in_specs=(tokens, P("dp"), tokens, vector, vector, matrix, matrix, vector, vector, matrix, matrix),
        out_specs=(tokens, tokens, vector, vector, matrix, matrix, vector, vector, matrix, matrix),
        check_vma=False,
    )
```
